32 devices in a mesh: rep: 8 (over y, x, core), shard: 4 (over z).
Axes of the slice: x: 2, y: 2, z: 4, core: 2. Of those that a mesh axis runs over, the one named last changes fastest.
Arguments:
- hidden_in: bfloat16 [16, 512, 1024], P('rep', 'shard'), may hold values from -6 to 6
- segments: int32 [16, 512], P('rep'), may hold values from 0 to 3, as said below
- norm_gains: bfloat16 [2, 2, 1024], P(None, None, 'shard'), may hold values from 0.5 to 1.5
- norm_biases: bfloat16 [2, 2, 1024], P(None, None, 'shard'), may hold values from -3 to 3
- qkv_weight: bfloat16 [2, 1024, 3072], P(None, 'shard'), may hold values from -0.1875 to 0.1875
- qkv_bias: bfloat16 [2, 3072], P(None, 'shard'), may hold values from -3 to 3
- out_weight: bfloat16 [2, 1024, 1024], P(None, 'shard'), may hold values from -0.75 to 0.75
- out_bias: bfloat16 [2, 1024], P(None, 'shard'), may hold values from -3 to 3
- up_weight: bfloat16 [2, 1024, 4096], P(None, 'shard'), may hold values from -0.1875 to 0.1875
- up_bias: bfloat16 [2, 4096], P(None, 'shard'), may hold values from -3 to 3
- down_weight: bfloat16 [2, 4096, 1024], P(None, 'shard'), may hold values from -0.09375 to 0.09375
- down_bias: bfloat16 [2, 1024], P(None, 'shard'), may hold values from -3 to 3
- out_grad: bfloat16 [16, 512, 1024], P('rep', 'shard'), may hold values from -6 to 6
Outputs:
- block_out: bfloat16 [16, 512, 1024], P('rep', 'shard')
- in_grad: float32 [16, 512, 1024], P('rep', 'shard')
- norm_gains_grad: float32 [2, 2, 1024], P(None, None, 'shard')
- norm_biases_grad: float32 [2, 2, 1024], P(None, None, 'shard')
- qkv_weight_grad: float32 [2, 1024, 3072], P(None, 'shard')
- qkv_bias_grad: float32 [2, 3072], P(None, 'shard')
- out_weight_grad: float32 [2, 1024, 1024], P(None, 'shard')
- out_bias_grad: float32 [2, 1024], P(None, 'shard')
- up_weight_grad: float32 [2, 1024, 4096], P(None, 'shard')
- up_bias_grad: float32 [2, 4096], P(None, 'shard')
- down_weight_grad: float32 [2, 4096, 1024], P(None, 'shard')
- down_bias_grad: float32 [2, 1024], P(None, 'shard')
The draws below stay inside these ranges and needn't reach their ends.
Inputs may be any that keep to these rules, and one draw needn't show every extreme that they name: `segments`: in every row the segment numbers start at 0, never fall and rise by at most one from one token to the next.
All inputs are finite; a program needn't handle non-finite values.
Results may differ from the reference program's by a relative error of at most 0.02.
Values may be sent and summed in bfloat16 or wider, within the bound.
No kernel may reach another device: no remote copies, remote signals or barrier semaphores. Data moves between devices by JAX's collectives and lax.ppermute only.
A program may use at most 320 MiB of HBM per device.

```python
import math
import jax
import jax.numpy as jnp
from jax import lax

D = 1024
H = 16
HD = 64
FF = 4096
ROT = 16
LAYERS = 2
ROWS_DEV = 2
SEQ = 512
ROWS = 16


def draw_segments(key, part):
    key = jax.random.fold_in(key, 11)
    keys = jax.random.split(key, 5)
    quarter = SEQ // 4
    lead = jax.random.randint(keys[0], (ROWS, 1), 1, quarter)
    tail = jax.random.randint(keys[1], (ROWS, 1), 3 * quarter, SEQ)
    middle = jax.random.randint(keys[2], (ROWS, 1), quarter, 3 * quarter)
    split_row = jax.random.randint(keys[3], (ROWS, 1), 0, 2)
    whole_row = jax.random.randint(keys[4], (), 0, ROWS_DEV)
    row_index = jnp.arange(ROWS, dtype=jnp.int32)[:, None]
    split_row = jnp.where(row_index % ROWS_DEV == whole_row, 0, split_row)
    place = jnp.arange(SEQ, dtype=jnp.int32)[None, :]
    return ((place >= lead).astype(jnp.int32) + split_row * (place >= middle).astype(jnp.int32) + (place >= tail).astype(jnp.int32)).astype(jnp.int32)


def block_scale(rng, extent, cuts, low, largest):
    loudness, own = 1.0, jax.random.fold_in(rng, 6)
    for dim, shards_of in cuts:
        draws = jnp.exp(jax.random.uniform(jax.random.fold_in(own, dim), (shards_of,), jnp.float32, low / len(cuts), largest / len(cuts)))
        loudness = loudness * jnp.repeat(draws, extent[dim] // shards_of).reshape([-1 if axis == dim else 1 for axis in range(len(extent))])
    return loudness


def bell_draw(key, shape, width, bound, cuts=(), kind=jnp.bfloat16):
    values = width * jax.random.normal(key, shape, jnp.float32)
    if cuts:
        values = values * block_scale(key, shape, cuts, -0.22, 0.18)
    return jnp.clip(values, -bound, bound).astype(kind)


def setup_inputs(seed: int = 0) -> dict:
    splits = jax.random.split(jax.random.key(seed), 14)
    hidden_in = bell_draw(splits[0], (ROWS, SEQ, D), 1.0, 6.0, ((0, 8), (1, 4)))
    segments = draw_segments(jax.random.fold_in(splits[13], 71), 0)
    norm_gains = jnp.clip(1.0 + 0.1 * jax.random.normal(splits[2], (LAYERS, 2, D), jnp.float32), 0.5, 1.5).astype(jnp.bfloat16)
    norm_biases = bell_draw(splits[3], (LAYERS, 2, D), 0.3, 3.0, ((2, 4),))
    qkv_weight = bell_draw(splits[4], (LAYERS, D, 3 * D), D ** -0.5, 0.1875, ((1, 4),))
    qkv_bias = bell_draw(splits[5], (LAYERS, 3 * D), 0.3, 3.0, ((1, 4),))
    out_weight = bell_draw(splits[6], (LAYERS, D, D), (D // 16) ** -0.5, 0.75, ((1, 4),))
    out_bias = bell_draw(splits[7], (LAYERS, D), 0.3, 3.0, ((1, 4),))
    up_weight = bell_draw(splits[8], (LAYERS, D, FF), D ** -0.5, 0.1875, ((1, 4),))
    up_bias = bell_draw(splits[9], (LAYERS, FF), 0.3, 3.0, ((1, 4),))
    down_weight = bell_draw(splits[10], (LAYERS, FF, D), FF ** -0.5, 0.09375, ((1, 4),))
    down_bias = bell_draw(splits[11], (LAYERS, D), 0.3, 3.0, ((1, 4),))
    out_grad = bell_draw(splits[12], (ROWS, SEQ, D), 1.0, 6.0, ((0, 8), (1, 4)))
    return dict(hidden_in=hidden_in, segments=segments, norm_gains=norm_gains, norm_biases=norm_biases, qkv_weight=qkv_weight, qkv_bias=qkv_bias, out_weight=out_weight, out_bias=out_bias, up_weight=up_weight, up_bias=up_bias, down_weight=down_weight, down_bias=down_bias, out_grad=out_grad)


@jax.custom_vjp
def low(v):
    return lax.optimization_barrier(v.astype(jnp.bfloat16)).astype(jnp.float32)

@jax.custom_vjp
def low_back(v):
    return v

def low_keep(v):
    return (low(v), None)

def low_pass(kept, grad):
    return (grad,)

def back_keep(v):
    return (v, None)

def back_low(kept, grad):
    return (low(grad),)
low.defvjp(low_keep, low_pass)
low_back.defvjp(back_keep, back_low)
epsilon = 1e-05
HIGH = lax.Precision.HIGHEST

def layer_norm(stream, gain_vec, shift_vec):
    average = lax.optimization_barrier(jnp.mean(stream, -1, keepdims=True))
    centred = stream - average
    spread = lax.optimization_barrier(jnp.mean(centred * centred, -1, keepdims=True))
    return centred * lax.rsqrt(spread + epsilon) * gain_vec + shift_vec

def rotary_tables(positions):
    half_rot = ROT // 2
    inverse = jnp.power(10000.0, -2.0 * jnp.arange(half_rot, dtype=jnp.float32) / ROT)
    angles = positions.astype(jnp.float32)[..., None] * inverse
    return (jnp.cos(angles)[..., None, :], jnp.sin(angles)[..., None, :])

def rotate(vectors, cosine_tab, sine_tab):
    half_rot = ROT // 2
    first_part = vectors[..., :half_rot]
    second = vectors[..., half_rot:ROT]
    return jnp.concatenate([first_part * cosine_tab - second * sine_tab, second * cosine_tab + first_part * sine_tab, vectors[..., ROT:]], -1)

def attention(query_low, key_low, value_low, visible_mask):
    scores = low_back(jnp.einsum('gqhd,gkhd->ghqk', query_low, key_low, precision=HIGH) * (1.0 / math.sqrt(HD)))
    scores = jnp.where(visible_mask[:, None], scores, -1e+30)
    run_max = lax.optimization_barrier(jnp.max(scores, -1, keepdims=True))
    expo = jnp.exp(scores - run_max)
    attn_weights = low(expo / lax.optimization_barrier(jnp.sum(expo, -1, keepdims=True)))
    return low_back(jnp.einsum('ghqk,gkhd->gqhd', attn_weights, value_low, precision=HIGH))

def block_layer(stream, parameters, layer_idx, cosine_tab, sine_tab, visible_mask):
    gains, shifts, w_qkv, b_qkv, w_out, b_out, w_up, b_up, w_down, b_down = [stacked[layer_idx] for stacked in parameters]
    group_rows = stream.shape[0]
    attn_low = low(layer_norm(stream, gains[0], shifts[0]))
    mlp_low = low(layer_norm(stream, gains[1], shifts[1]))
    projected = low_back(jnp.dot(attn_low, w_qkv, precision=HIGH) + b_qkv).reshape(group_rows, SEQ, 3, H, HD)
    query_low = low(rotate(projected[:, :, 0], cosine_tab, sine_tab))
    key_low = low(rotate(projected[:, :, 1], cosine_tab, sine_tab))
    value_low = low(projected[:, :, 2])
    mixed = jax.checkpoint(attention)(query_low, key_low, value_low, visible_mask)
    mixed_low = low(mixed.reshape(group_rows, SEQ, D))
    attn_out = low_back(jnp.dot(mixed_low, w_out, precision=HIGH) + b_out)
    hidden_pre = low_back(jnp.dot(mlp_low, w_up, precision=HIGH) + b_up)
    hidden_low = low(jax.nn.gelu(hidden_pre, approximate=False))
    mlp_out = low_back(jnp.dot(hidden_low, w_down, precision=HIGH) + b_down)
    return stream + attn_out + mlp_out

def stack_forward(stream, parameters, seg_rows):
    place = jnp.arange(SEQ, dtype=jnp.int32)
    earlier = lax.optimization_barrier(jnp.sum((seg_rows[:, None, :] < seg_rows[:, :, None]).astype(jnp.int32), -1))
    positions = place[None, :] - earlier
    cosine_tab, sine_tab = rotary_tables(positions)
    visible_mask = (place[None, :] <= place[:, None])[None] & (seg_rows[:, None, :] == seg_rows[:, :, None])
    for layer_idx in range(LAYERS):
        stream = block_layer(stream, parameters, layer_idx, cosine_tab, sine_tab, visible_mask)
    return stream

def reference(hidden_in, segments, norm_gains, norm_biases, qkv_weight, qkv_bias, out_weight, out_bias, up_weight, up_bias, down_weight, down_bias, out_grad):
    parameters = tuple((stacked.astype(jnp.float32) for stacked in (norm_gains, norm_biases, qkv_weight, qkv_bias, out_weight, out_bias, up_weight, up_bias, down_weight, down_bias)))
    group_rows = 8 if ROWS % 8 == 0 else 1
    group_count = ROWS // group_rows
    inputs_in = hidden_in.astype(jnp.float32).reshape(group_count, group_rows, SEQ, D)
    grads_in = out_grad.astype(jnp.float32).reshape(group_count, group_rows, SEQ, D)
    seg_groups = segments.reshape(group_count, group_rows, SEQ)

    def step(totals, batch_item):
        stream, cotangent, seg_rows = batch_item
        result, pullback = jax.vjp(lambda inputs, weights: stack_forward(inputs, weights, seg_rows), stream, parameters)
        d_stream, d_params = pullback(cotangent)
        totals = jax.tree.map(lambda left, right: left + right, totals, d_params)
        return (totals, (result.astype(jnp.bfloat16), d_stream))
    zero_grads = jax.tree.map(jnp.zeros_like, parameters)
    totals, (results, d_inputs) = lax.scan(step, zero_grads, (inputs_in, grads_in, seg_groups))
    return (results.reshape(ROWS, SEQ, D), d_inputs.reshape(ROWS, SEQ, D), totals[0], totals[1], totals[2], totals[3], totals[4], totals[5], totals[6], totals[7], totals[8], totals[9])
```

```python
import math

import jax
import jax.numpy as jnp
from jax import lax
from jax.experimental import pallas as pl
from jax.experimental.pallas import tpu as pltpu
from jax.sharding import Mesh
from jax.sharding import PartitionSpec as P

H = 16
ROT = 16
LAYERS = 2
EPS = 1e-05
ROOT_HALF = math.sqrt(0.5)
F32 = jnp.float32
BF16 = jnp.bfloat16
AXES = ("outer", "ybit", "xbit", "core")
VMEM_LIMIT = 48 * 1024 * 1024


def swap(x, axis):
    return lax.ppermute(x, axis, [(0, 1), (1, 0)])


def spin(x, k, span):
    return lax.ppermute(x, "shard", [(j, (j + k) % span) for j in range(span)])


def after(x, dep):
    return lax.optimization_barrier((x, dep))[0]


def dot(a, b):
    return jnp.dot(a, b, preferred_element_type=F32)


def dot_t(a, b):
    return lax.dot_general(a, b, (((1,), (1,)), ((), ())), preferred_element_type=F32)


class Place:
    def __init__(self, span):
        self.span = span
        self.z = lax.axis_index("shard")
        self.c = lax.axis_index("core")
        self.bx = lax.axis_index("xbit")
        self.by = lax.axis_index("ybit")
        self.q = 2 * self.by + self.bx
        self.scalars = jnp.stack([self.z, self.q, self.c]).astype(jnp.int32)


def from_relative(blocks, place):
    span = place.span
    order = [blocks[(-m) % span] for m in range(2 * span - 1)]
    return lax.dynamic_slice_in_dim(
        jnp.stack(order), lax.rem(span - place.z, span), span, 0
    )


def by_core(place, own, other, axis):
    return jnp.where(
        place.c == 0,
        jnp.concatenate([own, other], axis),
        jnp.concatenate([other, own], axis),
    )


def copy_call(body, out_shape, copies, operands, place):
    def kernel(scalars, *refs):
        ins, out, sems = refs[: len(operands)], refs[len(operands)], refs[-1]
        started = []
        for slot, (src, dst) in enumerate(body(scalars, ins, out)):
            copy = pltpu.make_async_copy(src, dst, sems.at[slot])
            copy.start()
            started.append(copy)
        for copy in started:
            copy.wait()

    size = 2 * math.prod(out_shape.shape) * out_shape.dtype.itemsize
    return pl.pallas_call(
        kernel,
        out_shape=out_shape,
        in_specs=[pl.BlockSpec(memory_space=pltpu.SMEM)]
        + [pl.BlockSpec(memory_space=pl.ANY)] * len(operands),
        out_specs=pl.BlockSpec(memory_space=pltpu.VMEM),
        scratch_shapes=[pltpu.SemaphoreType.DMA((copies,))],
        compiler_params=pltpu.CompilerParams(vmem_limit_bytes=VMEM_LIMIT),
        cost_estimate=pl.CostEstimate(flops=0, bytes_accessed=size, transcendentals=0),
    )(place.scalars, *operands)


def pick_columns(shard, width, place):
    rows, columns = shard.shape
    count = columns // (2 * width)

    def body(scalars, ins, out):
        core = scalars[2]
        for j in range(count):
            start = pl.multiple_of((2 * j + core) * width, width)
            yield ins[0].at[:, pl.ds(start, width)], out.at[:, pl.ds(j * width, width)]

    shape = jax.ShapeDtypeStruct((rows, count * width), shard.dtype)
    return copy_call(body, shape, count, [shard], place)


def assemble(half, pieces, flips, place):
    span = place.span
    quarter, columns = half.shape[0] // 4, half.shape[1]

    def body(scalars, ins, out):
        z, q = scalars[0], scalars[1]
        yield ins[0], out.at[z]
        for i, flip in enumerate(flips):
            slot = lax.bitwise_xor(q, jnp.int32(flip))
            for k in range(1, span):
                source = lax.rem(z + (span - k), span)
                yield ins[1 + i].at[k - 1], out.at[source, slot]

    shape = jax.ShapeDtypeStruct((span, 4, quarter, columns), half.dtype)
    half = half.reshape(4, quarter, columns)
    out = copy_call(body, shape, 1 + len(flips) * (span - 1), [half, *pieces], place)
    return out.reshape(span * 4 * quarter, columns)


def relative_rows(table, flips, place):
    span = place.span
    quarter = table.shape[0] // (4 * span)
    table = table.reshape(span, 4, quarter, table.shape[1])

    def body(scalars, ins, out):
        z, q = scalars[0], scalars[1]
        for j, flip in enumerate(flips):
            for k in range(span):
                target = lax.rem(z + k, span)
                yield ins[0].at[target, lax.bitwise_xor(q, jnp.int32(flip))], out.at[j, k]

    shape = jax.ShapeDtypeStruct((4, span, quarter, table.shape[3]), table.dtype)
    return copy_call(body, shape, 4 * span, [table], place)


def absolute_quarters(parts, flips, place):
    quarter, columns = parts[0].shape

    def body(scalars, ins, out):
        for i, flip in enumerate(flips):
            yield ins[i], out.at[lax.bitwise_xor(scalars[1], jnp.int32(flip))]

    shape = jax.ShapeDtypeStruct((4, quarter, columns), parts[0].dtype)
    return copy_call(body, shape, 4, list(parts), place).reshape(4 * quarter, columns)


def row_to_chip(x, place):
    span = place.span
    rows, tokens, width = x.shape
    half = width // 2
    mine = lax.dynamic_slice_in_dim(x, place.c * half, half, 2)
    theirs = lax.dynamic_slice_in_dim(x, (1 - place.c) * half, half, 2)
    rows_all = by_core(place, mine, swap(theirs, "core"), 0)
    blocks = []
    for k in range(span):
        block = lax.dynamic_index_in_dim(
            rows_all, lax.rem(place.z + k, span), 0, keepdims=False
        )
        blocks.append(block if k == 0 else spin(block, k, span))
    own = from_relative(blocks, place).reshape(span * tokens, half)
    return by_core(place, own, swap(own, "core"), 1)


def chip_to_rows(y, rows, place):
    span = place.span
    width = y.shape[1]
    tokens = y.shape[0] // span
    half = width // 2
    mine = lax.dynamic_slice_in_dim(y, place.c * half, half, 1)
    mine = mine.reshape(span, tokens, half)
    blocks = []
    for k in range(span):
        block = lax.dynamic_index_in_dim(
            mine, lax.rem(place.z + k, span), 0, keepdims=False
        )
        blocks.append(block if k == 0 else spin(block, k, span))
    stacked = from_relative(blocks, place)
    own = lax.dynamic_slice_in_dim(stacked, place.c * rows, rows, 0)
    theirs = lax.dynamic_slice_in_dim(stacked, (1 - place.c) * rows, rows, 0)
    return by_core(place, own, swap(theirs, "core"), 2)


def axis_order(x_first):
    return ("xbit", 1, "ybit", 2) if x_first else ("ybit", 2, "xbit", 1)


def gather_weight(half, x_first, gate, place):
    span = place.span
    quarter = half.shape[0] // 4
    first, flip_first, second, flip_second = axis_order(x_first)
    mine = lax.dynamic_slice_in_dim(half, place.q * quarter, quarter, 0)
    if gate is not None:
        mine = after(mine, gate)
    near = jnp.stack([spin(mine, k, span) for k in range(1, span)])
    near_first = swap(near, first)
    near_second = swap(near, second)
    far = swap(near_first, second)
    flips = (0, flip_first, flip_second, flip_first ^ flip_second)
    return assemble(half, (near, near_first, near_second, far), flips, place), near


def reduce_weight(left_t, right, x_first, place):
    span = place.span
    first, flip_first, second, flip_second = axis_order(x_first)
    both = flip_first ^ flip_second
    rows = relative_rows(left_t, (0, flip_second, flip_first, both), place)
    quarter, tokens = rows.shape[2:]
    columns = right.shape[1]
    rows = rows.reshape(4 * span * quarter, tokens)
    cut = 2 * span * quarter
    send = dot(rows[cut:], right).astype(BF16)
    keep = dot(rows[:cut], right).astype(BF16)
    got = swap(send, first)
    keep = keep.reshape(2, span, quarter, columns)
    got = got.reshape(2, span, quarter, columns)
    onward = (keep[1].astype(F32) + got[1].astype(F32)).astype(BF16)
    got_second = swap(onward, second)
    total = (
        keep[0].astype(F32) + got[0].astype(F32) + got_second.astype(F32)
    ).astype(BF16)
    summed = total[0].astype(F32)
    for k in range(1, span):
        summed = summed + spin(total[k], k, span).astype(F32)
    summed = summed.astype(BF16)
    if lax.axis_size("outer") > 1:
        summed = lax.psum(summed, "outer")
    near_first = swap(summed, first)
    near_second = swap(summed, second)
    far = swap(near_first, second)
    flips = (0, flip_first, flip_second, both)
    return absolute_quarters((summed, near_first, near_second, far), flips, place)


def gather_small(vectors, place):
    flat = jnp.concatenate([v.reshape(-1) for v in vectors])
    blocks = [flat] + [spin(flat, k, place.span) for k in range(1, place.span)]
    table = from_relative(blocks, place)
    out, start = [], 0
    for v in vectors:
        part = table[:, start : start + v.size].reshape(place.span, *v.shape)
        start += v.size
        part = jnp.moveaxis(part, 0, -2)
        out.append(part.reshape(*v.shape[:-1], -1).astype(F32))
    return out


def blocks_of(length):
    step = 128 if length % 128 == 0 else length
    return [(i * step, step) for i in range(length // step)]


def seen(seg_col, seg_row, start, step):
    stop = start + step
    row = start + lax.broadcasted_iota(jnp.int32, (step, stop), 0)
    col = lax.broadcasted_iota(jnp.int32, (step, stop), 1)
    return (col <= row) & (seg_col[start:stop, :] == seg_row[:, :stop])


def attend_kernel(scale, head, q_ref, k_ref, v_ref, seg_col, seg_row, o_ref, lse_ref):
    length = q_ref.shape[0]
    for start, step in blocks_of(length):
        stop = start + step
        mask = seen(seg_col, seg_row, start, step)
        for h in range(q_ref.shape[1] // head):
            lanes = slice(h * head, (h + 1) * head)
            scores = dot_t(q_ref[start:stop, lanes], k_ref[:stop, lanes]) * scale
            scores = jnp.where(mask, scores, -1e30)
            top = jnp.max(scores, -1, keepdims=True)
            expo = jnp.exp(scores - top)
            total = jnp.sum(expo, -1, keepdims=True)
            probs = (expo * (1.0 / total)).astype(BF16)
            o_ref[start:stop, lanes] = dot(probs, v_ref[:stop, lanes]).astype(BF16)
            lse_ref[h, start:stop, :] = top + jnp.log(total)


def attend_back_kernel(
    scale, head, q_ref, k_ref, v_ref, do_ref, lse_ref, seg_col, seg_row, dq_ref, dk_ref, dv_ref
):
    length = q_ref.shape[0]
    dk_ref[...] = jnp.zeros_like(dk_ref)
    dv_ref[...] = jnp.zeros_like(dv_ref)
    over_rows = (((0,), (0,)), ((), ()))
    for start, step in blocks_of(length):
        stop = start + step
        mask = seen(seg_col, seg_row, start, step)
        for h in range(q_ref.shape[1] // head):
            lanes = slice(h * head, (h + 1) * head)
            query = q_ref[start:stop, lanes]
            keys = k_ref[:stop, lanes]
            grad = do_ref[start:stop, lanes]
            scores = dot_t(query, keys) * scale
            probs = jnp.exp(jnp.where(mask, scores - lse_ref[h, start:stop, :], -1e30))
            d_probs = dot_t(grad, v_ref[:stop, lanes])
            delta = jnp.sum(probs * d_probs, -1, keepdims=True)
            d_scores = (probs * (d_probs - delta)).astype(BF16)
            dq_ref[start:stop, lanes] = dot(d_scores, keys) * scale
            dk_ref[:stop, lanes] += (
                lax.dot_general(d_scores, query, over_rows, preferred_element_type=F32) * scale
            )
            dv_ref[:stop, lanes] += lax.dot_general(
                probs.astype(BF16), grad, over_rows, preferred_element_type=F32
            )


def attention_specs(length, width, head):
    group = max(head, 128)
    wide = pl.BlockSpec((length, group), lambda i: (0, i))
    lse = pl.BlockSpec((group // head, length, 1), lambda i: (i, 0, 0))
    segs = [
        pl.BlockSpec((length, 1), lambda i: (0, 0)),
        pl.BlockSpec((1, length), lambda i: (0, 0)),
    ]
    return wide, lse, segs, (width // group,)


def attend(query, keys, values, seg_col, seg_row, head):
    length, width = query.shape
    wide, lse, segs, grid = attention_specs(length, width, head)
    heads = width // head

    def kernel(*refs):
        attend_kernel(1.0 / math.sqrt(head), head, *refs)

    return pl.pallas_call(
        kernel,
        grid=grid,
        in_specs=[wide, wide, wide, *segs],
        out_specs=[wide, lse],
        out_shape=[
            jax.ShapeDtypeStruct((length, width), BF16),
            jax.ShapeDtypeStruct((heads, length, 1), F32),
        ],
        compiler_params=pltpu.CompilerParams(vmem_limit_bytes=VMEM_LIMIT),
        cost_estimate=pl.CostEstimate(
            flops=4 * length * length * width,
            bytes_accessed=8 * length * width,
            transcendentals=heads * length * length,
        ),
    )(query, keys, values, seg_col, seg_row)


def attend_back(query, keys, values, d_mixed, lse_all, seg_col, seg_row, head):
    length, width = query.shape
    wide, lse, segs, grid = attention_specs(length, width, head)
    heads = width // head

    def kernel(*refs):
        attend_back_kernel(1.0 / math.sqrt(head), head, *refs)

    out = jax.ShapeDtypeStruct((length, width), F32)
    return pl.pallas_call(
        kernel,
        grid=grid,
        in_specs=[wide, wide, wide, wide, lse, *segs],
        out_specs=[wide, wide, wide],
        out_shape=[out, out, out],
        compiler_params=pltpu.CompilerParams(vmem_limit_bytes=VMEM_LIMIT),
        cost_estimate=pl.CostEstimate(
            flops=10 * length * length * width,
            bytes_accessed=20 * length * width,
            transcendentals=heads * length * length,
        ),
    )(query, keys, values, d_mixed, lse_all, seg_col, seg_row)


def rotary_tables(positions, head, heads):
    half = ROT // 2
    inverse = jnp.power(10000.0, -2.0 * jnp.arange(half, dtype=F32) / ROT)
    angles = positions.astype(F32)[:, None] * inverse
    cos, sin = jnp.cos(angles), jnp.sin(angles)
    rest = jnp.zeros((positions.shape[0], head - ROT), F32)
    none = jnp.zeros_like(sin)
    keep = jnp.concatenate([cos, cos, rest + 1.0], 1)
    upper = jnp.concatenate([-sin, none, rest], 1)
    lower = jnp.concatenate([none, sin, rest], 1)
    return [jnp.tile(t, (1, heads)) for t in (keep, upper, lower)]


def rotate(u, tables):
    keep, upper, lower = tables
    half = ROT // 2
    return u * keep + jnp.roll(u, -half, 1) * upper + jnp.roll(u, half, 1) * lower


def rotate_back(d, tables):
    keep, upper, lower = tables
    half = ROT // 2
    return d * keep + jnp.roll(d * upper, half, 1) + jnp.roll(d * lower, -half, 1)


def normalise(x):
    centred = x - jnp.mean(x, -1, keepdims=True)
    spread = jnp.mean(centred * centred, -1, keepdims=True)
    inverse = lax.rsqrt(spread + EPS)
    return centred * inverse, inverse


def forward_layer(x, weights, small, tables, segs, head):
    w_qkv, w_out, w_up, w_down = weights
    gains, shifts, b_qkv, b_out, b_up, b_down = small
    xhat, inverse = normalise(x)
    attn_low = (xhat * gains[0] + shifts[0]).astype(BF16)
    mlp_low = (xhat * gains[1] + shifts[1]).astype(BF16)
    projected = dot(attn_low, w_qkv) + b_qkv
    width = projected.shape[1] // 3
    query = rotate(projected[:, :width], tables).astype(BF16)
    keys = rotate(projected[:, width : 2 * width], tables).astype(BF16)
    values = projected[:, 2 * width :].astype(BF16)
    mixed_low, lse = attend(query, keys, values, *segs, head)
    hidden_pre = dot(mlp_low, w_up) + b_up
    cdf = 0.5 * (1.0 + lax.erf(hidden_pre * ROOT_HALF))
    hidden_low = (hidden_pre * cdf).astype(BF16)
    part = (dot(mixed_low, w_out) + dot(hidden_low, w_down)).astype(BF16)
    other = swap(part, "core")
    y = x + (part.astype(F32) + other.astype(F32) + b_out + b_down)
    return y, (
        xhat,
        inverse,
        attn_low,
        mlp_low,
        query,
        keys,
        values,
        mixed_low,
        lse,
        hidden_pre,
        hidden_low,
    )


def backward_layer(dy, weights, small, saved, tables, segs, head, place, x_first):
    w_qkv, w_out, w_up, w_down = weights
    gains = small[0]
    (
        xhat,
        inverse,
        attn_low,
        mlp_low,
        query,
        keys,
        values,
        mixed_low,
        lse,
        hidden_pre,
        hidden_low,
    ) = saved
    dy_low = dy.astype(BF16)
    d_down = reduce_weight(hidden_low.T, dy_low, x_first, place)
    d_out = reduce_weight(mixed_low.T, dy_low, not x_first, place)
    d_branch_b = jnp.sum(dy_low.astype(F32), 0)
    d_hidden = dot_t(dy_low, w_down)
    cdf = 0.5 * (1.0 + lax.erf(hidden_pre * ROOT_HALF))
    density = jnp.exp(-0.5 * hidden_pre * hidden_pre) * (1.0 / math.sqrt(2.0 * math.pi))
    d_pre = (d_hidden * (cdf + hidden_pre * density)).astype(BF16)
    d_up = reduce_weight(mlp_low.T, d_pre, not x_first, place)
    d_up_b = jnp.sum(d_pre.astype(F32), 0)
    d_mlp = dot_t(d_pre, w_up)
    d_mixed = dot_t(dy_low, w_out).astype(BF16)
    d_query, d_keys, d_values = attend_back(
        query, keys, values, d_mixed, lse, *segs, head
    )
    d_qkv = jnp.concatenate(
        [
            rotate_back(d_query, tables).astype(BF16),
            rotate_back(d_keys, tables).astype(BF16),
            d_values.astype(BF16),
        ],
        1,
    )
    d_qkv_w = reduce_weight(attn_low.T, d_qkv, x_first, place)
    d_qkv_b = jnp.sum(d_qkv.astype(F32), 0)
    d_attn = dot_t(d_qkv, w_qkv)
    d_gains = jnp.stack([jnp.sum(d_attn * xhat, 0), jnp.sum(d_mlp * xhat, 0)])
    d_shifts = jnp.stack([jnp.sum(d_attn, 0), jnp.sum(d_mlp, 0)])
    part = (d_attn * gains[0] + d_mlp * gains[1]).astype(BF16)
    d_xhat = part.astype(F32) + swap(part, "core").astype(F32)
    dx = dy + inverse * (
        d_xhat
        - jnp.mean(d_xhat, -1, keepdims=True)
        - xhat * jnp.mean(d_xhat * xhat, -1, keepdims=True)
    )
    return dx, (d_qkv_w, d_out, d_up, d_down), (d_gains, d_shifts, d_qkv_b, d_branch_b, d_up_b)


def pick_vector(v, width, place):
    return jnp.take(v.reshape(*v.shape[:-1], -1, 2, width), place.c, axis=-2).reshape(
        *v.shape[:-1], -1
    )


def spread_vector(v, width, place):
    blocks = v.reshape(-1, 1, width)
    here = (jnp.arange(2) == place.c)[None, :, None]
    return jnp.where(here, blocks, 0.0).reshape(-1)


def reduce_small(grads, head_cols, ff_cols, place):
    d_gains, d_shifts, d_qkv_b, d_branch_b, d_up_b = grads
    parts = [
        d_gains,
        d_shifts,
        spread_vector(d_qkv_b, head_cols, place),
        jnp.where(place.c == 0, d_branch_b, 0.0),
        spread_vector(d_up_b, ff_cols, place),
    ]
    shapes = [p.shape for p in parts]
    flat = lax.psum(
        jnp.concatenate([p.reshape(-1) for p in parts]), (*AXES, "shard")
    )
    out, start = [], 0
    for shape in shapes:
        size = math.prod(shape)
        part = flat[start : start + size].reshape(shape)
        start += size
        own = shape[-1] // place.span
        out.append(lax.dynamic_slice_in_dim(part, place.z * own, own, len(shape) - 1))
    return out


def join_columns(half, width, place):
    other = swap(half, "core")
    even = jnp.where(place.c == 0, half, other)
    odd = jnp.where(place.c == 0, other, half)
    parts = []
    for j in range(half.shape[1] // width):
        lanes = slice(j * width, (j + 1) * width)
        parts += [even[:, lanes], odd[:, lanes]]
    return jnp.concatenate(parts, 1).astype(F32)


def join_rows(half, place):
    return by_core(place, half, swap(half, "core"), 0).astype(F32)


def on_device(span, *arguments):
    (
        hidden_in,
        segments,
        norm_gains,
        norm_biases,
        qkv_weight,
        qkv_bias,
        out_weight,
        out_bias,
        up_weight,
        up_bias,
        down_weight,
        down_bias,
        out_grad,
    ) = arguments
    place = Place(span)
    rows = hidden_in.shape[0]
    width = hidden_in.shape[2]
    head = width // H
    head_cols = width // (2 * span)
    ff_cols = up_weight.shape[2] // (2 * span)
    assert 2 * rows == span

    x = row_to_chip(hidden_in, place)
    seg_all = by_core(place, segments, swap(segments, "core"), 0)
    seg = lax.dynamic_index_in_dim(seg_all, place.z, 0, keepdims=False)
    seg_col, seg_row = seg[:, None], seg[None, :]
    length = seg.shape[0]
    earlier = jnp.sum((seg_row < seg_col).astype(jnp.int32), -1)
    positions = jnp.arange(length, dtype=jnp.int32) - earlier
    tables = rotary_tables(positions, head, H // 2)
    segs = (seg_col, seg_row)

    small = gather_small(
        [norm_gains, norm_biases, qkv_bias, out_bias, up_bias, down_bias], place
    )
    gains, shifts, b_qkv, b_out, b_up, b_down = small
    b_qkv = pick_vector(b_qkv, head_cols, place)
    b_up = pick_vector(b_up, ff_cols, place)

    def my_rows(w):
        half = w.shape[0] // 2
        return lax.dynamic_slice_in_dim(w, place.c * half, half, 0)

    gate = x
    weights = []
    for layer in range(LAYERS):
        x_first = layer % 2 == 0
        w_qkv, gate = gather_weight(
            pick_columns(qkv_weight[layer], head_cols, place), x_first, gate, place
        )
        w_up, gate = gather_weight(
            pick_columns(up_weight[layer], ff_cols, place), not x_first, gate, place
        )
        w_out, gate = gather_weight(my_rows(out_weight[layer]), x_first, gate, place)
        w_down, gate = gather_weight(
            my_rows(down_weight[layer]), not x_first, gate, place
        )
        weights.append((w_qkv, w_out, w_up, w_down))
    dy = row_to_chip(after(out_grad, gate), place)

    stream = x.astype(F32)
    kept = []
    smalls = []
    for layer in range(LAYERS):
        small = (
            gains[layer],
            shifts[layer],
            b_qkv[layer],
            b_out[layer],
            b_up[layer],
            b_down[layer],
        )
        smalls.append(small)
        stream, saved = forward_layer(stream, weights[layer], small, tables, segs, head)
        kept.append(saved)
    block_out = chip_to_rows(stream.astype(BF16), rows, place)

    dy = dy.astype(F32)
    big = [None] * LAYERS
    little = [None] * LAYERS
    for layer in reversed(range(LAYERS)):
        dy, grads, small_grads = backward_layer(
            dy,
            weights[layer],
            smalls[layer],
            kept[layer],
            tables,
            segs,
            head,
            place,
            layer % 2 == 0,
        )
        d_qkv_w, d_out, d_up, d_down = grads
        big[layer] = (
            join_columns(d_qkv_w, head_cols, place),
            join_rows(d_out, place),
            join_columns(d_up, ff_cols, place),
            join_rows(d_down, place),
        )
        little[layer] = reduce_small(small_grads, head_cols, ff_cols, place)
    in_grad = chip_to_rows(dy.astype(BF16), rows, place).astype(F32)
    d_qkv_w, d_out_w, d_up_w, d_down_w = [
        jnp.stack([grads[i] for grads in big]) for i in range(4)
    ]
    d_gains, d_shifts, d_qkv_b, d_branch_b, d_up_b = [
        jnp.stack([grads[i] for grads in little]) for i in range(5)
    ]
    return (
        block_out,
        in_grad,
        d_gains,
        d_shifts,
        d_qkv_w,
        d_qkv_b,
        d_out_w,
        d_branch_b,
        d_up_w,
        d_up_b,
        d_down_w,
        d_branch_b,
    )


def solution(mesh):
    rep, span = mesh.shape["rep"], mesh.shape["shard"]
    fine = Mesh(mesh.devices.reshape(rep // 8, 2, 2, 2, span), (*AXES, "shard"))
    tokens = P(AXES, "shard", None)
    last = P(None, None, "shard")
    middle = P(None, "shard", None)
    vector = P(None, "shard")
    in_specs = (
        tokens,
        P(AXES, None),
        last,
        last,
        middle,
        vector,
        middle,
        vector,
        middle,
        vector,
        middle,
        vector,
        tokens,
    )
    out_specs = (
        tokens,
        tokens,
        last,
        last,
        middle,
        vector,
        middle,
        vector,
        middle,
        vector,
        middle,
        vector,
    )

    def step(*arguments):
        return on_device(span, *arguments)

    return jax.shard_map(
        step, mesh=fine, in_specs=in_specs, out_specs=out_specs, check_vma=False
    )
```

```python
import math

import jax
import jax.numpy as jnp
from jax import lax
from jax.experimental import pallas as pl
from jax.experimental.pallas import tpu as pltpu
from jax.sharding import Mesh
from jax.sharding import PartitionSpec as P

H = 16
ROT = 16
LAYERS = 2
EPS = 1e-05
ROOT_HALF = math.sqrt(0.5)
F32 = jnp.float32
BF16 = jnp.bfloat16
AXES = ("outer", "ybit", "xbit", "core")
VMEM_LIMIT = 48 * 1024 * 1024


def swap(x, axis):
    return lax.ppermute(x, axis, [(0, 1), (1, 0)])


def spin(x, k, span):
    return lax.ppermute(x, "shard", [(j, (j + k) % span) for j in range(span)])


def dot(a, b):
    return jnp.dot(a, b, preferred_element_type=F32)


def dot_t(a, b):
    return lax.dot_general(a, b, (((1,), (1,)), ((), ())), preferred_element_type=F32)


class Place:
    def __init__(self, span):
        self.span = span
        self.z = lax.axis_index("shard")
        self.c = lax.axis_index("core")
        self.bx = lax.axis_index("xbit")
        self.by = lax.axis_index("ybit")
        self.q = 2 * self.by + self.bx
        self.scalars = jnp.stack([self.z, self.q, self.c]).astype(jnp.int32)


def from_relative(blocks, place):
    span = place.span
    order = [blocks[(-m) % span] for m in range(2 * span - 1)]
    return lax.dynamic_slice_in_dim(
        jnp.stack(order), lax.rem(span - place.z, span), span, 0
    )


def by_core(place, own, other, axis):
    return jnp.where(
        place.c == 0,
        jnp.concatenate([own, other], axis),
        jnp.concatenate([other, own], axis),
    )


def copy_call(body, out_shape, copies, operands, place):
    def kernel(scalars, *refs):
        ins, out, sems = refs[: len(operands)], refs[len(operands)], refs[-1]
        started = []
        for slot, (src, dst) in enumerate(body(scalars, ins, out)):
            copy = pltpu.make_async_copy(src, dst, sems.at[slot])
            copy.start()
            started.append(copy)
        for copy in started:
            copy.wait()

    size = 2 * math.prod(out_shape.shape) * out_shape.dtype.itemsize
    return pl.pallas_call(
        kernel,
        out_shape=out_shape,
        in_specs=[pl.BlockSpec(memory_space=pltpu.SMEM)]
        + [pl.BlockSpec(memory_space=pl.ANY)] * len(operands),
        out_specs=pl.BlockSpec(memory_space=pltpu.VMEM),
        scratch_shapes=[pltpu.SemaphoreType.DMA((copies,))],
        compiler_params=pltpu.CompilerParams(vmem_limit_bytes=VMEM_LIMIT),
        cost_estimate=pl.CostEstimate(flops=0, bytes_accessed=size, transcendentals=0),
    )(place.scalars, *operands)


def pick_columns(weights, layer, width, place):
    rows, columns = weights.shape[1:]
    count = columns // (2 * width)

    def body(scalars, ins, out):
        core = scalars[2]
        for j in range(count):
            start = pl.multiple_of((2 * j + core) * width, width)
            yield (
                ins[0].at[layer, :, pl.ds(start, width)],
                out.at[:, pl.ds(j * width, width)],
            )

    shape = jax.ShapeDtypeStruct((rows, count * width), weights.dtype)
    return copy_call(body, shape, count, [weights], place)


def pick_rows(arrays, layer, place):
    halves = [w.shape[1] // 2 for w in arrays]

    def body(scalars, ins, out):
        start = 0
        for ref, half in zip(ins, halves, strict=True):
            first = pl.multiple_of(scalars[2] * half, half)
            yield ref.at[layer, pl.ds(first, half)], out.at[pl.ds(start, half)]
            start += half

    shape = jax.ShapeDtypeStruct((sum(halves), arrays[0].shape[2]), arrays[0].dtype)
    return copy_call(body, shape, len(arrays), list(arrays), place)


def other_shards(table, place):
    span = place.span

    def body(scalars, ins, out):
        for k in range(1, span):
            source = lax.rem(scalars[0] + (span - k), span)
            for i in range(2):
                yield ins[0].at[source, i], out.at[i, k - 1]

    shape = jax.ShapeDtypeStruct((2, span - 1, *table.shape[2:]), table.dtype)
    return copy_call(body, shape, 2 * (span - 1), [table], place)


def flipped(q, flip):
    return lax.bitwise_xor(q, jnp.int32(flip))


def assemble(half, near, near_x, near_y, far_a, far_b, place):
    span = place.span
    eighth, columns = half.shape[0] // 8, half.shape[1]

    def body(scalars, ins, out):
        z, q = scalars[0], scalars[1]
        yield ins[0], out.at[z]
        for k in range(1, span):
            source = lax.rem(z + (span - k), span)
            for i in range(2):
                for flip in range(3):
                    yield ins[1 + flip].at[i, k - 1], out.at[source, flipped(q, flip), i]
                yield ins[4 + i].at[k - 1], out.at[source, flipped(q, 3), i]

    shape = jax.ShapeDtypeStruct((span, 4, 2, eighth, columns), half.dtype)
    half = half.reshape(4, 2, eighth, columns)
    operands = [half, near, near_x, near_y, far_a, far_b]
    out = copy_call(body, shape, 1 + 8 * (span - 1), operands, place)
    return out.reshape(8 * span * eighth, columns)


def weight_gradient(left, right, place):
    span = place.span
    tokens, columns = left.shape[0], right.shape[1]
    rows = left.shape[1] // span
    eighth = rows // 8

    def kernel(scalars, left_ref, right_ref, own, pass_a, pass_b, send_a, send_b, table):
        q = scalars[1]
        product = lax.dot_general(
            left_ref[...],
            right_ref[...],
            (((0,), (0,)), ((), ())),
            preferred_element_type=F32,
        ).astype(BF16)
        for j in range(8):
            table[j // 2, j % 2] = product[j * eighth : (j + 1) * eighth]
        near_x, near_y, far = flipped(q, 1), flipped(q, 2), flipped(q, 3)
        own[0, 0], own[0, 1] = table[q, 0], table[q, 1]
        pass_a[0], pass_b[0] = table[near_y, 0], table[near_x, 1]
        send_a[0, 0], send_a[1, 0] = table[near_x, 0], table[far, 0]
        send_b[0, 0], send_b[1, 0] = table[near_y, 1], table[far, 1]

    block = (eighth, columns)
    one = pl.BlockSpec((1, *block), lambda k, s: (k, 0, 0))
    two = pl.BlockSpec((2, 1, *block), lambda k, s: (0, k, 0, 0))
    return pl.pallas_call(
        kernel,
        grid_spec=pltpu.PrefetchScalarGridSpec(
            num_scalar_prefetch=1,
            grid=(span,),
            in_specs=[
                pl.BlockSpec((tokens, rows), lambda k, s: (0, lax.rem(s[0] + k, span))),
                pl.BlockSpec((tokens, columns), lambda k, s: (0, 0)),
            ],
            out_specs=[
                pl.BlockSpec((1, 2, *block), lambda k, s: (k, 0, 0, 0)),
                one,
                one,
                two,
                two,
            ],
            scratch_shapes=[pltpu.VMEM((4, 2, *block), BF16)],
        ),
        out_shape=[
            jax.ShapeDtypeStruct((span, 2, *block), BF16),
            jax.ShapeDtypeStruct((span, *block), BF16),
            jax.ShapeDtypeStruct((span, *block), BF16),
            jax.ShapeDtypeStruct((2, span, *block), BF16),
            jax.ShapeDtypeStruct((2, span, *block), BF16),
        ],
        compiler_params=pltpu.CompilerParams(vmem_limit_bytes=VMEM_LIMIT),
        cost_estimate=pl.CostEstimate(
            flops=2 * tokens * span * rows * columns,
            bytes_accessed=2 * (tokens * (span * rows + columns) + span * rows * columns),
            transcendentals=0,
        ),
    )(place.scalars, left, right)


def combine(own, got_a, got_b, more_a, more_b):
    span, _, eighth, columns = own.shape
    part = columns // 4 if columns % 512 == 0 else columns

    def kernel(own_ref, ga_ref, gb_ref, ma_ref, mb_ref, *outs):
        for k in range(span):
            for i, (got, more) in enumerate(((ga_ref, ma_ref), (gb_ref, mb_ref))):
                total = own_ref[k, i].astype(F32) + got[0, k].astype(F32)
                outs[k][i] = (total + more[k].astype(F32)).astype(BF16)

    got = pl.BlockSpec((1, span, eighth, part), lambda j: (0, 0, 0, j))
    more = pl.BlockSpec((span, eighth, part), lambda j: (0, 0, j))
    out = pl.BlockSpec((2, eighth, part), lambda j: (0, 0, j))
    return pl.pallas_call(
        kernel,
        grid=(columns // part,),
        in_specs=[
            pl.BlockSpec((span, 2, eighth, part), lambda j: (0, 0, 0, j)),
            got,
            got,
            more,
            more,
        ],
        out_specs=[out] * span,
        out_shape=[jax.ShapeDtypeStruct((2, eighth, columns), BF16)] * span,
        compiler_params=pltpu.CompilerParams(vmem_limit_bytes=VMEM_LIMIT),
        cost_estimate=pl.CostEstimate(
            flops=4 * span * eighth * columns,
            bytes_accessed=16 * span * eighth * columns,
            transcendentals=0,
        ),
    )(own, got_a, got_b, more_a, more_b)


def finish_columns(parts, width, layer, previous):
    _, _, rows, columns = parts.shape

    def kernel(part_ref, *rest):
        out_ref = rest[-1]
        for core in range(2):
            for j in range(columns // width):
                start = (2 * j + core) * width
                out_ref[0, :, start : start + width] = part_ref[
                    0, core, :, j * width : (j + 1) * width
                ].astype(F32)

    operands, in_specs, aliases = (
        [parts],
        [pl.BlockSpec((1, 2, rows, columns), lambda q: (q, 0, 0, 0))],
        {},
    )
    if previous is not None:
        operands.append(previous)
        in_specs.append(pl.BlockSpec(memory_space=pl.ANY))
        aliases = {1: 0}
    return pl.pallas_call(
        kernel,
        grid=(4,),
        in_specs=in_specs,
        out_specs=pl.BlockSpec((1, rows, 2 * columns), lambda q: (layer, q, 0)),
        out_shape=jax.ShapeDtypeStruct((LAYERS, 4 * rows, 2 * columns), F32),
        input_output_aliases=aliases,
        compiler_params=pltpu.CompilerParams(vmem_limit_bytes=VMEM_LIMIT),
        cost_estimate=pl.CostEstimate(
            flops=0, bytes_accessed=48 * rows * columns, transcendentals=0
        ),
    )(*operands)


def finish_rows(parts, first_rows, layer, previous):
    _, _, quarter, columns = parts.shape
    sizes = (first_rows, 4 * quarter - first_rows)

    def kernel(part_ref, *rest):
        first, second = rest[-2:]
        for q in range(4):
            start, stop = q * quarter, (q + 1) * quarter
            cut = min(max(first_rows, start), stop)
            if cut > start:
                first[0, :, start:cut] = part_ref[q, :, : cut - start].astype(F32)
            if stop > cut:
                second[0, :, cut - first_rows : stop - first_rows] = part_ref[
                    q, :, cut - start :
                ].astype(F32)

    half = columns // 4 if columns % 512 == 0 else columns
    operands, aliases = [parts], {}
    in_specs = [pl.BlockSpec((4, 2, quarter, half), lambda j: (0, 0, 0, j))]
    if previous is not None:
        operands += list(previous)
        in_specs += [pl.BlockSpec(memory_space=pl.ANY)] * 2
        aliases = {1: 0, 2: 1}
    return pl.pallas_call(
        kernel,
        grid=(columns // half,),
        in_specs=in_specs,
        out_specs=[
            pl.BlockSpec((1, 2, size, half), lambda j: (layer, 0, 0, j)) for size in sizes
        ],
        out_shape=[
            jax.ShapeDtypeStruct((LAYERS, 2, size, columns), F32) for size in sizes
        ],
        input_output_aliases=aliases,
        compiler_params=pltpu.CompilerParams(vmem_limit_bytes=VMEM_LIMIT),
        cost_estimate=pl.CostEstimate(
            flops=0, bytes_accessed=48 * quarter * columns, transcendentals=0
        ),
    )(*operands)


def row_to_chip(x, place):
    span = place.span
    rows, tokens, width = x.shape
    half = width // 2
    mine = lax.dynamic_slice_in_dim(x, place.c * half, half, 2)
    theirs = lax.dynamic_slice_in_dim(x, (1 - place.c) * half, half, 2)
    rows_all = by_core(place, mine, swap(theirs, "core"), 0)
    blocks = []
    for k in range(span):
        block = lax.dynamic_index_in_dim(
            rows_all, lax.rem(place.z + k, span), 0, keepdims=False
        )
        blocks.append(block if k == 0 else spin(block, k, span))
    own = from_relative(blocks, place).reshape(span * tokens, half)
    return by_core(place, own, swap(own, "core"), 1)


def chip_to_rows(y, rows, place):
    span = place.span
    width = y.shape[1]
    tokens = y.shape[0] // span
    half = width // 2
    mine = lax.dynamic_slice_in_dim(y, place.c * half, half, 1)
    mine = mine.reshape(span, tokens, half)
    blocks = []
    for k in range(span):
        block = lax.dynamic_index_in_dim(
            mine, lax.rem(place.z + k, span), 0, keepdims=False
        )
        blocks.append(block if k == 0 else spin(block, k, span))
    stacked = from_relative(blocks, place)
    own = lax.dynamic_slice_in_dim(stacked, place.c * rows, rows, 0)
    theirs = lax.dynamic_slice_in_dim(stacked, (1 - place.c) * rows, rows, 0)
    return by_core(place, own, swap(theirs, "core"), 2)


class Slots:
    def __init__(self):
        self.parts = []

    def add(self, part, done):
        self.parts.append([part, next(part), done])

    def step(self, extra=()):
        pending, extra = lax.optimization_barrier(
            ([part[1] for part in self.parts], extra)
        )
        alive = []
        for part, arrived in zip(self.parts, pending, strict=True):
            try:
                part[1] = part[0].send(arrived)
                alive.append(part)
            except StopIteration as end:
                part[2](end.value)
        self.parts = alive
        return extra


def gather_weight(half, place):
    eighth, columns = half.shape[0] // 8, half.shape[1]
    mine = lax.dynamic_index_in_dim(
        half.reshape(4, 2, eighth, columns), place.q, 0, keepdims=False
    )
    mine = yield mine
    every = yield lax.all_gather(mine, "shard")
    near = other_shards(every, place)
    near_x, near_y = yield [swap(near, "xbit"), swap(near, "ybit")]
    far_a, far_b = yield [swap(near_x[0], "ybit"), swap(near_y[1], "xbit")]
    return assemble(half, near, near_x, near_y, far_a, far_b, place)


def reduce_weight(left, right, place):
    span = place.span
    own, pass_a, pass_b, send_a, send_b = yield weight_gradient(left, right, place)
    got_a, got_b = yield [swap(send_a, "xbit"), swap(send_b, "ybit")]
    onward_a = (pass_a.astype(F32) + got_a[1].astype(F32)).astype(BF16)
    onward_b = (pass_b.astype(F32) + got_b[1].astype(F32)).astype(BF16)
    more_a, more_b = yield [swap(onward_a, "ybit"), swap(onward_b, "xbit")]
    total = combine(own, got_a, got_b, more_a, more_b)
    arrived = yield [spin(total[k], k, span) for k in range(1, span)]
    summed = total[0].astype(F32)
    for other in arrived:
        summed = summed + other.astype(F32)
    summed = summed.astype(BF16)
    if lax.axis_size("outer") > 1:
        summed = lax.psum(summed, "outer")
    parts = lax.all_gather(summed, ("ybit", "xbit", "core"))
    _, eighth, columns = summed.shape
    return parts.reshape(4, 2, 2 * eighth, columns)


def gather_small(vectors, place):
    flat = jnp.concatenate([v.reshape(-1) for v in vectors])
    blocks = [flat] + [spin(flat, k, place.span) for k in range(1, place.span)]
    table = from_relative(blocks, place)
    out, start = [], 0
    for v in vectors:
        part = table[:, start : start + v.size].reshape(place.span, *v.shape)
        start += v.size
        part = jnp.moveaxis(part, 0, -2)
        out.append(part.reshape(*v.shape[:-1], -1).astype(F32))
    return out


def blocks_of(length):
    step = 128 if length % 128 == 0 else length
    return [(i * step, step) for i in range(length // step)]


def seen(seg_col, seg_row, start, step):
    stop = start + step
    row = start + lax.broadcasted_iota(jnp.int32, (step, stop), 0)
    col = lax.broadcasted_iota(jnp.int32, (step, stop), 1)
    return (col <= row) & (seg_col[start:stop, :] == seg_row[:, :stop])


def turn(u, tables):
    keep, upper, lower = tables
    half, lanes = ROT // 2, u.shape[1]
    return u * keep + pltpu.roll(u, lanes - half, 1) * upper + pltpu.roll(u, half, 1) * lower


def turn_back(d, tables):
    keep, upper, lower = tables
    half, lanes = ROT // 2, d.shape[1]
    return d * keep + pltpu.roll(d * upper, half, 1) + pltpu.roll(d * lower, lanes - half, 1)


def attend_kernel(scale, head, *refs):
    q_in, k_in, v_in, keep, upper, lower, seg_col, seg_row = refs[:8]
    q_ref, k_ref, v_ref, o_ref, lse_ref = refs[8:]
    tables = keep[...], upper[...], lower[...]
    q_ref[...] = turn(q_in[...], tables).astype(BF16)
    k_ref[...] = turn(k_in[...], tables).astype(BF16)
    v_ref[...] = v_in[...].astype(BF16)
    for start, step in blocks_of(q_ref.shape[0]):
        stop = start + step
        mask = seen(seg_col, seg_row, start, step)
        for h in range(q_ref.shape[1] // head):
            lanes = slice(h * head, (h + 1) * head)
            scores = dot_t(q_ref[start:stop, lanes], k_ref[:stop, lanes]) * scale
            scores = jnp.where(mask, scores, -1e30)
            top = jnp.max(scores, -1, keepdims=True)
            expo = jnp.exp(scores - top)
            total = jnp.sum(expo, -1, keepdims=True)
            probs = (expo * (1.0 / total)).astype(BF16)
            o_ref[start:stop, lanes] = dot(probs, v_ref[:stop, lanes]).astype(BF16)
            lse_ref[h, start:stop, :] = top + jnp.log(total)


def attend_back_kernel(scale, head, *refs):
    q_ref, k_ref, v_ref, do_ref, lse_ref, keep, upper, lower, seg_col, seg_row = refs[:10]
    dq_out, dk_out, dv_out, dq_ref, dk_ref, dv_ref = refs[10:]
    dk_ref[...] = jnp.zeros_like(dk_ref)
    dv_ref[...] = jnp.zeros_like(dv_ref)
    over_rows = (((0,), (0,)), ((), ()))
    for start, step in blocks_of(q_ref.shape[0]):
        stop = start + step
        mask = seen(seg_col, seg_row, start, step)
        for h in range(q_ref.shape[1] // head):
            lanes = slice(h * head, (h + 1) * head)
            query = q_ref[start:stop, lanes]
            keys = k_ref[:stop, lanes]
            grad = do_ref[start:stop, lanes]
            scores = dot_t(query, keys) * scale
            probs = jnp.exp(jnp.where(mask, scores - lse_ref[h, start:stop, :], -1e30))
            d_probs = dot_t(grad, v_ref[:stop, lanes])
            delta = jnp.sum(probs * d_probs, -1, keepdims=True)
            d_scores = (probs * (d_probs - delta)).astype(BF16)
            dq_ref[start:stop, lanes] = dot(d_scores, keys) * scale
            dk_ref[:stop, lanes] += (
                lax.dot_general(d_scores, query, over_rows, preferred_element_type=F32) * scale
            )
            dv_ref[:stop, lanes] += lax.dot_general(
                probs.astype(BF16), grad, over_rows, preferred_element_type=F32
            )
    tables = keep[...], upper[...], lower[...]
    dq_out[...] = turn_back(dq_ref[...], tables).astype(BF16)
    dk_out[...] = turn_back(dk_ref[...], tables).astype(BF16)
    dv_out[...] = dv_ref[...].astype(BF16)


def attention_specs(length, width, head):
    group = max(head, 128)
    count = width // group
    wide = pl.BlockSpec((length, group), lambda i: (0, i))
    lse = pl.BlockSpec((group // head, length, 1), lambda i: (i, 0, 0))
    same = [pl.BlockSpec((length, group), lambda i: (0, 0))] * 3 + [
        pl.BlockSpec((length, 1), lambda i: (0, 0)),
        pl.BlockSpec((1, length), lambda i: (0, 0)),
    ]
    return group, count, wide, lse, same


def attend(projected, fixed, head):
    length, width = projected.shape[0], projected.shape[1] // 3
    group, count, wide, lse, same = attention_specs(length, width, head)

    def kernel(*refs):
        attend_kernel(1.0 / math.sqrt(head), head, *refs)

    low = jax.ShapeDtypeStruct((length, width), BF16)
    return pl.pallas_call(
        kernel,
        grid=(count,),
        in_specs=[
            wide,
            pl.BlockSpec((length, group), lambda i: (0, count + i)),
            pl.BlockSpec((length, group), lambda i: (0, 2 * count + i)),
            *same,
        ],
        out_specs=[wide, wide, wide, wide, lse],
        out_shape=[
            low,
            low,
            low,
            low,
            jax.ShapeDtypeStruct((width // head, length, 1), F32),
        ],
        compiler_params=pltpu.CompilerParams(vmem_limit_bytes=VMEM_LIMIT),
        cost_estimate=pl.CostEstimate(
            flops=4 * length * length * width,
            bytes_accessed=20 * length * width,
            transcendentals=width // head * length * length,
        ),
    )(projected, projected, projected, *fixed)


def attend_back(query, keys, values, d_mixed, lse_all, fixed, head):
    length, width = query.shape
    group, count, wide, lse, same = attention_specs(length, width, head)

    def kernel(*refs):
        attend_back_kernel(1.0 / math.sqrt(head), head, *refs)

    out = jax.ShapeDtypeStruct((length, width), BF16)
    return pl.pallas_call(
        kernel,
        grid=(count,),
        in_specs=[wide, wide, wide, wide, lse, *same],
        out_specs=[wide, wide, wide],
        out_shape=[out, out, out],
        scratch_shapes=[pltpu.VMEM((length, group), F32)] * 3,
        compiler_params=pltpu.CompilerParams(vmem_limit_bytes=VMEM_LIMIT),
        cost_estimate=pl.CostEstimate(
            flops=10 * length * length * width,
            bytes_accessed=20 * length * width,
            transcendentals=width // head * length * length,
        ),
    )(query, keys, values, d_mixed, lse_all, *fixed)


def rotary_tables(positions, head):
    half = ROT // 2
    inverse = jnp.power(10000.0, -2.0 * jnp.arange(half, dtype=F32) / ROT)
    angles = positions.astype(F32)[:, None] * inverse
    cos, sin = jnp.cos(angles), jnp.sin(angles)
    rest = jnp.zeros((positions.shape[0], head - ROT), F32)
    none = jnp.zeros_like(sin)
    keep = [cos, cos, rest + 1.0]
    upper = [-sin, none, rest]
    lower = [none, sin, rest]
    times = max(1, 128 // head)
    return [jnp.concatenate(t * times, 1) for t in (keep, upper, lower)]


def normalise(x):
    centred = x - jnp.mean(x, -1, keepdims=True)
    spread = jnp.mean(centred * centred, -1, keepdims=True)
    inverse = lax.rsqrt(spread + EPS)
    return centred * inverse, inverse


def interleave(first, second, span):
    a, b = first.shape[1] // span, second.shape[1] // span
    parts = []
    for k in range(span):
        parts += [first[:, k * a : (k + 1) * a], second[:, k * b : (k + 1) * b]]
    return jnp.concatenate(parts, 1)


def separate(both, a, b, span):
    parts = [both[:, k * (a + b) : (k + 1) * (a + b)] for k in range(span)]
    first = jnp.concatenate([p[:, :a] for p in parts], 1)
    return first, jnp.concatenate([p[:, a:] for p in parts], 1)


def forward_layer(x, weights, small, fixed, head, span):
    w_qkv, w_up, w_last = weights
    gains, shifts, b_qkv, b_out, b_up, b_down = small
    xhat, inverse = normalise(x)
    attn_low = (xhat * gains[0] + shifts[0]).astype(BF16)
    mlp_low = (xhat * gains[1] + shifts[1]).astype(BF16)
    projected = dot(attn_low, w_qkv) + b_qkv
    query, keys, values, mixed_low, lse = attend(projected, fixed, head)
    hidden_pre = dot(mlp_low, w_up) + b_up
    cdf = 0.5 * (1.0 + lax.erf(hidden_pre * ROOT_HALF))
    hidden_low = (hidden_pre * cdf).astype(BF16)
    last_low = interleave(mixed_low, hidden_low, span)
    part = dot(last_low, w_last).astype(BF16)
    other = swap(part, "core")
    y = x + (part.astype(F32) + other.astype(F32) + b_out + b_down)
    attention = (query, keys, values, lse)
    return y, (xhat, inverse, attn_low, mlp_low, attention, hidden_pre, last_low)


def backward_layer(dy, weights, small, saved, fixed, head, place, slots, done):
    w_qkv, w_up, w_last = weights
    gains = small[0]
    xhat, inverse, attn_low, mlp_low, attention, hidden_pre, last_low = saved
    query, keys, values, lse = attention
    span = place.span
    dy_low = dy.astype(BF16)
    slots.add(reduce_weight(last_low, dy_low, place), done(2))
    d_branch_b = jnp.sum(dy_low.astype(F32), 0)

    dy_low = slots.step(dy_low)
    d_mixed, d_hidden = separate(
        dot_t(dy_low, w_last), query.shape[1] // span, hidden_pre.shape[1] // span, span
    )
    d_mixed = d_mixed.astype(BF16)
    cdf = 0.5 * (1.0 + lax.erf(hidden_pre * ROOT_HALF))
    density = jnp.exp(-0.5 * hidden_pre * hidden_pre) * (1.0 / math.sqrt(2.0 * math.pi))
    d_pre = (d_hidden * (cdf + hidden_pre * density)).astype(BF16)
    slots.add(reduce_weight(mlp_low, d_pre, place), done(1))
    d_up_b = jnp.sum(d_pre.astype(F32), 0)

    d_mixed, d_pre = slots.step((d_mixed, d_pre))
    d_qkv = jnp.concatenate(
        attend_back(query, keys, values, d_mixed, lse, fixed, head), 1
    )
    slots.add(reduce_weight(attn_low, d_qkv, place), done(0))
    d_mlp = dot_t(d_pre, w_up)

    d_qkv, d_mlp = slots.step((d_qkv, d_mlp))
    d_qkv_b = jnp.sum(d_qkv.astype(F32), 0)
    d_attn = dot_t(d_qkv, w_qkv)
    part = (d_attn * gains[0] + d_mlp * gains[1]).astype(BF16)
    d_xhat = part.astype(F32) + swap(part, "core").astype(F32)
    dx = dy + inverse * (
        d_xhat
        - jnp.mean(d_xhat, -1, keepdims=True)
        - xhat * jnp.mean(d_xhat * xhat, -1, keepdims=True)
    )
    d_gains = jnp.stack([jnp.sum(d_attn * xhat, 0), jnp.sum(d_mlp * xhat, 0)])
    d_shifts = jnp.stack([jnp.sum(d_attn, 0), jnp.sum(d_mlp, 0)])
    return dx, (d_gains, d_shifts, d_qkv_b, d_branch_b, d_up_b)


def pick_vector(v, width, place):
    return jnp.take(v.reshape(*v.shape[:-1], -1, 2, width), place.c, axis=-2).reshape(
        *v.shape[:-1], -1
    )


def spread_vector(v, width, place):
    blocks = v.reshape(-1, 1, width)
    here = (jnp.arange(2) == place.c)[None, :, None]
    return jnp.where(here, blocks, 0.0).reshape(-1)


def reduce_small(layers, head_cols, ff_cols, place):
    span = place.span
    parts = []
    for d_gains, d_shifts, d_qkv_b, d_branch_b, d_up_b in layers:
        parts += [
            d_gains,
            d_shifts,
            spread_vector(d_qkv_b, head_cols, place),
            jnp.where(place.c == 0, d_branch_b, 0.0),
            spread_vector(d_up_b, ff_cols, place),
        ]
    tables = [p.reshape(-1, span, p.shape[-1] // span) for p in parts]
    flat = jnp.concatenate(
        [jnp.moveaxis(t, 1, 0).reshape(span, -1, 128) for t in tables], 1
    )
    for axis in ("core", "xbit", "ybit"):
        flat = flat + swap(flat, axis)
    if lax.axis_size("outer") > 1:
        flat = lax.psum(flat, "outer")
    mine = [
        lax.dynamic_index_in_dim(flat, lax.rem(place.z + k, span), 0, keepdims=False)
        for k in range(span)
    ]
    total = mine[0]
    for k in range(1, span):
        total = total + spin(mine[k], k, span)
    total = total.reshape(-1)
    out, start = [], 0
    for p in parts:
        size = p.size // span
        out.append(total[start : start + size].reshape(*p.shape[:-1], p.shape[-1] // span))
        start += size
    count = len(parts) // len(layers)
    return [jnp.stack(out[i::count]) for i in range(count)]


def on_device(span, *arguments):
    (
        hidden_in,
        segments,
        norm_gains,
        norm_biases,
        qkv_weight,
        qkv_bias,
        out_weight,
        out_bias,
        up_weight,
        up_bias,
        down_weight,
        down_bias,
        out_grad,
    ) = arguments
    place = Place(span)
    rows = hidden_in.shape[0]
    width = hidden_in.shape[2]
    head = width // H
    head_cols = width // (2 * span)
    ff_cols = up_weight.shape[2] // (2 * span)
    assert 2 * rows == span

    halves = []
    for layer in range(LAYERS):
        halves += [
            pick_columns(qkv_weight, layer, head_cols, place),
            pick_columns(up_weight, layer, ff_cols, place),
            pick_rows((out_weight, down_weight), layer, place),
        ]
    gathered = [None] * len(halves)
    slots = Slots()
    for index in range(len(halves) + 3):
        if index < len(halves):

            def arrived(value, index=index):
                gathered[index] = value

            slots.add(gather_weight(halves[index], place), arrived)
        slots.step()
    weights = [gathered[3 * layer : 3 * layer + 3] for layer in range(LAYERS)]

    both = row_to_chip(jnp.concatenate([hidden_in, out_grad], 2), place)
    stream, dy = both[:, :width].astype(F32), both[:, width:].astype(F32)
    seg_all = by_core(place, segments, swap(segments, "core"), 0)
    seg = lax.dynamic_index_in_dim(seg_all, place.z, 0, keepdims=False)
    seg_col, seg_row = seg[:, None], seg[None, :]
    length = seg.shape[0]
    earlier = jnp.sum((seg_row < seg_col).astype(jnp.int32), -1)
    positions = jnp.arange(length, dtype=jnp.int32) - earlier
    fixed = (*rotary_tables(positions, head), seg_col, seg_row)

    small = gather_small(
        [norm_gains, norm_biases, qkv_bias, out_bias, up_bias, down_bias], place
    )
    gains, shifts, b_qkv, b_out, b_up, b_down = small
    b_qkv = pick_vector(b_qkv, head_cols, place)
    b_up = pick_vector(b_up, ff_cols, place)
    smalls = [
        (gains[i], shifts[i], b_qkv[i], b_out[i], b_up[i], b_down[i]) for i in range(LAYERS)
    ]

    kept = []
    for layer in range(LAYERS):
        stream, saved = forward_layer(
            stream, weights[layer], smalls[layer], fixed, head, span
        )
        kept.append(saved)

    big = [None] * 3
    little = [None] * LAYERS
    slots = Slots()

    def done_for(layer):
        def of(index):
            def done(parts):
                if index == 2:
                    first_rows = out_weight.shape[1] // 2
                    big[2] = finish_rows(parts, first_rows, layer, big[2])
                else:
                    by = (head_cols, ff_cols)[index]
                    big[index] = finish_columns(parts, by, layer, big[index])

            return done

        return of

    for layer in reversed(range(LAYERS)):
        dy, little[layer] = backward_layer(
            dy,
            weights[layer],
            smalls[layer],
            kept[layer],
            fixed,
            head,
            place,
            slots,
            done_for(layer),
        )
    while slots.parts:
        slots.step()
    results = jnp.concatenate([stream.astype(BF16), dy.astype(BF16)], 1)
    results = chip_to_rows(results, rows, place)
    block_out, in_grad = results[..., :width], results[..., width:].astype(F32)
    d_gains, d_shifts, d_qkv_b, d_branch_b, d_up_b = reduce_small(
        little, head_cols, ff_cols, place
    )
    d_qkv_w, d_up_w, (d_out_w, d_down_w) = big
    d_out_w = d_out_w.reshape(LAYERS, -1, width)
    d_down_w = d_down_w.reshape(LAYERS, -1, width)
    return (
        block_out,
        in_grad,
        d_gains,
        d_shifts,
        d_qkv_w,
        d_qkv_b,
        d_out_w,
        d_branch_b,
        d_up_w,
        d_up_b,
        d_down_w,
        d_branch_b,
    )


def solution(mesh):
    rep, span = mesh.shape["rep"], mesh.shape["shard"]
    fine = Mesh(mesh.devices.reshape(rep // 8, 2, 2, 2, span), (*AXES, "shard"))
    tokens = P(AXES, "shard", None)
    last = P(None, None, "shard")
    middle = P(None, "shard", None)
    vector = P(None, "shard")
    in_specs = (
        tokens,
        P(AXES, None),
        last,
        last,
        middle,
        vector,
        middle,
        vector,
        middle,
        vector,
        middle,
        vector,
        tokens,
    )
    out_specs = (
        tokens,
        tokens,
        last,
        last,
        middle,
        vector,
        middle,
        vector,
        middle,
        vector,
        middle,
        vector,
    )

    def step(*arguments):
        return on_device(span, *arguments)

    return jax.shard_map(
        step, mesh=fine, in_specs=in_specs, out_specs=out_specs, check_vma=False
    )
```

```python
import math

import jax
import jax.numpy as jnp
from jax import lax
from jax.experimental import pallas as pl
from jax.experimental.pallas import tpu as pltpu
from jax.sharding import Mesh
from jax.sharding import PartitionSpec as P

H = 16
ROT = 16
LAYERS = 2
EPS = 1e-05
ROOT_HALF = math.sqrt(0.5)
F32 = jnp.float32
BF16 = jnp.bfloat16
AXES = ("outer", "ybit", "xbit", "core")
VMEM_LIMIT = 48 * 1024 * 1024
FORWARD_ROWS = 256
BACKWARD_ROWS = 512


def swap(x, axis):
    return lax.ppermute(x, axis, [(0, 1), (1, 0)])


def spin(x, k, span):
    return lax.ppermute(x, "shard", [(j, (j + k) % span) for j in range(span)])


def dot(a, b):
    return jnp.dot(a, b, preferred_element_type=F32)


def dot_t(a, b):
    return lax.dot_general(a, b, (((1,), (1,)), ((), ())), preferred_element_type=F32)


class Place:
    def __init__(self, span):
        self.span = span
        self.z = lax.axis_index("shard")
        self.c = lax.axis_index("core")
        self.bx = lax.axis_index("xbit")
        self.by = lax.axis_index("ybit")
        self.q = 2 * self.by + self.bx
        self.scalars = jnp.stack([self.z, self.q, self.c]).astype(jnp.int32)


def from_relative(blocks, place):
    span = place.span
    order = [blocks[(-m) % span] for m in range(2 * span - 1)]
    return lax.dynamic_slice_in_dim(
        jnp.stack(order), lax.rem(span - place.z, span), span, 0
    )


def by_core(place, own, other, axis):
    return jnp.where(
        place.c == 0,
        jnp.concatenate([own, other], axis),
        jnp.concatenate([other, own], axis),
    )


def copy_call(body, out_shape, copies, operands, place):
    def kernel(scalars, *refs):
        ins, out, sems = refs[: len(operands)], refs[len(operands)], refs[-1]
        started = []
        for slot, (src, dst) in enumerate(body(scalars, ins, out)):
            copy = pltpu.make_async_copy(src, dst, sems.at[slot])
            copy.start()
            started.append(copy)
        for copy in started:
            copy.wait()

    size = 2 * math.prod(out_shape.shape) * out_shape.dtype.itemsize
    return pl.pallas_call(
        kernel,
        out_shape=out_shape,
        in_specs=[pl.BlockSpec(memory_space=pltpu.SMEM)]
        + [pl.BlockSpec(memory_space=pl.ANY)] * len(operands),
        out_specs=pl.BlockSpec(memory_space=pltpu.VMEM),
        scratch_shapes=[pltpu.SemaphoreType.DMA((copies,))],
        compiler_params=pltpu.CompilerParams(vmem_limit_bytes=VMEM_LIMIT),
        cost_estimate=pl.CostEstimate(flops=0, bytes_accessed=size, transcendentals=0),
    )(place.scalars, *operands)


def pick_columns(weights, layer, width, place):
    rows, columns = weights.shape[1:]
    count = columns // (2 * width)
    group = 2 if count % 2 == 0 else 1

    def kernel(scalars, *refs):
        out = refs[-1]
        for j in range(group):
            out[:, j * width : (j + 1) * width] = refs[j][0]

    def spec(j):
        return pl.BlockSpec(
            (1, rows, width), lambda i, s: (layer, 0, 2 * (group * i + j) + s[2])
        )

    return pl.pallas_call(
        kernel,
        grid_spec=pltpu.PrefetchScalarGridSpec(
            num_scalar_prefetch=1,
            grid=(count // group,),
            in_specs=[spec(j) for j in range(group)],
            out_specs=pl.BlockSpec((rows, group * width), lambda i, s: (0, i)),
        ),
        out_shape=jax.ShapeDtypeStruct((rows, count * width), weights.dtype),
        compiler_params=pltpu.CompilerParams(vmem_limit_bytes=VMEM_LIMIT),
        cost_estimate=pl.CostEstimate(
            flops=0, bytes_accessed=4 * rows * count * width, transcendentals=0
        ),
    )(place.scalars, *[weights] * group)


def pick_rows(arrays, layer, place):
    halves = [w.shape[1] // 2 for w in arrays]
    columns = arrays[0].shape[2]
    part = columns // 4 if columns % 512 == 0 else columns

    def kernel(scalars, *refs):
        start = 0
        for ref, half in zip(refs, halves, strict=False):
            refs[-1][start : start + half] = ref[0]
            start += half

    return pl.pallas_call(
        kernel,
        grid_spec=pltpu.PrefetchScalarGridSpec(
            num_scalar_prefetch=1,
            grid=(columns // part,),
            in_specs=[
                pl.BlockSpec((1, half, part), lambda i, s: (layer, s[2], i))
                for half in halves
            ],
            out_specs=pl.BlockSpec((sum(halves), part), lambda i, s: (0, i)),
        ),
        out_shape=jax.ShapeDtypeStruct((sum(halves), columns), arrays[0].dtype),
        compiler_params=pltpu.CompilerParams(vmem_limit_bytes=VMEM_LIMIT),
        cost_estimate=pl.CostEstimate(
            flops=0, bytes_accessed=4 * sum(halves) * columns, transcendentals=0
        ),
    )(place.scalars, *arrays)


def other_shards(table, place):
    span = place.span

    def body(scalars, ins, out):
        for k in range(1, span):
            source = lax.rem(scalars[0] + (span - k), span)
            for i in range(2):
                yield ins[0].at[source, i], out.at[i, k - 1]

    shape = jax.ShapeDtypeStruct((2, span - 1, *table.shape[2:]), table.dtype)
    return copy_call(body, shape, 2 * (span - 1), [table], place)


def flipped(q, flip):
    return lax.bitwise_xor(q, jnp.int32(flip))


def assemble(half, near, near_x, near_y, far_a, far_b, place):
    span = place.span
    eighth, columns = half.shape[0] // 8, half.shape[1]
    block = (eighth, columns)

    def kernel(scalars, half_ref, n_ref, x_ref, y_ref, a_ref, b_ref, out):
        z, q = scalars[0], scalars[1]
        own = pl.program_id(0) == z

        @pl.when(own)
        def _():
            out[0] = half_ref[...]

        @pl.when(jnp.logical_not(own))
        def _():
            for i in range(2):
                for flip, ref in enumerate((n_ref, x_ref, y_ref)):
                    out[0, flipped(q, flip), i] = ref[i, 0]
            out[0, flipped(q, 3), 0] = a_ref[0]
            out[0, flipped(q, 3), 1] = b_ref[0]

    def behind(j, s):
        return jnp.maximum(lax.rem(s[0] + span - j, span), 1) - 1

    near_spec = pl.BlockSpec((2, 1, *block), lambda j, s: (0, behind(j, s), 0, 0))
    far_spec = pl.BlockSpec((1, *block), lambda j, s: (behind(j, s), 0, 0))
    out = pl.pallas_call(
        kernel,
        grid_spec=pltpu.PrefetchScalarGridSpec(
            num_scalar_prefetch=1,
            grid=(span,),
            in_specs=[
                pl.BlockSpec((4, 2, *block), lambda j, s: (0, 0, 0, 0)),
                near_spec,
                near_spec,
                near_spec,
                far_spec,
                far_spec,
            ],
            out_specs=pl.BlockSpec((1, 4, 2, *block), lambda j, s: (j, 0, 0, 0, 0)),
        ),
        out_shape=jax.ShapeDtypeStruct((span, 4, 2, *block), half.dtype),
        compiler_params=pltpu.CompilerParams(vmem_limit_bytes=VMEM_LIMIT),
        cost_estimate=pl.CostEstimate(
            flops=0, bytes_accessed=32 * span * eighth * columns, transcendentals=0
        ),
    )(
        place.scalars,
        half.reshape(4, 2, *block),
        near,
        near_x,
        near_y,
        far_a,
        far_b,
    )
    return out.reshape(8 * span * eighth, columns)


def weight_gradient(left, right, place):
    span = place.span
    tokens, columns = left.shape[0], right.shape[1]
    rows = left.shape[1] // span
    eighth = rows // 8

    def kernel(scalars, left_ref, right_ref, own, pass_a, pass_b, send_a, send_b, table):
        q = scalars[1]
        product = lax.dot_general(
            left_ref[...],
            right_ref[...],
            (((0,), (0,)), ((), ())),
            preferred_element_type=F32,
        ).astype(BF16)
        for j in range(8):
            table[j // 2, j % 2] = product[j * eighth : (j + 1) * eighth]
        near_x, near_y, far = flipped(q, 1), flipped(q, 2), flipped(q, 3)
        own[0, 0], own[0, 1] = table[q, 0], table[q, 1]
        pass_a[0], pass_b[0] = table[near_y, 0], table[near_x, 1]
        send_a[0, 0], send_a[1, 0] = table[near_x, 0], table[far, 0]
        send_b[0, 0], send_b[1, 0] = table[near_y, 1], table[far, 1]

    block = (eighth, columns)
    one = pl.BlockSpec((1, *block), lambda k, s: (k, 0, 0))
    two = pl.BlockSpec((2, 1, *block), lambda k, s: (0, k, 0, 0))
    return pl.pallas_call(
        kernel,
        grid_spec=pltpu.PrefetchScalarGridSpec(
            num_scalar_prefetch=1,
            grid=(span,),
            in_specs=[
                pl.BlockSpec((tokens, rows), lambda k, s: (0, lax.rem(s[0] + k, span))),
                pl.BlockSpec((tokens, columns), lambda k, s: (0, 0)),
            ],
            out_specs=[
                pl.BlockSpec((1, 2, *block), lambda k, s: (k, 0, 0, 0)),
                one,
                one,
                two,
                two,
            ],
            scratch_shapes=[pltpu.VMEM((4, 2, *block), BF16)],
        ),
        out_shape=[
            jax.ShapeDtypeStruct((span, 2, *block), BF16),
            jax.ShapeDtypeStruct((span, *block), BF16),
            jax.ShapeDtypeStruct((span, *block), BF16),
            jax.ShapeDtypeStruct((2, span, *block), BF16),
            jax.ShapeDtypeStruct((2, span, *block), BF16),
        ],
        compiler_params=pltpu.CompilerParams(vmem_limit_bytes=VMEM_LIMIT),
        cost_estimate=pl.CostEstimate(
            flops=2 * tokens * span * rows * columns,
            bytes_accessed=2 * (tokens * (span * rows + columns) + span * rows * columns),
            transcendentals=0,
        ),
    )(place.scalars, left, right)


def combine(own, got_a, got_b, more_a, more_b):
    span, _, eighth, columns = own.shape
    part = columns // 4 if columns % 512 == 0 else columns

    def kernel(own_ref, ga_ref, gb_ref, ma_ref, mb_ref, *outs):
        for k in range(span):
            for i, (got, more) in enumerate(((ga_ref, ma_ref), (gb_ref, mb_ref))):
                total = own_ref[k, i].astype(F32) + got[0, k].astype(F32)
                outs[k][i] = (total + more[k].astype(F32)).astype(BF16)

    got = pl.BlockSpec((1, span, eighth, part), lambda j: (0, 0, 0, j))
    more = pl.BlockSpec((span, eighth, part), lambda j: (0, 0, j))
    out = pl.BlockSpec((2, eighth, part), lambda j: (0, 0, j))
    return pl.pallas_call(
        kernel,
        grid=(columns // part,),
        in_specs=[
            pl.BlockSpec((span, 2, eighth, part), lambda j: (0, 0, 0, j)),
            got,
            got,
            more,
            more,
        ],
        out_specs=[out] * span,
        out_shape=[jax.ShapeDtypeStruct((2, eighth, columns), BF16)] * span,
        compiler_params=pltpu.CompilerParams(vmem_limit_bytes=VMEM_LIMIT),
        cost_estimate=pl.CostEstimate(
            flops=4 * span * eighth * columns,
            bytes_accessed=16 * span * eighth * columns,
            transcendentals=0,
        ),
    )(own, got_a, got_b, more_a, more_b)


def finish_columns(parts, width, layer, previous):
    _, _, rows, columns = parts.shape

    def kernel(part_ref, *rest):
        out_ref = rest[-1]
        for core in range(2):
            for j in range(columns // width):
                start = (2 * j + core) * width
                out_ref[0, :, start : start + width] = part_ref[
                    0, core, :, j * width : (j + 1) * width
                ].astype(F32)

    operands, in_specs, aliases = (
        [parts],
        [pl.BlockSpec((1, 2, rows, columns), lambda q: (q, 0, 0, 0))],
        {},
    )
    if previous is not None:
        operands.append(previous)
        in_specs.append(pl.BlockSpec(memory_space=pl.ANY))
        aliases = {1: 0}
    return pl.pallas_call(
        kernel,
        grid=(4,),
        in_specs=in_specs,
        out_specs=pl.BlockSpec((1, rows, 2 * columns), lambda q: (layer, q, 0)),
        out_shape=jax.ShapeDtypeStruct((LAYERS, 4 * rows, 2 * columns), F32),
        input_output_aliases=aliases,
        compiler_params=pltpu.CompilerParams(vmem_limit_bytes=VMEM_LIMIT),
        cost_estimate=pl.CostEstimate(
            flops=0, bytes_accessed=48 * rows * columns, transcendentals=0
        ),
    )(*operands)


def finish_rows(parts, first_rows, layer, previous):
    _, _, quarter, columns = parts.shape
    sizes = (first_rows, 4 * quarter - first_rows)

    def kernel(part_ref, *rest):
        first, second = rest[-2:]
        for q in range(4):
            start, stop = q * quarter, (q + 1) * quarter
            cut = min(max(first_rows, start), stop)
            if cut > start:
                first[0, :, start:cut] = part_ref[q, :, : cut - start].astype(F32)
            if stop > cut:
                second[0, :, cut - first_rows : stop - first_rows] = part_ref[
                    q, :, cut - start :
                ].astype(F32)

    half = columns // 4 if columns % 512 == 0 else columns
    operands, aliases = [parts], {}
    in_specs = [pl.BlockSpec((4, 2, quarter, half), lambda j: (0, 0, 0, j))]
    if previous is not None:
        operands += list(previous)
        in_specs += [pl.BlockSpec(memory_space=pl.ANY)] * 2
        aliases = {1: 0, 2: 1}
    return pl.pallas_call(
        kernel,
        grid=(columns // half,),
        in_specs=in_specs,
        out_specs=[
            pl.BlockSpec((1, 2, size, half), lambda j: (layer, 0, 0, j)) for size in sizes
        ],
        out_shape=[
            jax.ShapeDtypeStruct((LAYERS, 2, size, columns), F32) for size in sizes
        ],
        input_output_aliases=aliases,
        compiler_params=pltpu.CompilerParams(vmem_limit_bytes=VMEM_LIMIT),
        cost_estimate=pl.CostEstimate(
            flops=0, bytes_accessed=48 * quarter * columns, transcendentals=0
        ),
    )(*operands)


def spread(blocks, place):
    span = place.span
    out = []
    for k in range(span):
        block = lax.dynamic_index_in_dim(
            blocks, lax.rem(place.z + k, span), 0, keepdims=False
        )
        out.append(block if k == 0 else spin(block, k, span))
    return out


def row_to_chip(x, place):
    rows, tokens, width = x.shape
    half = width // 2
    mine = lax.dynamic_slice_in_dim(x, place.c * half, half, 2)
    theirs = lax.dynamic_slice_in_dim(x, (1 - place.c) * half, half, 2)
    theirs = yield swap(theirs, "core")
    blocks = yield spread(by_core(place, mine, theirs, 0), place)
    own = from_relative(blocks, place).reshape(place.span * tokens, half)
    other = yield swap(own, "core")
    return by_core(place, own, other, 1)


def chip_to_rows(y, rows, place):
    span = place.span
    width = y.shape[1]
    tokens = y.shape[0] // span
    half = width // 2
    mine = lax.dynamic_slice_in_dim(y, place.c * half, half, 1)
    blocks = yield spread(mine.reshape(span, tokens, half), place)
    stacked = from_relative(blocks, place)
    own = lax.dynamic_slice_in_dim(stacked, place.c * rows, rows, 0)
    theirs = lax.dynamic_slice_in_dim(stacked, (1 - place.c) * rows, rows, 0)
    other = yield swap(theirs, "core")
    return by_core(place, own, other, 2)


class Slots:
    def __init__(self):
        self.parts = []

    def add(self, part, done):
        self.parts.append([part, next(part), done])

    def step(self, extra=()):
        pending, extra = lax.optimization_barrier(
            ([part[1] for part in self.parts], extra)
        )
        alive = []
        for part, arrived in zip(self.parts, pending, strict=True):
            try:
                part[1] = part[0].send(arrived)
                alive.append(part)
            except StopIteration as end:
                part[2](end.value)
        self.parts = alive
        return extra


def gather_weight(half, by_call, wait, place):
    span = place.span
    eighth, columns = half.shape[0] // 8, half.shape[1]
    mine = lax.dynamic_index_in_dim(
        half.reshape(4, 2, eighth, columns), place.q, 0, keepdims=False
    )
    if wait:
        mine = yield mine
    if by_call:
        every = yield lax.all_gather(mine, "shard")
        near = other_shards(every, place)
    else:
        arrived = yield [spin(mine, k, span) for k in range(1, span)]
        near = jnp.stack(arrived, 1)
    near_x, near_y = yield [swap(near, "xbit"), swap(near, "ybit")]
    far_a, far_b = yield [swap(near_x[0], "ybit"), swap(near_y[1], "xbit")]
    return assemble(half, near, near_x, near_y, far_a, far_b, place)


def reduce_weight(left, right, place):
    span = place.span
    own, pass_a, pass_b, send_a, send_b = yield weight_gradient(left, right, place)
    got_a, got_b = yield [swap(send_a, "xbit"), swap(send_b, "ybit")]
    onward_a = (pass_a.astype(F32) + got_a[1].astype(F32)).astype(BF16)
    onward_b = (pass_b.astype(F32) + got_b[1].astype(F32)).astype(BF16)
    more_a, more_b = yield [swap(onward_a, "ybit"), swap(onward_b, "xbit")]
    total = combine(own, got_a, got_b, more_a, more_b)
    arrived = yield [spin(total[k], k, span) for k in range(1, span)]
    summed = total[0].astype(F32)
    for other in arrived:
        summed = summed + other.astype(F32)
    summed = summed.astype(BF16)
    if lax.axis_size("outer") > 1:
        summed = lax.psum(summed, "outer")
    parts = yield lax.all_gather(summed, ("ybit", "xbit", "core"))
    _, eighth, columns = summed.shape
    return parts.reshape(4, 2, 2 * eighth, columns)


def gather_small(vectors, place):
    flat = jnp.concatenate([v.reshape(-1) for v in vectors])
    blocks = yield [flat] + [spin(flat, k, place.span) for k in range(1, place.span)]
    table = from_relative(blocks, place)
    out, start = [], 0
    for v in vectors:
        part = table[:, start : start + v.size].reshape(place.span, *v.shape)
        start += v.size
        part = jnp.moveaxis(part, 0, -2)
        out.append(part.reshape(*v.shape[:-1], -1).astype(F32))
    return out


def blocks_of(length, step):
    step = step if length % step == 0 else length
    return [(i * step, step) for i in range(length // step)]


def fill_bias(bias, seg_col, seg_row):
    @pl.when(pl.program_id(0) == 0)
    def _():
        row = lax.broadcasted_iota(jnp.int32, bias.shape, 0)
        col = lax.broadcasted_iota(jnp.int32, bias.shape, 1)
        mask = (col <= row) & (seg_col[...] == seg_row[...])
        bias[...] = jnp.where(mask, 0.0, -1e30)


def turn(u, tables):
    keep, upper, lower = tables
    half, lanes = ROT // 2, u.shape[1]
    return u * keep + pltpu.roll(u, lanes - half, 1) * upper + pltpu.roll(u, half, 1) * lower


def turn_back(d, tables):
    keep, upper, lower = tables
    half, lanes = ROT // 2, d.shape[1]
    return d * keep + pltpu.roll(d * upper, half, 1) + pltpu.roll(d * lower, lanes - half, 1)


def attend_kernel(scale, head, *refs):
    q_in, k_in, v_in, keep, upper, lower, seg_col, seg_row = refs[:8]
    q_ref, k_ref, v_ref, o_ref, lse_ref, bias = refs[8:]
    fill_bias(bias, seg_col, seg_row)
    tables = keep[...], upper[...], lower[...]
    q_ref[...] = turn(q_in[...], tables).astype(BF16)
    k_ref[...] = turn(k_in[...], tables).astype(BF16)
    v_ref[...] = v_in[...].astype(BF16)
    for start, step in blocks_of(q_ref.shape[0], FORWARD_ROWS):
        stop = start + step
        for h in range(q_ref.shape[1] // head):
            lanes = slice(h * head, (h + 1) * head)
            query = q_ref[start:stop, lanes] * scale
            scores = dot_t(query, k_ref[:stop, lanes]) + bias[start:stop, :stop]
            top = jnp.max(scores, -1, keepdims=True)
            expo = jnp.exp(scores - top)
            total = jnp.sum(expo, -1, keepdims=True)
            probs = (expo * (1.0 / total)).astype(BF16)
            o_ref[start:stop, lanes] = dot(probs, v_ref[:stop, lanes]).astype(BF16)
            lse_ref[h, start:stop, :] = top + jnp.log(total)


def attend_back_kernel(scale, head, *refs):
    q_ref, k_ref, v_ref, do_ref, lse_ref, keep, upper, lower, seg_col, seg_row = refs[:10]
    dq_out, dk_out, dv_out, dq_ref, dk_ref, dv_ref, bias = refs[10:]
    fill_bias(bias, seg_col, seg_row)
    over_rows = (((0,), (0,)), ((), ()))
    length = q_ref.shape[0]
    if len(blocks_of(length, BACKWARD_ROWS)) > 1:
        dk_ref[...] = jnp.zeros_like(dk_ref)
        dv_ref[...] = jnp.zeros_like(dv_ref)
    for start, step in blocks_of(length, BACKWARD_ROWS):
        stop = start + step
        for h in range(q_ref.shape[1] // head):
            lanes = slice(h * head, (h + 1) * head)
            query = q_ref[start:stop, lanes] * scale
            keys = k_ref[:stop, lanes]
            grad = do_ref[start:stop, lanes]
            scores = dot_t(query, keys) + bias[start:stop, :stop]
            probs = jnp.exp(scores - lse_ref[h, start:stop, :])
            d_probs = dot_t(grad, v_ref[:stop, lanes])
            delta = jnp.sum(probs * d_probs, -1, keepdims=True)
            d_scores = (probs * (d_probs - delta)).astype(BF16)
            dq_ref[start:stop, lanes] = dot(d_scores, keys) * scale
            d_key = lax.dot_general(d_scores, query, over_rows, preferred_element_type=F32)
            d_value = lax.dot_general(
                probs.astype(BF16), grad, over_rows, preferred_element_type=F32
            )
            if step == length:
                dk_ref[:, lanes], dv_ref[:, lanes] = d_key, d_value
            else:
                dk_ref[:stop, lanes] += d_key
                dv_ref[:stop, lanes] += d_value
    tables = keep[...], upper[...], lower[...]
    dq_out[...] = turn_back(dq_ref[...], tables).astype(BF16)
    dk_out[...] = turn_back(dk_ref[...], tables).astype(BF16)
    dv_out[...] = dv_ref[...].astype(BF16)


def attention_specs(length, width, head):
    group = max(head, 128)
    count = width // group
    wide = pl.BlockSpec((length, group), lambda i: (0, i))
    lse = pl.BlockSpec((group // head, length, 1), lambda i: (i, 0, 0))
    same = [pl.BlockSpec((length, group), lambda i: (0, 0))] * 3 + [
        pl.BlockSpec((length, 1), lambda i: (0, 0)),
        pl.BlockSpec((1, length), lambda i: (0, 0)),
    ]
    return group, count, wide, lse, same


def attend(projected, fixed, head):
    length, width = projected.shape[0], projected.shape[1] // 3
    group, count, wide, lse, same = attention_specs(length, width, head)

    def kernel(*refs):
        attend_kernel(1.0 / math.sqrt(head), head, *refs)

    low = jax.ShapeDtypeStruct((length, width), BF16)
    return pl.pallas_call(
        kernel,
        grid=(count,),
        in_specs=[
            wide,
            pl.BlockSpec((length, group), lambda i: (0, count + i)),
            pl.BlockSpec((length, group), lambda i: (0, 2 * count + i)),
            *same,
        ],
        out_specs=[wide, wide, wide, wide, lse],
        out_shape=[
            low,
            low,
            low,
            low,
            jax.ShapeDtypeStruct((width // head, length, 1), F32),
        ],
        scratch_shapes=[pltpu.VMEM((length, length), F32)],
        compiler_params=pltpu.CompilerParams(vmem_limit_bytes=VMEM_LIMIT),
        cost_estimate=pl.CostEstimate(
            flops=4 * length * length * width,
            bytes_accessed=20 * length * width,
            transcendentals=width // head * length * length,
        ),
    )(projected, projected, projected, *fixed)


def attend_back(query, keys, values, d_mixed, lse_all, fixed, head):
    length, width = query.shape
    group, count, wide, lse, same = attention_specs(length, width, head)

    def kernel(*refs):
        attend_back_kernel(1.0 / math.sqrt(head), head, *refs)

    out = jax.ShapeDtypeStruct((length, width), BF16)
    return pl.pallas_call(
        kernel,
        grid=(count,),
        in_specs=[wide, wide, wide, wide, lse, *same],
        out_specs=[wide, wide, wide],
        out_shape=[out, out, out],
        scratch_shapes=[pltpu.VMEM((length, group), F32)] * 3
        + [pltpu.VMEM((length, length), F32)],
        compiler_params=pltpu.CompilerParams(vmem_limit_bytes=VMEM_LIMIT),
        cost_estimate=pl.CostEstimate(
            flops=10 * length * length * width,
            bytes_accessed=20 * length * width,
            transcendentals=width // head * length * length,
        ),
    )(query, keys, values, d_mixed, lse_all, *fixed)


def rotary_tables(positions, head):
    half = ROT // 2
    inverse = jnp.power(10000.0, -2.0 * jnp.arange(half, dtype=F32) / ROT)
    angles = positions.astype(F32)[:, None] * inverse
    cos, sin = jnp.cos(angles), jnp.sin(angles)
    rest = jnp.zeros((positions.shape[0], head - ROT), F32)
    none = jnp.zeros_like(sin)
    keep = [cos, cos, rest + 1.0]
    upper = [-sin, none, rest]
    lower = [none, sin, rest]
    times = max(1, 128 // head)
    return [jnp.concatenate(t * times, 1) for t in (keep, upper, lower)]


def normalise(x):
    centred = x - jnp.mean(x, -1, keepdims=True)
    spread = jnp.mean(centred * centred, -1, keepdims=True)
    inverse = lax.rsqrt(spread + EPS)
    return centred * inverse, inverse


def interleave(first, second, span):
    a, b = first.shape[1] // span, second.shape[1] // span
    parts = []
    for k in range(span):
        parts += [first[:, k * a : (k + 1) * a], second[:, k * b : (k + 1) * b]]
    return jnp.concatenate(parts, 1)


def separate(both, a, b, span):
    parts = [both[:, k * (a + b) : (k + 1) * (a + b)] for k in range(span)]
    first = jnp.concatenate([p[:, :a] for p in parts], 1)
    return first, jnp.concatenate([p[:, a:] for p in parts], 1)


def forward_layer(x, weights, small, fixed, head, span):
    w_qkv, w_up, w_last = weights
    gains, shifts, b_qkv, b_out, b_up, b_down = small
    xhat, inverse = normalise(x)
    attn_low = (xhat * gains[0] + shifts[0]).astype(BF16)
    mlp_low = (xhat * gains[1] + shifts[1]).astype(BF16)
    projected = dot(attn_low, w_qkv) + b_qkv
    query, keys, values, mixed_low, lse = attend(projected, fixed, head)
    hidden_pre = dot(mlp_low, w_up) + b_up
    cdf = 0.5 * (1.0 + lax.erf(hidden_pre * ROOT_HALF))
    hidden_low = (hidden_pre * cdf).astype(BF16)
    last_low = interleave(mixed_low, hidden_low, span)
    part = dot(last_low, w_last).astype(BF16)
    other = swap(part, "core")
    y = x + (part.astype(F32) + other.astype(F32) + b_out + b_down)
    attention = (query, keys, values, lse)
    return y, (xhat, inverse, attn_low, mlp_low, attention, hidden_pre, last_low)


def backward_layer(dy, weights, small, saved, fixed, head, place, slots, done):
    w_qkv, w_up, w_last = weights
    gains = small[0]
    xhat, inverse, attn_low, mlp_low, attention, hidden_pre, last_low = saved
    query, keys, values, lse = attention
    span = place.span
    dy_low = dy.astype(BF16)
    slots.add(reduce_weight(last_low, dy_low, place), done(2))
    d_branch_b = jnp.sum(dy_low.astype(F32), 0)

    dy_low = slots.step(dy_low)
    d_mixed, d_hidden = separate(
        dot_t(dy_low, w_last), query.shape[1] // span, hidden_pre.shape[1] // span, span
    )
    d_mixed = d_mixed.astype(BF16)
    cdf = 0.5 * (1.0 + lax.erf(hidden_pre * ROOT_HALF))
    density = jnp.exp(-0.5 * hidden_pre * hidden_pre) * (1.0 / math.sqrt(2.0 * math.pi))
    d_pre = (d_hidden * (cdf + hidden_pre * density)).astype(BF16)
    slots.add(reduce_weight(mlp_low, d_pre, place), done(1))
    d_up_b = jnp.sum(d_pre.astype(F32), 0)

    d_mixed, d_pre = slots.step((d_mixed, d_pre))
    d_qkv = jnp.concatenate(
        attend_back(query, keys, values, d_mixed, lse, fixed, head), 1
    )
    slots.add(reduce_weight(attn_low, d_qkv, place), done(0))
    d_mlp = dot_t(d_pre, w_up)

    d_qkv, d_mlp = slots.step((d_qkv, d_mlp))
    d_qkv_b = jnp.sum(d_qkv.astype(F32), 0)
    d_attn = dot_t(d_qkv, w_qkv)
    part = (d_attn * gains[0] + d_mlp * gains[1]).astype(BF16)
    d_xhat = part.astype(F32) + swap(part, "core").astype(F32)
    dx = dy + inverse * (
        d_xhat
        - jnp.mean(d_xhat, -1, keepdims=True)
        - xhat * jnp.mean(d_xhat * xhat, -1, keepdims=True)
    )
    d_gains = jnp.stack([jnp.sum(d_attn * xhat, 0), jnp.sum(d_mlp * xhat, 0)])
    d_shifts = jnp.stack([jnp.sum(d_attn, 0), jnp.sum(d_mlp, 0)])
    return dx, (d_gains, d_shifts, d_qkv_b, d_branch_b, d_up_b)


def pick_vector(v, width, place):
    return jnp.take(v.reshape(*v.shape[:-1], -1, 2, width), place.c, axis=-2).reshape(
        *v.shape[:-1], -1
    )


def spread_vector(v, width, place):
    blocks = v.reshape(-1, 1, width)
    here = (jnp.arange(2) == place.c)[None, :, None]
    return jnp.where(here, blocks, 0.0).reshape(-1)


def reduce_small(layers, head_cols, ff_cols, place):
    span = place.span
    parts = []
    for d_gains, d_shifts, d_qkv_b, d_branch_b, d_up_b in layers:
        parts += [
            d_gains,
            d_shifts,
            spread_vector(d_qkv_b, head_cols, place),
            jnp.where(place.c == 0, d_branch_b, 0.0),
            spread_vector(d_up_b, ff_cols, place),
        ]
    tables = [p.reshape(-1, span, p.shape[-1] // span) for p in parts]
    flat = jnp.concatenate(
        [jnp.moveaxis(t, 1, 0).reshape(span, -1, 128) for t in tables], 1
    )
    for axis in ("core", "xbit", "ybit"):
        other = yield swap(flat, axis)
        flat = flat + other
    if lax.axis_size("outer") > 1:
        flat = lax.psum(flat, "outer")
    blocks = yield spread(flat, place)
    total = sum(blocks)
    total = total.reshape(-1)
    out, start = [], 0
    for p in parts:
        size = p.size // span
        out.append(total[start : start + size].reshape(*p.shape[:-1], p.shape[-1] // span))
        start += size
    count = len(parts) // len(layers)
    return [jnp.stack(out[i::count]) for i in range(count)]


def on_device(span, *arguments):
    (
        hidden_in,
        segments,
        norm_gains,
        norm_biases,
        qkv_weight,
        qkv_bias,
        out_weight,
        out_bias,
        up_weight,
        up_bias,
        down_weight,
        down_bias,
        out_grad,
    ) = arguments
    place = Place(span)
    rows = hidden_in.shape[0]
    width = hidden_in.shape[2]
    head = width // H
    head_cols = width // (2 * span)
    ff_cols = up_weight.shape[2] // (2 * span)
    assert 2 * rows == span

    halves = []
    for layer in range(LAYERS):
        halves += [
            pick_columns(qkv_weight, layer, head_cols, place),
            pick_columns(up_weight, layer, ff_cols, place),
            pick_rows((out_weight, down_weight), layer, place),
        ]
    found = {}

    def keep(name):
        def done(value):
            found[name] = value

        return done

    slots = Slots()
    slots.add(gather_weight(halves[0], False, False, place), keep(0))
    both = jnp.concatenate([hidden_in, out_grad], 2)
    slots.add(row_to_chip(both, place), keep("rows"))
    vectors = [norm_gains, norm_biases, qkv_bias, out_bias, up_bias, down_bias]
    slots.add(gather_small(vectors, place), keep("vectors"))
    seg_other = swap(segments, "core")
    for index in range(1, len(halves)):
        slots.add(gather_weight(halves[index], index % 3 != 0, True, place), keep(index))
        slots.step()
    while slots.parts:
        slots.step()
    weights = [[found[3 * layer + i] for i in range(3)] for layer in range(LAYERS)]

    both = found["rows"]
    stream, dy = both[:, :width].astype(F32), both[:, width:].astype(F32)
    seg_all = by_core(place, segments, seg_other, 0)
    seg = lax.dynamic_index_in_dim(seg_all, place.z, 0, keepdims=False)
    seg_col, seg_row = seg[:, None], seg[None, :]
    length = seg.shape[0]
    earlier = jnp.sum((seg_row < seg_col).astype(jnp.int32), -1)
    positions = jnp.arange(length, dtype=jnp.int32) - earlier
    fixed = (*rotary_tables(positions, head), seg_col, seg_row)

    gains, shifts, b_qkv, b_out, b_up, b_down = found["vectors"]
    b_qkv = pick_vector(b_qkv, head_cols, place)
    b_up = pick_vector(b_up, ff_cols, place)
    smalls = [
        (gains[i], shifts[i], b_qkv[i], b_out[i], b_up[i], b_down[i]) for i in range(LAYERS)
    ]

    kept = []
    for layer in range(LAYERS):
        stream, saved = forward_layer(
            stream, weights[layer], smalls[layer], fixed, head, span
        )
        kept.append(saved)

    big = [None] * 3
    little = [None] * LAYERS
    slots = Slots()

    def done_for(layer):
        def of(index):
            def done(parts):
                if index == 2:
                    first_rows = out_weight.shape[1] // 2
                    big[2] = finish_rows(parts, first_rows, layer, big[2])
                else:
                    by = (head_cols, ff_cols)[index]
                    big[index] = finish_columns(parts, by, layer, big[index])

            return done

        return of

    for layer in reversed(range(LAYERS)):
        dy, little[layer] = backward_layer(
            dy,
            weights[layer],
            smalls[layer],
            kept[layer],
            fixed,
            head,
            place,
            slots,
            done_for(layer),
        )
    results = jnp.concatenate([stream.astype(BF16), dy.astype(BF16)], 1)
    slots.add(chip_to_rows(results, rows, place), keep("results"))
    slots.add(reduce_small(little, head_cols, ff_cols, place), keep("sums"))
    while slots.parts:
        slots.step()
    results = found["results"]
    block_out, in_grad = results[..., :width], results[..., width:].astype(F32)
    d_gains, d_shifts, d_qkv_b, d_branch_b, d_up_b = found["sums"]
    d_qkv_w, d_up_w, (d_out_w, d_down_w) = big
    d_out_w = d_out_w.reshape(LAYERS, -1, width)
    d_down_w = d_down_w.reshape(LAYERS, -1, width)
    return (
        block_out,
        in_grad,
        d_gains,
        d_shifts,
        d_qkv_w,
        d_qkv_b,
        d_out_w,
        d_branch_b,
        d_up_w,
        d_up_b,
        d_down_w,
        d_branch_b,
    )


def solution(mesh):
    rep, span = mesh.shape["rep"], mesh.shape["shard"]
    fine = Mesh(mesh.devices.reshape(rep // 8, 2, 2, 2, span), (*AXES, "shard"))
    tokens = P(AXES, "shard", None)
    last = P(None, None, "shard")
    middle = P(None, "shard", None)
    vector = P(None, "shard")
    in_specs = (
        tokens,
        P(AXES, None),
        last,
        last,
        middle,
        vector,
        middle,
        vector,
        middle,
        vector,
        middle,
        vector,
        tokens,
    )
    out_specs = (
        tokens,
        tokens,
        last,
        last,
        middle,
        vector,
        middle,
        vector,
        middle,
        vector,
        middle,
        vector,
    )

    def step(*arguments):
        return on_device(span, *arguments)

    return jax.shard_map(
        step, mesh=fine, in_specs=in_specs, out_specs=out_specs, check_vma=False
    )
```

```python
import math

import jax
import jax.numpy as jnp
from jax import lax
from jax.experimental import pallas as pl
from jax.experimental.pallas import tpu as pltpu
from jax.sharding import Mesh
from jax.sharding import PartitionSpec as P

H = 16
ROT = 16
LAYERS = 2
EPS = 1e-05
ROOT_HALF = math.sqrt(0.5)
F32 = jnp.float32
BF16 = jnp.bfloat16
AXES = ("outer", "ybit", "xbit", "core")
VMEM_LIMIT = 48 * 1024 * 1024
FORWARD_ROWS = 256
BACKWARD_ROWS = 512
LIGHT = pl.CostEstimate(flops=1024, bytes_accessed=1024, transcendentals=0)


def swap(x, axis):
    return lax.ppermute(x, axis, [(0, 1), (1, 0)])


def spin(x, k, span):
    return lax.ppermute(x, "shard", [(j, (j + k) % span) for j in range(span)])


def dot(a, b):
    return jnp.dot(a, b, preferred_element_type=F32)


def dot_t(a, b):
    return lax.dot_general(a, b, (((1,), (1,)), ((), ())), preferred_element_type=F32)


class Place:
    def __init__(self, span):
        self.span = span
        self.z = lax.axis_index("shard")
        self.c = lax.axis_index("core")
        self.bx = lax.axis_index("xbit")
        self.by = lax.axis_index("ybit")
        self.q = 2 * self.by + self.bx
        self.scalars = jnp.stack([self.z, self.q, self.c]).astype(jnp.int32)


def from_relative(blocks, place):
    span = place.span
    order = [blocks[(-m) % span] for m in range(2 * span - 1)]
    return lax.dynamic_slice_in_dim(
        jnp.stack(order), lax.rem(span - place.z, span), span, 0
    )


def by_core(place, own, other, axis):
    return jnp.where(
        place.c == 0,
        jnp.concatenate([own, other], axis),
        jnp.concatenate([other, own], axis),
    )


def copy_call(body, out_shape, copies, operands, place):
    def kernel(scalars, *refs):
        ins, out, sems = refs[: len(operands)], refs[len(operands)], refs[-1]
        started = []
        for slot, (src, dst) in enumerate(body(scalars, ins, out)):
            copy = pltpu.make_async_copy(src, dst, sems.at[slot])
            copy.start()
            started.append(copy)
        for copy in started:
            copy.wait()

    return pl.pallas_call(
        kernel,
        out_shape=out_shape,
        in_specs=[pl.BlockSpec(memory_space=pltpu.SMEM)]
        + [pl.BlockSpec(memory_space=pl.ANY)] * len(operands),
        out_specs=pl.BlockSpec(memory_space=pltpu.VMEM),
        scratch_shapes=[pltpu.SemaphoreType.DMA((copies,))],
        compiler_params=pltpu.CompilerParams(vmem_limit_bytes=VMEM_LIMIT),
        cost_estimate=LIGHT,
    )(place.scalars, *operands)


def pick_columns(weights, layer, width, place):
    rows, columns = weights.shape[1:]
    count = columns // (2 * width)
    group = 2 if count % 2 == 0 else 1

    def kernel(scalars, *refs):
        out = refs[-1]
        for j in range(group):
            out[:, j * width : (j + 1) * width] = refs[j][0]

    def spec(j):
        return pl.BlockSpec(
            (1, rows, width), lambda i, s: (layer, 0, 2 * (group * i + j) + s[2])
        )

    return pl.pallas_call(
        kernel,
        grid_spec=pltpu.PrefetchScalarGridSpec(
            num_scalar_prefetch=1,
            grid=(count // group,),
            in_specs=[spec(j) for j in range(group)],
            out_specs=pl.BlockSpec((rows, group * width), lambda i, s: (0, i)),
        ),
        out_shape=jax.ShapeDtypeStruct((rows, count * width), weights.dtype),
        compiler_params=pltpu.CompilerParams(vmem_limit_bytes=VMEM_LIMIT),
        cost_estimate=LIGHT,
    )(place.scalars, *[weights] * group)


def pick_rows(arrays, layer, place):
    halves = [w.shape[1] // 2 for w in arrays]
    columns = arrays[0].shape[2]
    part = columns // 4 if columns % 512 == 0 else columns

    def kernel(scalars, *refs):
        start = 0
        for ref, half in zip(refs, halves, strict=False):
            refs[-1][start : start + half] = ref[0]
            start += half

    return pl.pallas_call(
        kernel,
        grid_spec=pltpu.PrefetchScalarGridSpec(
            num_scalar_prefetch=1,
            grid=(columns // part,),
            in_specs=[
                pl.BlockSpec((1, half, part), lambda i, s: (layer, s[2], i))
                for half in halves
            ],
            out_specs=pl.BlockSpec((sum(halves), part), lambda i, s: (0, i)),
        ),
        out_shape=jax.ShapeDtypeStruct((sum(halves), columns), arrays[0].dtype),
        compiler_params=pltpu.CompilerParams(vmem_limit_bytes=VMEM_LIMIT),
        cost_estimate=LIGHT,
    )(place.scalars, *arrays)


def other_shards(table, place):
    span = place.span

    def body(scalars, ins, out):
        for k in range(1, span):
            source = lax.rem(scalars[0] + (span - k), span)
            for i in range(2):
                yield ins[0].at[source, i], out.at[i, k - 1]

    shape = jax.ShapeDtypeStruct((2, span - 1, *table.shape[2:]), table.dtype)
    return copy_call(body, shape, 2 * (span - 1), [table], place)


def flipped(q, flip):
    return lax.bitwise_xor(q, jnp.int32(flip))


def assemble(half, near, near_x, near_y, far_a, far_b, place):
    span = place.span
    eighth, columns = half.shape[0] // 8, half.shape[1]
    block = (eighth, columns)

    def kernel(scalars, half_ref, n_ref, x_ref, y_ref, a_ref, b_ref, out):
        z, q = scalars[0], scalars[1]
        own = pl.program_id(0) == z

        @pl.when(own)
        def _():
            out[0] = half_ref[...]

        @pl.when(jnp.logical_not(own))
        def _():
            for i in range(2):
                for flip, ref in enumerate((n_ref, x_ref, y_ref)):
                    out[0, flipped(q, flip), i] = ref[i, 0]
            out[0, flipped(q, 3), 0] = a_ref[0]
            out[0, flipped(q, 3), 1] = b_ref[0]

    def behind(j, s):
        return jnp.maximum(lax.rem(s[0] + span - j, span), 1) - 1

    near_spec = pl.BlockSpec((2, 1, *block), lambda j, s: (0, behind(j, s), 0, 0))
    far_spec = pl.BlockSpec((1, *block), lambda j, s: (behind(j, s), 0, 0))
    out = pl.pallas_call(
        kernel,
        grid_spec=pltpu.PrefetchScalarGridSpec(
            num_scalar_prefetch=1,
            grid=(span,),
            in_specs=[
                pl.BlockSpec((4, 2, *block), lambda j, s: (0, 0, 0, 0)),
                near_spec,
                near_spec,
                near_spec,
                far_spec,
                far_spec,
            ],
            out_specs=pl.BlockSpec((1, 4, 2, *block), lambda j, s: (j, 0, 0, 0, 0)),
        ),
        out_shape=jax.ShapeDtypeStruct((span, 4, 2, *block), half.dtype),
        compiler_params=pltpu.CompilerParams(vmem_limit_bytes=VMEM_LIMIT),
        cost_estimate=LIGHT,
    )(
        place.scalars,
        half.reshape(4, 2, *block),
        near,
        near_x,
        near_y,
        far_a,
        far_b,
    )
    return out.reshape(8 * span * eighth, columns)


def absolute_quarters(summed, near_x, near_y, far_a, far_b, place):
    def body(scalars, ins, out):
        q = scalars[1]
        for flip in range(3):
            yield ins[flip], out.at[flipped(q, flip)]
        for i in range(2):
            yield ins[3 + i], out.at[flipped(q, 3), i]

    shape = jax.ShapeDtypeStruct((4, *summed.shape), summed.dtype)
    return copy_call(body, shape, 5, [summed, near_x, near_y, far_a, far_b], place)


def weight_gradient(left, right, place):
    span = place.span
    tokens, columns = left.shape[0], right.shape[1]
    rows = left.shape[1] // span
    eighth = rows // 8

    def kernel(scalars, left_ref, right_ref, own, pass_a, pass_b, send_a, send_b, table):
        q = scalars[1]
        product = lax.dot_general(
            left_ref[...],
            right_ref[...],
            (((0,), (0,)), ((), ())),
            preferred_element_type=F32,
        ).astype(BF16)
        for j in range(8):
            table[j // 2, j % 2] = product[j * eighth : (j + 1) * eighth]
        near_x, near_y, far = flipped(q, 1), flipped(q, 2), flipped(q, 3)
        own[0, 0], own[0, 1] = table[q, 0], table[q, 1]
        pass_a[0], pass_b[0] = table[near_y, 0], table[near_x, 1]
        send_a[0, 0], send_a[1, 0] = table[near_x, 0], table[far, 0]
        send_b[0, 0], send_b[1, 0] = table[near_y, 1], table[far, 1]

    block = (eighth, columns)
    one = pl.BlockSpec((1, *block), lambda k, s: (k, 0, 0))
    two = pl.BlockSpec((2, 1, *block), lambda k, s: (0, k, 0, 0))
    return pl.pallas_call(
        kernel,
        grid_spec=pltpu.PrefetchScalarGridSpec(
            num_scalar_prefetch=1,
            grid=(span,),
            in_specs=[
                pl.BlockSpec((tokens, rows), lambda k, s: (0, lax.rem(s[0] + k, span))),
                pl.BlockSpec((tokens, columns), lambda k, s: (0, 0)),
            ],
            out_specs=[
                pl.BlockSpec((1, 2, *block), lambda k, s: (k, 0, 0, 0)),
                one,
                one,
                two,
                two,
            ],
            scratch_shapes=[pltpu.VMEM((4, 2, *block), BF16)],
        ),
        out_shape=[
            jax.ShapeDtypeStruct((span, 2, *block), BF16),
            jax.ShapeDtypeStruct((span, *block), BF16),
            jax.ShapeDtypeStruct((span, *block), BF16),
            jax.ShapeDtypeStruct((2, span, *block), BF16),
            jax.ShapeDtypeStruct((2, span, *block), BF16),
        ],
        compiler_params=pltpu.CompilerParams(vmem_limit_bytes=VMEM_LIMIT),
        cost_estimate=pl.CostEstimate(
            flops=2 * tokens * span * rows * columns,
            bytes_accessed=2 * (tokens * (span * rows + columns) + span * rows * columns),
            transcendentals=0,
        ),
    )(place.scalars, left, right)


def combine(own, got_a, got_b, more_a, more_b):
    span, _, eighth, columns = own.shape
    part = columns // 4 if columns % 512 == 0 else columns

    def kernel(own_ref, ga_ref, gb_ref, ma_ref, mb_ref, *outs):
        for k in range(span):
            for i, (got, more) in enumerate(((ga_ref, ma_ref), (gb_ref, mb_ref))):
                total = own_ref[k, i].astype(F32) + got[0, k].astype(F32)
                outs[k][i] = (total + more[k].astype(F32)).astype(BF16)

    got = pl.BlockSpec((1, span, eighth, part), lambda j: (0, 0, 0, j))
    more = pl.BlockSpec((span, eighth, part), lambda j: (0, 0, j))
    out = pl.BlockSpec((2, eighth, part), lambda j: (0, 0, j))
    return pl.pallas_call(
        kernel,
        grid=(columns // part,),
        in_specs=[
            pl.BlockSpec((span, 2, eighth, part), lambda j: (0, 0, 0, j)),
            got,
            got,
            more,
            more,
        ],
        out_specs=[out] * span,
        out_shape=[jax.ShapeDtypeStruct((2, eighth, columns), BF16)] * span,
        compiler_params=pltpu.CompilerParams(vmem_limit_bytes=VMEM_LIMIT),
        cost_estimate=LIGHT,
    )(own, got_a, got_b, more_a, more_b)


def finish_columns(parts, width, layer, previous):
    _, _, rows, columns = parts.shape

    def kernel(part_ref, *rest):
        out_ref = rest[-1]
        for core in range(2):
            for j in range(columns // width):
                start = (2 * j + core) * width
                out_ref[0, :, start : start + width] = part_ref[
                    0, core, :, j * width : (j + 1) * width
                ].astype(F32)

    operands, in_specs, aliases = (
        [parts],
        [pl.BlockSpec((1, 2, rows, columns), lambda q: (q, 0, 0, 0))],
        {},
    )
    if previous is not None:
        operands.append(previous)
        in_specs.append(pl.BlockSpec(memory_space=pl.ANY))
        aliases = {1: 0}
    return pl.pallas_call(
        kernel,
        grid=(4,),
        in_specs=in_specs,
        out_specs=pl.BlockSpec((1, rows, 2 * columns), lambda q: (layer, q, 0)),
        out_shape=jax.ShapeDtypeStruct((LAYERS, 4 * rows, 2 * columns), F32),
        input_output_aliases=aliases,
        compiler_params=pltpu.CompilerParams(vmem_limit_bytes=VMEM_LIMIT),
        cost_estimate=LIGHT,
    )(*operands)


def finish_rows(parts, first_rows, layer, previous):
    _, _, quarter, columns = parts.shape
    sizes = (first_rows, 4 * quarter - first_rows)

    def kernel(part_ref, *rest):
        first, second = rest[-2:]
        for q in range(4):
            start, stop = q * quarter, (q + 1) * quarter
            cut = min(max(first_rows, start), stop)
            if cut > start:
                first[0, :, start:cut] = part_ref[q, :, : cut - start].astype(F32)
            if stop > cut:
                second[0, :, cut - first_rows : stop - first_rows] = part_ref[
                    q, :, cut - start :
                ].astype(F32)

    half = columns // 4 if columns % 512 == 0 else columns
    operands, aliases = [parts], {}
    in_specs = [pl.BlockSpec((4, 2, quarter, half), lambda j: (0, 0, 0, j))]
    if previous is not None:
        operands += list(previous)
        in_specs += [pl.BlockSpec(memory_space=pl.ANY)] * 2
        aliases = {1: 0, 2: 1}
    return pl.pallas_call(
        kernel,
        grid=(columns // half,),
        in_specs=in_specs,
        out_specs=[
            pl.BlockSpec((1, 2, size, half), lambda j: (layer, 0, 0, j)) for size in sizes
        ],
        out_shape=[
            jax.ShapeDtypeStruct((LAYERS, 2, size, columns), F32) for size in sizes
        ],
        input_output_aliases=aliases,
        compiler_params=pltpu.CompilerParams(vmem_limit_bytes=VMEM_LIMIT),
        cost_estimate=LIGHT,
    )(*operands)


def spread(blocks, place):
    span = place.span
    out = []
    for k in range(span):
        block = lax.dynamic_index_in_dim(
            blocks, lax.rem(place.z + k, span), 0, keepdims=False
        )
        out.append(block if k == 0 else spin(block, k, span))
    return out


def swap_once(x):
    other = yield swap(x, "core")
    return other


def row_to_chip(x, place):
    rows, tokens, width = x.shape
    half = width // 2
    mine = lax.dynamic_slice_in_dim(x, place.c * half, half, 2)
    theirs = lax.dynamic_slice_in_dim(x, (1 - place.c) * half, half, 2)
    theirs = yield swap(theirs, "core")
    blocks = yield spread(by_core(place, mine, theirs, 0), place)
    own = from_relative(blocks, place).reshape(place.span * tokens, half)
    other = yield swap(own, "core")
    return by_core(place, own, other, 1)


def chip_to_rows(y, rows, place):
    span = place.span
    width = y.shape[1]
    tokens = y.shape[0] // span
    half = width // 2
    mine = lax.dynamic_slice_in_dim(y, place.c * half, half, 1)
    blocks = yield spread(mine.reshape(span, tokens, half), place)
    stacked = from_relative(blocks, place)
    own = lax.dynamic_slice_in_dim(stacked, place.c * rows, rows, 0)
    theirs = lax.dynamic_slice_in_dim(stacked, (1 - place.c) * rows, rows, 0)
    other = yield swap(theirs, "core")
    return by_core(place, own, other, 2)


class Slots:
    def __init__(self):
        self.parts = []

    def add(self, part, done):
        self.parts.append([part, next(part), done])

    def step(self, extra=()):
        pending, extra = lax.optimization_barrier(
            ([part[1] for part in self.parts], extra)
        )
        alive = []
        for part, arrived in zip(self.parts, pending, strict=True):
            try:
                part[1] = part[0].send(arrived)
                alive.append(part)
            except StopIteration as end:
                part[2](end.value)
        self.parts = alive
        return extra


def gather_weight(half, by_call, wait, place):
    span = place.span
    eighth, columns = half.shape[0] // 8, half.shape[1]
    mine = lax.dynamic_index_in_dim(
        half.reshape(4, 2, eighth, columns), place.q, 0, keepdims=False
    )
    if by_call:
        moving = lax.all_gather(mine, "shard")
    else:
        moving = [spin(mine, k, span) for k in range(1, span)]
    if wait:
        yield ()
    arrived = yield moving
    near = other_shards(arrived, place) if by_call else jnp.stack(arrived, 1)
    near_x, near_y = yield [swap(near, "xbit"), swap(near, "ybit")]
    far_a, far_b = yield [swap(near_x[0], "ybit"), swap(near_y[1], "xbit")]
    return assemble(half, near, near_x, near_y, far_a, far_b, place)


def reduce_weight(left, right, place, last=False):
    span = place.span
    own, pass_a, pass_b, send_a, send_b = yield weight_gradient(left, right, place)
    got_a, got_b = yield [swap(send_a, "xbit"), swap(send_b, "ybit")]
    onward_a = (pass_a.astype(F32) + got_a[1].astype(F32)).astype(BF16)
    onward_b = (pass_b.astype(F32) + got_b[1].astype(F32)).astype(BF16)
    more_a, more_b = yield [swap(onward_a, "ybit"), swap(onward_b, "xbit")]
    total = combine(own, got_a, got_b, more_a, more_b)
    arrived = yield [spin(total[k], k, span) for k in range(1, span)]
    summed = total[0].astype(F32)
    for other in arrived:
        summed = summed + other.astype(F32)
    summed = summed.astype(BF16)
    if lax.axis_size("outer") > 1:
        summed = lax.psum(summed, "outer")
    _, eighth, columns = summed.shape
    if last:
        near_x, near_y = yield [swap(summed, "xbit"), swap(summed, "ybit")]
        far_a, far_b = yield [swap(near_x[0], "ybit"), swap(near_y[1], "xbit")]
        half = absolute_quarters(summed, near_x, near_y, far_a, far_b, place)
        other = yield swap(half, "core")
        parts = by_core(place, half[:, None], other[:, None], 1)
    else:
        parts = yield lax.all_gather(summed, ("ybit", "xbit", "core"))
    return parts.reshape(4, 2, 2 * eighth, columns)


def gather_small(vectors, place):
    flat = jnp.concatenate([v.reshape(-1) for v in vectors])
    blocks = yield [flat] + [spin(flat, k, place.span) for k in range(1, place.span)]
    table = from_relative(blocks, place)
    out, start = [], 0
    for v in vectors:
        part = table[:, start : start + v.size].reshape(place.span, *v.shape)
        start += v.size
        part = jnp.moveaxis(part, 0, -2)
        out.append(part.reshape(*v.shape[:-1], -1).astype(F32))
    return out


def blocks_of(length, step):
    step = step if length % step == 0 else length
    return [(i * step, step) for i in range(length // step)]


def fill_bias(bias, seg_col, seg_row):
    @pl.when(pl.program_id(0) == 0)
    def _():
        row = lax.broadcasted_iota(jnp.int32, bias.shape, 0)
        col = lax.broadcasted_iota(jnp.int32, bias.shape, 1)
        mask = (col <= row) & (seg_col[...] == seg_row[...])
        bias[...] = jnp.where(mask, 0.0, -1e30)


def turn(u, tables):
    keep, upper, lower = tables
    half, lanes = ROT // 2, u.shape[1]
    return u * keep + pltpu.roll(u, lanes - half, 1) * upper + pltpu.roll(u, half, 1) * lower


def turn_back(d, tables):
    keep, upper, lower = tables
    half, lanes = ROT // 2, d.shape[1]
    return d * keep + pltpu.roll(d * upper, half, 1) + pltpu.roll(d * lower, lanes - half, 1)


def attend_kernel(scale, head, *refs):
    q_in, k_in, v_in, keep, upper, lower, seg_col, seg_row = refs[:8]
    q_ref, k_ref, v_ref, o_ref, lse_ref, bias = refs[8:]
    fill_bias(bias, seg_col, seg_row)
    tables = keep[...], upper[...], lower[...]
    q_ref[...] = turn(q_in[...], tables).astype(BF16)
    k_ref[...] = turn(k_in[...], tables).astype(BF16)
    v_ref[...] = v_in[...].astype(BF16)
    for start, step in blocks_of(q_ref.shape[0], FORWARD_ROWS):
        stop = start + step
        for h in range(q_ref.shape[1] // head):
            lanes = slice(h * head, (h + 1) * head)
            query = q_ref[start:stop, lanes] * scale
            scores = dot_t(query, k_ref[:stop, lanes]) + bias[start:stop, :stop]
            top = jnp.max(scores, -1, keepdims=True)
            expo = jnp.exp(scores - top)
            total = jnp.sum(expo, -1, keepdims=True)
            probs = (expo * (1.0 / total)).astype(BF16)
            o_ref[start:stop, lanes] = dot(probs, v_ref[:stop, lanes]).astype(BF16)
            lse_ref[h, start:stop, :] = top + jnp.log(total)


def attend_back_kernel(scale, head, *refs):
    q_ref, k_ref, v_ref, do_ref, lse_ref, keep, upper, lower, seg_col, seg_row = refs[:10]
    dq_out, dk_out, dv_out, dq_ref, dk_ref, dv_ref, bias = refs[10:]
    fill_bias(bias, seg_col, seg_row)
    over_rows = (((0,), (0,)), ((), ()))
    length = q_ref.shape[0]
    if len(blocks_of(length, BACKWARD_ROWS)) > 1:
        dk_ref[...] = jnp.zeros_like(dk_ref)
        dv_ref[...] = jnp.zeros_like(dv_ref)
    for start, step in blocks_of(length, BACKWARD_ROWS):
        stop = start + step
        for h in range(q_ref.shape[1] // head):
            lanes = slice(h * head, (h + 1) * head)
            query = q_ref[start:stop, lanes] * scale
            keys = k_ref[:stop, lanes]
            grad = do_ref[start:stop, lanes]
            scores = dot_t(query, keys) + bias[start:stop, :stop]
            probs = jnp.exp(scores - lse_ref[h, start:stop, :])
            d_probs = dot_t(grad, v_ref[:stop, lanes])
            delta = jnp.sum(probs * d_probs, -1, keepdims=True)
            d_scores = (probs * (d_probs - delta)).astype(BF16)
            dq_ref[start:stop, lanes] = dot(d_scores, keys) * scale
            d_key = lax.dot_general(d_scores, query, over_rows, preferred_element_type=F32)
            d_value = lax.dot_general(
                probs.astype(BF16), grad, over_rows, preferred_element_type=F32
            )
            if step == length:
                dk_ref[:, lanes], dv_ref[:, lanes] = d_key, d_value
            else:
                dk_ref[:stop, lanes] += d_key
                dv_ref[:stop, lanes] += d_value
    tables = keep[...], upper[...], lower[...]
    dq_out[...] = turn_back(dq_ref[...], tables).astype(BF16)
    dk_out[...] = turn_back(dk_ref[...], tables).astype(BF16)
    dv_out[...] = dv_ref[...].astype(BF16)


def attention_specs(length, width, head):
    group = max(head, 128)
    count = width // group
    wide = pl.BlockSpec((length, group), lambda i: (0, i))
    lse = pl.BlockSpec((group // head, length, 1), lambda i: (i, 0, 0))
    same = [pl.BlockSpec((length, group), lambda i: (0, 0))] * 3 + [
        pl.BlockSpec((length, 1), lambda i: (0, 0)),
        pl.BlockSpec((1, length), lambda i: (0, 0)),
    ]
    return group, count, wide, lse, same


def attend(projected, fixed, head):
    length, width = projected.shape[0], projected.shape[1] // 3
    group, count, wide, lse, same = attention_specs(length, width, head)

    def kernel(*refs):
        attend_kernel(1.0 / math.sqrt(head), head, *refs)

    low = jax.ShapeDtypeStruct((length, width), BF16)
    return pl.pallas_call(
        kernel,
        grid=(count,),
        in_specs=[
            wide,
            pl.BlockSpec((length, group), lambda i: (0, count + i)),
            pl.BlockSpec((length, group), lambda i: (0, 2 * count + i)),
            *same,
        ],
        out_specs=[wide, wide, wide, wide, lse],
        out_shape=[
            low,
            low,
            low,
            low,
            jax.ShapeDtypeStruct((width // head, length, 1), F32),
        ],
        scratch_shapes=[pltpu.VMEM((length, length), F32)],
        compiler_params=pltpu.CompilerParams(vmem_limit_bytes=VMEM_LIMIT),
        cost_estimate=LIGHT,
    )(projected, projected, projected, *fixed)


def attend_back(query, keys, values, d_mixed, lse_all, fixed, head):
    length, width = query.shape
    group, count, wide, lse, same = attention_specs(length, width, head)

    def kernel(*refs):
        attend_back_kernel(1.0 / math.sqrt(head), head, *refs)

    out = jax.ShapeDtypeStruct((length, width), BF16)
    return pl.pallas_call(
        kernel,
        grid=(count,),
        in_specs=[wide, wide, wide, wide, lse, *same],
        out_specs=[wide, wide, wide],
        out_shape=[out, out, out],
        scratch_shapes=[pltpu.VMEM((length, group), F32)] * 3
        + [pltpu.VMEM((length, length), F32)],
        compiler_params=pltpu.CompilerParams(vmem_limit_bytes=VMEM_LIMIT),
        cost_estimate=LIGHT,
    )(query, keys, values, d_mixed, lse_all, *fixed)


def rotary_tables(positions, head):
    half = ROT // 2
    inverse = jnp.power(10000.0, -2.0 * jnp.arange(half, dtype=F32) / ROT)
    angles = positions.astype(F32)[:, None] * inverse
    cos, sin = jnp.cos(angles), jnp.sin(angles)
    rest = jnp.zeros((positions.shape[0], head - ROT), F32)
    none = jnp.zeros_like(sin)
    keep = [cos, cos, rest + 1.0]
    upper = [-sin, none, rest]
    lower = [none, sin, rest]
    times = max(1, 128 // head)
    return [jnp.concatenate(t * times, 1) for t in (keep, upper, lower)]


def normalise(x):
    centred = x - jnp.mean(x, -1, keepdims=True)
    spread = jnp.mean(centred * centred, -1, keepdims=True)
    inverse = lax.rsqrt(spread + EPS)
    return centred * inverse, inverse


def interleave(first, second, span):
    a, b = first.shape[1] // span, second.shape[1] // span
    parts = []
    for k in range(span):
        parts += [first[:, k * a : (k + 1) * a], second[:, k * b : (k + 1) * b]]
    return jnp.concatenate(parts, 1)


def separate(both, a, b, span):
    parts = [both[:, k * (a + b) : (k + 1) * (a + b)] for k in range(span)]
    first = jnp.concatenate([p[:, :a] for p in parts], 1)
    return first, jnp.concatenate([p[:, a:] for p in parts], 1)


def forward_layer(x, weights, small, fixed, head, span):
    w_qkv, w_up, w_last = weights
    gains, shifts, b_qkv, b_out, b_up, b_down = small
    xhat, inverse = normalise(x)
    attn_low = (xhat * gains[0] + shifts[0]).astype(BF16)
    mlp_low = (xhat * gains[1] + shifts[1]).astype(BF16)
    projected = dot(attn_low, w_qkv) + b_qkv
    query, keys, values, mixed_low, lse = attend(projected, fixed, head)
    hidden_pre = dot(mlp_low, w_up) + b_up
    cdf = 0.5 * (1.0 + lax.erf(hidden_pre * ROOT_HALF))
    hidden_low = (hidden_pre * cdf).astype(BF16)
    last_low = interleave(mixed_low, hidden_low, span)
    part = dot(last_low, w_last).astype(BF16)
    other = swap(part, "core")
    y = x + (part.astype(F32) + other.astype(F32) + b_out + b_down)
    attention = (query, keys, values, lse)
    return y, (xhat, inverse, attn_low, mlp_low, attention, hidden_pre, last_low)


def backward_layer(dy, weights, small, saved, fixed, head, place, slots, done, last):
    w_qkv, w_up, w_last = weights
    gains = small[0]
    xhat, inverse, attn_low, mlp_low, attention, hidden_pre, last_low = saved
    query, keys, values, lse = attention
    span = place.span
    dy_low = dy.astype(BF16)
    slots.add(reduce_weight(last_low, dy_low, place), done(2))
    d_branch_b = jnp.sum(dy_low.astype(F32), 0)

    dy_low = slots.step(dy_low)
    d_mixed, d_hidden = separate(
        dot_t(dy_low, w_last), query.shape[1] // span, hidden_pre.shape[1] // span, span
    )
    d_mixed = d_mixed.astype(BF16)
    cdf = 0.5 * (1.0 + lax.erf(hidden_pre * ROOT_HALF))
    density = jnp.exp(-0.5 * hidden_pre * hidden_pre) * (1.0 / math.sqrt(2.0 * math.pi))
    d_pre = (d_hidden * (cdf + hidden_pre * density)).astype(BF16)
    slots.add(reduce_weight(mlp_low, d_pre, place), done(1))
    d_up_b = jnp.sum(d_pre.astype(F32), 0)

    d_mixed, d_pre = slots.step((d_mixed, d_pre))
    d_qkv = jnp.concatenate(
        attend_back(query, keys, values, d_mixed, lse, fixed, head), 1
    )
    slots.add(reduce_weight(attn_low, d_qkv, place, last), done(0))
    d_mlp = dot_t(d_pre, w_up)

    d_qkv, d_mlp = slots.step((d_qkv, d_mlp))
    d_qkv_b = jnp.sum(d_qkv.astype(F32), 0)
    d_attn = dot_t(d_qkv, w_qkv)
    part = (d_attn * gains[0] + d_mlp * gains[1]).astype(BF16)
    d_xhat = part.astype(F32) + swap(part, "core").astype(F32)
    dx = dy + inverse * (
        d_xhat
        - jnp.mean(d_xhat, -1, keepdims=True)
        - xhat * jnp.mean(d_xhat * xhat, -1, keepdims=True)
    )
    d_gains = jnp.stack([jnp.sum(d_attn * xhat, 0), jnp.sum(d_mlp * xhat, 0)])
    d_shifts = jnp.stack([jnp.sum(d_attn, 0), jnp.sum(d_mlp, 0)])
    return dx, (d_gains, d_shifts, d_qkv_b, d_branch_b, d_up_b)


def pick_vector(v, width, place):
    return jnp.take(v.reshape(*v.shape[:-1], -1, 2, width), place.c, axis=-2).reshape(
        *v.shape[:-1], -1
    )


def spread_vector(v, width, place):
    blocks = v.reshape(-1, 1, width)
    here = (jnp.arange(2) == place.c)[None, :, None]
    return jnp.where(here, blocks, 0.0).reshape(-1)


def reduce_small(layers, head_cols, ff_cols, place):
    span = place.span
    parts = []
    for d_gains, d_shifts, d_qkv_b, d_branch_b, d_up_b in layers:
        parts += [
            d_gains,
            d_shifts,
            spread_vector(d_qkv_b, head_cols, place),
            jnp.where(place.c == 0, d_branch_b, 0.0),
            spread_vector(d_up_b, ff_cols, place),
        ]
    tables = [p.reshape(-1, span, p.shape[-1] // span) for p in parts]
    flat = jnp.concatenate(
        [jnp.moveaxis(t, 1, 0).reshape(span, -1, 128) for t in tables], 1
    )
    for axis in ("core", "xbit", "ybit"):
        other = yield swap(flat, axis)
        flat = flat + other
    if lax.axis_size("outer") > 1:
        flat = lax.psum(flat, "outer")
    blocks = yield spread(flat, place)
    total = sum(blocks)
    total = total.reshape(-1)
    out, start = [], 0
    for p in parts:
        size = p.size // span
        out.append(total[start : start + size].reshape(*p.shape[:-1], p.shape[-1] // span))
        start += size
    count = len(parts) // len(layers)
    return [jnp.stack(out[i::count]) for i in range(count)]


def on_device(span, *arguments):
    (
        hidden_in,
        segments,
        norm_gains,
        norm_biases,
        qkv_weight,
        qkv_bias,
        out_weight,
        out_bias,
        up_weight,
        up_bias,
        down_weight,
        down_bias,
        out_grad,
    ) = arguments
    place = Place(span)
    rows = hidden_in.shape[0]
    width = hidden_in.shape[2]
    head = width // H
    head_cols = width // (2 * span)
    ff_cols = up_weight.shape[2] // (2 * span)
    assert 2 * rows == span

    found = {}

    def keep(name):
        def done(value):
            found[name] = value

        return done

    def unit(index, arrays, wait):
        qkv, up, out, down = arrays
        layer, kind = divmod(index, 3)
        if kind == 0:
            half = pick_columns(qkv, layer, head_cols, place)
        elif kind == 1:
            half = pick_columns(up, layer, ff_cols, place)
        else:
            half = pick_rows((out, down), layer, place)
        slots.add(gather_weight(half, kind != 0, wait, place), keep(index))

    slots = Slots()
    arrays = (qkv_weight, up_weight, out_weight, down_weight)
    vectors = (norm_gains, norm_biases, qkv_bias, out_bias, up_bias, down_bias)
    unit(0, arrays, False)
    slots.add(row_to_chip(hidden_in, place), keep("rows"))
    slots.add(swap_once(segments), keep("segments"))
    arrays, vectors, out_grad = slots.step((arrays, vectors, out_grad))
    slots.add(gather_small(vectors, place), keep("vectors"))
    for index in range(1, 3 * LAYERS):
        unit(index, arrays, True)
        arrays, out_grad = slots.step((arrays, out_grad))
        if index == 3:
            slots.add(row_to_chip(out_grad, place), keep("grads"))
    while slots.parts:
        slots.step()
    weights = [[found[3 * layer + i] for i in range(3)] for layer in range(LAYERS)]

    stream, dy = found["rows"].astype(F32), found["grads"].astype(F32)
    seg_all = by_core(place, segments, found["segments"], 0)
    seg = lax.dynamic_index_in_dim(seg_all, place.z, 0, keepdims=False)
    seg_col, seg_row = seg[:, None], seg[None, :]
    length = seg.shape[0]
    earlier = jnp.sum((seg_row < seg_col).astype(jnp.int32), -1)
    positions = jnp.arange(length, dtype=jnp.int32) - earlier
    fixed = (*rotary_tables(positions, head), seg_col, seg_row)

    gains, shifts, b_qkv, b_out, b_up, b_down = found["vectors"]
    b_qkv = pick_vector(b_qkv, head_cols, place)
    b_up = pick_vector(b_up, ff_cols, place)
    smalls = [
        (gains[i], shifts[i], b_qkv[i], b_out[i], b_up[i], b_down[i]) for i in range(LAYERS)
    ]

    kept = []
    for layer in range(LAYERS):
        stream, saved = forward_layer(
            stream, weights[layer], smalls[layer], fixed, head, span
        )
        kept.append(saved)

    big = [None] * 3
    little = [None] * LAYERS
    slots = Slots()

    def done_for(layer):
        def of(index):
            def done(parts):
                if index == 2:
                    first_rows = out_weight.shape[1] // 2
                    big[2] = finish_rows(parts, first_rows, layer, big[2])
                else:
                    by = (head_cols, ff_cols)[index]
                    big[index] = finish_columns(parts, by, layer, big[index])

            return done

        return of

    out_low = stream.astype(BF16)
    for layer in reversed(range(LAYERS)):
        if layer == LAYERS - 2:
            slots.add(chip_to_rows(out_low, rows, place), keep("block_out"))
        dy, little[layer] = backward_layer(
            dy,
            weights[layer],
            smalls[layer],
            kept[layer],
            fixed,
            head,
            place,
            slots,
            done_for(layer),
            layer == 0,
        )
    slots.add(chip_to_rows(dy.astype(BF16), rows, place), keep("in_grad"))
    slots.add(reduce_small(little, head_cols, ff_cols, place), keep("sums"))
    while slots.parts:
        before = list(big)
        gated = slots.step(before)
        for i in range(3):
            if big[i] is before[i]:
                big[i] = gated[i]
    block_out, in_grad = found["block_out"], found["in_grad"].astype(F32)
    d_gains, d_shifts, d_qkv_b, d_branch_b, d_up_b = found["sums"]
    d_qkv_w, d_up_w, (d_out_w, d_down_w) = big
    d_out_w = d_out_w.reshape(LAYERS, -1, width)
    d_down_w = d_down_w.reshape(LAYERS, -1, width)
    return (
        block_out,
        in_grad,
        d_gains,
        d_shifts,
        d_qkv_w,
        d_qkv_b,
        d_out_w,
        d_branch_b,
        d_up_w,
        d_up_b,
        d_down_w,
        d_branch_b,
    )


def solution(mesh):
    rep, span = mesh.shape["rep"], mesh.shape["shard"]
    fine = Mesh(mesh.devices.reshape(rep // 8, 2, 2, 2, span), (*AXES, "shard"))
    tokens = P(AXES, "shard", None)
    last = P(None, None, "shard")
    middle = P(None, "shard", None)
    vector = P(None, "shard")
    in_specs = (
        tokens,
        P(AXES, None),
        last,
        last,
        middle,
        vector,
        middle,
        vector,
        middle,
        vector,
        middle,
        vector,
        tokens,
    )
    out_specs = (
        tokens,
        tokens,
        last,
        last,
        middle,
        vector,
        middle,
        vector,
        middle,
        vector,
        middle,
        vector,
    )

    def step(*arguments):
        return on_device(span, *arguments)

    return jax.shard_map(
        step, mesh=fine, in_specs=in_specs, out_specs=out_specs, check_vma=False
    )
```

```python
import math

import jax
import jax.numpy as jnp
from jax import lax
from jax.experimental import pallas as pl
from jax.experimental.pallas import tpu as pltpu
from jax.sharding import Mesh
from jax.sharding import PartitionSpec as P

H = 16
ROT = 16
LAYERS = 2
EPS = 1e-05
ROOT_HALF = math.sqrt(0.5)
F32 = jnp.float32
BF16 = jnp.bfloat16
AXES = ("outer", "ybit", "xbit", "core")
VMEM_LIMIT = 48 * 1024 * 1024
FORWARD_ROWS = 256
BACKWARD_ROWS = 512
FILLER = pl.CostEstimate(flops=8 * 10**9, bytes_accessed=1024, transcendentals=0)
LIGHT = pl.CostEstimate(flops=1024, bytes_accessed=1024, transcendentals=0)


def swap(x, axis):
    return lax.ppermute(x, axis, [(0, 1), (1, 0)])


def spin(x, k, span):
    return lax.ppermute(x, "shard", [(j, (j + k) % span) for j in range(span)])


def across(x, step, span):
    return lax.ppermute(x, "shard", [(j, j ^ step) for j in range(span)])


def dot(a, b):
    return jnp.dot(a, b, preferred_element_type=F32)


def dot_t(a, b):
    return lax.dot_general(a, b, (((1,), (1,)), ((), ())), preferred_element_type=F32)


class Place:
    def __init__(self, span):
        self.span = span
        self.z = lax.axis_index("shard")
        self.c = lax.axis_index("core")
        self.bx = lax.axis_index("xbit")
        self.by = lax.axis_index("ybit")
        self.q = 2 * self.by + self.bx
        self.scalars = jnp.stack([self.z, self.q, self.c]).astype(jnp.int32)


def from_relative(blocks, place):
    span = place.span
    order = [blocks[(-m) % span] for m in range(2 * span - 1)]
    return lax.dynamic_slice_in_dim(
        jnp.stack(order), lax.rem(span - place.z, span), span, 0
    )


def by_core(place, own, other, axis):
    return jnp.where(
        place.c == 0,
        jnp.concatenate([own, other], axis),
        jnp.concatenate([other, own], axis),
    )


def copy_call(body, out_shape, copies, operands, place):
    def kernel(scalars, *refs):
        ins, out, sems = refs[: len(operands)], refs[len(operands)], refs[-1]
        started = []
        for slot, (src, dst) in enumerate(body(scalars, ins, out)):
            copy = pltpu.make_async_copy(src, dst, sems.at[slot])
            copy.start()
            started.append(copy)
        for copy in started:
            copy.wait()

    return pl.pallas_call(
        kernel,
        out_shape=out_shape,
        in_specs=[pl.BlockSpec(memory_space=pltpu.SMEM)]
        + [pl.BlockSpec(memory_space=pltpu.HBM)] * len(operands),
        out_specs=pl.BlockSpec(memory_space=pltpu.VMEM),
        scratch_shapes=[pltpu.SemaphoreType.DMA((copies,))],
        compiler_params=pltpu.CompilerParams(vmem_limit_bytes=VMEM_LIMIT),
        cost_estimate=LIGHT,
    )(place.scalars, *operands)


def pick_columns(weights, layer, width, place):
    rows, columns = weights.shape[1:]
    count = columns // (2 * width)
    group = 2 if count % 2 == 0 else 1

    def kernel(scalars, *refs):
        out = refs[-1]
        for j in range(group):
            out[:, j * width : (j + 1) * width] = refs[j][0]

    def spec(j):
        return pl.BlockSpec(
            (1, rows, width), lambda i, s: (layer, 0, 2 * (group * i + j) + s[2])
        )

    return pl.pallas_call(
        kernel,
        grid_spec=pltpu.PrefetchScalarGridSpec(
            num_scalar_prefetch=1,
            grid=(count // group,),
            in_specs=[spec(j) for j in range(group)],
            out_specs=pl.BlockSpec((rows, group * width), lambda i, s: (0, i)),
        ),
        out_shape=jax.ShapeDtypeStruct((rows, count * width), weights.dtype),
        compiler_params=pltpu.CompilerParams(vmem_limit_bytes=VMEM_LIMIT),
        cost_estimate=LIGHT,
    )(place.scalars, *[weights] * group)


def pick_rows(arrays, layer, place):
    halves = [w.shape[1] // 2 for w in arrays]
    columns = arrays[0].shape[2]
    part = columns // 4 if columns % 512 == 0 else columns

    def kernel(scalars, *refs):
        start = 0
        for ref, half in zip(refs, halves, strict=False):
            refs[-1][start : start + half] = ref[0]
            start += half

    return pl.pallas_call(
        kernel,
        grid_spec=pltpu.PrefetchScalarGridSpec(
            num_scalar_prefetch=1,
            grid=(columns // part,),
            in_specs=[
                pl.BlockSpec((1, half, part), lambda i, s: (layer, s[2], i))
                for half in halves
            ],
            out_specs=pl.BlockSpec((sum(halves), part), lambda i, s: (0, i)),
        ),
        out_shape=jax.ShapeDtypeStruct((sum(halves), columns), arrays[0].dtype),
        compiler_params=pltpu.CompilerParams(vmem_limit_bytes=VMEM_LIMIT),
        cost_estimate=LIGHT,
    )(place.scalars, *arrays)


def other_shards(table, place):
    span = place.span

    def body(scalars, ins, out):
        for k in range(1, span):
            source = lax.rem(scalars[0] + (span - k), span)
            for i in range(2):
                yield ins[0].at[source, i], out.at[i, k - 1]

    shape = jax.ShapeDtypeStruct((2, span - 1, *table.shape[2:]), table.dtype)
    return copy_call(body, shape, 2 * (span - 1), [table], place)


def flipped(q, flip):
    return lax.bitwise_xor(q, jnp.int32(flip))


def overlaps(eighth, start, stop):
    for j in range(8):
        low, high = max(j * eighth, start), min((j + 1) * eighth, stop)
        if high > low:
            yield j, low, high


def assemble(half, cuts, near, near_x, near_y, far_a, far_b, place):
    span = place.span
    eighth, columns = half.shape[0] // 8, half.shape[1]
    block = (eighth, columns)

    def kernel(scalars, half_ref, n_ref, x_ref, y_ref, a_ref, b_ref, *rest):
        outs, table = rest[:-1], rest[-1]
        z, q = scalars[0], scalars[1]
        own = pl.program_id(0) == z

        @pl.when(own)
        def _():
            table[...] = half_ref[...]

        @pl.when(jnp.logical_not(own))
        def _():
            for i in range(2):
                for flip, ref in enumerate((n_ref, x_ref, y_ref)):
                    table[flipped(q, flip), i] = ref[i, 0]
            table[flipped(q, 3), 0] = a_ref[0]
            table[flipped(q, 3), 1] = b_ref[0]

        for out, (start, stop, left, right) in zip(outs, cuts, strict=True):
            for j, low, high in overlaps(eighth, start, stop):
                out[0, low - start : high - start] = table[
                    j // 2, j % 2, low - j * eighth : high - j * eighth, left:right
                ]

    def behind(j, s):
        return jnp.maximum(lax.rem(s[0] + span - j, span), 1) - 1

    near_spec = pl.BlockSpec((2, 1, *block), lambda j, s: (0, behind(j, s), 0, 0))
    far_spec = pl.BlockSpec((1, *block), lambda j, s: (behind(j, s), 0, 0))
    outs = pl.pallas_call(
        kernel,
        grid_spec=pltpu.PrefetchScalarGridSpec(
            num_scalar_prefetch=1,
            grid=(span,),
            in_specs=[
                pl.BlockSpec((4, 2, *block), lambda j, s: (0, 0, 0, 0)),
                near_spec,
                near_spec,
                near_spec,
                far_spec,
                far_spec,
            ],
            out_specs=[
                pl.BlockSpec((1, b - a, d - c), lambda j, s: (j, 0, 0)) for a, b, c, d in cuts
            ],
            scratch_shapes=[pltpu.VMEM((4, 2, *block), half.dtype)],
        ),
        out_shape=[
            jax.ShapeDtypeStruct((span, b - a, d - c), half.dtype) for a, b, c, d in cuts
        ],
        compiler_params=pltpu.CompilerParams(vmem_limit_bytes=VMEM_LIMIT),
        cost_estimate=LIGHT,
    )(
        place.scalars,
        half.reshape(4, 2, *block),
        near,
        near_x,
        near_y,
        far_a,
        far_b,
    )
    return [out.reshape(-1, out.shape[2]) for out in outs]


def absolute_quarters(summed, near_x, near_y, far_a, far_b, place):
    def body(scalars, ins, out):
        q = scalars[1]
        for flip in range(3):
            yield ins[flip], out.at[flipped(q, flip)]
        for i in range(2):
            yield ins[3 + i], out.at[flipped(q, 3), i]

    shape = jax.ShapeDtypeStruct((4, *summed.shape), summed.dtype)
    return copy_call(body, shape, 5, [summed, near_x, near_y, far_a, far_b], place)


def weight_gradient(lefts, right, place):
    span = place.span
    tokens, columns = right.shape
    sizes = [left.shape[1] // span for left in lefts]
    eighth = sum(sizes) // 8

    def kernel(scalars, *refs):
        left_refs, right_ref = refs[: len(sizes)], refs[len(sizes)]
        own, pass_a, pass_b, send_a, send_b, table = refs[len(sizes) + 1 :]
        q = scalars[1]
        start = 0
        for left_ref, size in zip(left_refs, sizes, strict=True):
            product = lax.dot_general(
                left_ref[...],
                right_ref[...],
                (((0,), (0,)), ((), ())),
                preferred_element_type=F32,
            ).astype(BF16)
            for j, low, high in overlaps(eighth, start, start + size):
                table[j // 2, j % 2, low - j * eighth : high - j * eighth] = product[
                    low - start : high - start
                ]
            start += size
        near_x, near_y, far = flipped(q, 1), flipped(q, 2), flipped(q, 3)
        own[0, 0], own[0, 1] = table[q, 0], table[q, 1]
        pass_a[0], pass_b[0] = table[near_y, 0], table[near_x, 1]
        send_a[0, 0], send_a[1, 0] = table[near_x, 0], table[far, 0]
        send_b[0, 0], send_b[1, 0] = table[near_y, 1], table[far, 1]

    block = (eighth, columns)
    one = pl.BlockSpec((1, *block), lambda k, s: (k, 0, 0))
    two = pl.BlockSpec((2, 1, *block), lambda k, s: (0, k, 0, 0))
    return pl.pallas_call(
        kernel,
        grid_spec=pltpu.PrefetchScalarGridSpec(
            num_scalar_prefetch=1,
            grid=(span,),
            in_specs=[
                *[
                    pl.BlockSpec((tokens, size), lambda k, s: (0, lax.bitwise_xor(s[0], k)))
                    for size in sizes
                ],
                pl.BlockSpec((tokens, columns), lambda k, s: (0, 0)),
            ],
            out_specs=[
                pl.BlockSpec((1, 2, *block), lambda k, s: (k, 0, 0, 0)),
                one,
                one,
                two,
                two,
            ],
            scratch_shapes=[pltpu.VMEM((4, 2, *block), BF16)],
        ),
        out_shape=[
            pltpu.HBM((span, 2, *block), BF16),
            pltpu.HBM((span, *block), BF16),
            pltpu.HBM((span, *block), BF16),
            pltpu.HBM((2, span, *block), BF16),
            pltpu.HBM((2, span, *block), BF16),
        ],
        compiler_params=pltpu.CompilerParams(vmem_limit_bytes=VMEM_LIMIT),
        cost_estimate=LIGHT,
    )(place.scalars, *lefts, right)


def combine(own, got_a, got_b, more_a, more_b):
    span, _, eighth, columns = own.shape
    part = columns // 4 if columns % 512 == 0 else columns

    def kernel(own_ref, ga_ref, gb_ref, ma_ref, mb_ref, *outs):
        for j, out in enumerate(outs):
            here = slice(j * span // 2, (j + 1) * span // 2)
            for i, (got, more) in enumerate(((ga_ref, ma_ref), (gb_ref, mb_ref))):
                total = own_ref[here, i].astype(F32) + got[0, here].astype(F32)
                out[:, i] = (total + more[here].astype(F32)).astype(BF16)

    got = pl.BlockSpec((1, span, eighth, part), lambda j: (0, 0, 0, j))
    more = pl.BlockSpec((span, eighth, part), lambda j: (0, 0, j))
    whole = pl.BlockSpec((span, 2, eighth, part), lambda j: (0, 0, 0, j))
    half = pl.BlockSpec((span // 2, 2, eighth, part), lambda j: (0, 0, 0, j))
    return pl.pallas_call(
        kernel,
        grid=(columns // part,),
        in_specs=[whole, got, got, more, more],
        out_specs=[half, half],
        out_shape=[jax.ShapeDtypeStruct((span // 2, *own.shape[1:]), BF16)] * 2,
        compiler_params=pltpu.CompilerParams(vmem_limit_bytes=VMEM_LIMIT),
        cost_estimate=LIGHT,
    )(own, got_a, got_b, more_a, more_b)


def finish_columns(parts, width, layer, previous):
    _, _, rows, columns = parts.shape

    def kernel(part_ref, *rest):
        out_ref = rest[-1]
        for core in range(2):
            for j in range(columns // width):
                start = (2 * j + core) * width
                out_ref[0, :, start : start + width] = part_ref[
                    0, core, :, j * width : (j + 1) * width
                ].astype(F32)

    operands, in_specs, aliases = (
        [parts],
        [pl.BlockSpec((1, 2, rows, columns), lambda q: (q, 0, 0, 0))],
        {},
    )
    if previous is not None:
        operands.append(previous)
        in_specs.append(pl.BlockSpec(memory_space=pl.ANY))
        aliases = {1: 0}
    return pl.pallas_call(
        kernel,
        grid=(4,),
        in_specs=in_specs,
        out_specs=pl.BlockSpec((1, rows, 2 * columns), lambda q: (layer, q, 0)),
        out_shape=jax.ShapeDtypeStruct((LAYERS, 4 * rows, 2 * columns), F32),
        input_output_aliases=aliases,
        compiler_params=pltpu.CompilerParams(vmem_limit_bytes=VMEM_LIMIT),
        cost_estimate=LIGHT,
    )(*operands)


def finish_rows(parts, first_rows, layer, previous):
    _, _, quarter, columns = parts.shape
    sizes = (first_rows, 4 * quarter - first_rows)

    def kernel(part_ref, *rest):
        first, second = rest[-2:]
        for q in range(4):
            start, stop = q * quarter, (q + 1) * quarter
            cut = min(max(first_rows, start), stop)
            if cut > start:
                first[0, :, start:cut] = part_ref[q, :, : cut - start].astype(F32)
            if stop > cut:
                second[0, :, cut - first_rows : stop - first_rows] = part_ref[
                    q, :, cut - start :
                ].astype(F32)

    half = columns // 4 if columns % 512 == 0 else columns
    operands, aliases = [parts], {}
    in_specs = [pl.BlockSpec((4, 2, quarter, half), lambda j: (0, 0, 0, j))]
    if previous is not None:
        operands += list(previous)
        in_specs += [pl.BlockSpec(memory_space=pl.ANY)] * 2
        aliases = {1: 0, 2: 1}
    return pl.pallas_call(
        kernel,
        grid=(columns // half,),
        in_specs=in_specs,
        out_specs=[
            pl.BlockSpec((1, 2, size, half), lambda j: (layer, 0, 0, j)) for size in sizes
        ],
        out_shape=[
            jax.ShapeDtypeStruct((LAYERS, 2, size, columns), F32) for size in sizes
        ],
        input_output_aliases=aliases,
        compiler_params=pltpu.CompilerParams(vmem_limit_bytes=VMEM_LIMIT),
        cost_estimate=LIGHT,
    )(*operands)


def in_order(blocks, place):
    span = place.span

    def body(scalars, ins, out):
        for k in range(span):
            yield ins[k], out.at[lax.rem(scalars[0] + (span - k), span)]

    shape = jax.ShapeDtypeStruct((span, *blocks[0].shape), blocks[0].dtype)
    return copy_call(body, shape, span, list(blocks), place)


def spread(blocks, place):
    span = place.span
    out = []
    for k in range(span):
        block = lax.dynamic_index_in_dim(
            blocks, lax.rem(place.z + k, span), 0, keepdims=False
        )
        out.append(block if k == 0 else spin(block, k, span))
    return out


def row_to_chip(x, place):
    rows, tokens, width = x.shape
    half = width // 2
    mine = lax.dynamic_slice_in_dim(x, place.c * half, half, 2)
    theirs = lax.dynamic_slice_in_dim(x, (1 - place.c) * half, half, 2)
    theirs = yield swap(theirs, "core")
    blocks = yield spread(by_core(place, mine, theirs, 0), place)
    own = in_order(blocks, place).reshape(place.span * tokens, half)
    other = yield swap(own, "core")
    return by_core(place, own, other, 1)


def chip_to_rows(y, rows, place):
    span = place.span
    width = y.shape[1]
    tokens = y.shape[0] // span
    half = width // 2
    mine = lax.dynamic_slice_in_dim(y, place.c * half, half, 1)
    blocks = yield spread(mine.reshape(span, tokens, half), place)
    stacked = in_order(blocks, place)
    own = lax.dynamic_slice_in_dim(stacked, place.c * rows, rows, 0)
    theirs = lax.dynamic_slice_in_dim(stacked, (1 - place.c) * rows, rows, 0)
    other = yield swap(theirs, "core")
    return by_core(place, own, other, 2)


class Slots:
    def __init__(self):
        self.parts = []

    def add(self, part, done):
        self.parts.append([part, next(part), done])

    def step(self, extra=()):
        pending, extra = lax.optimization_barrier(
            ([part[1] for part in self.parts], extra)
        )
        alive = []
        for part, arrived in zip(self.parts, pending, strict=True):
            try:
                part[1] = part[0].send(arrived)
                alive.append(part)
            except StopIteration as end:
                part[2](end.value)
        self.parts = alive
        return extra


def gather_weight(half, cuts, by_call, wait, place):
    span = place.span
    eighth, columns = half.shape[0] // 8, half.shape[1]
    mine = lax.dynamic_index_in_dim(
        half.reshape(4, 2, eighth, columns), place.q, 0, keepdims=False
    )
    if by_call:
        moving = lax.all_gather(mine, "shard")
    else:
        moving = [spin(mine, k, span) for k in range(1, span)]
    if wait:
        yield ()
    arrived = yield moving
    near = other_shards(arrived, place) if by_call else jnp.stack(arrived, 1)
    near_x, near_y = yield [swap(near, "xbit"), swap(near, "ybit")]
    far_a, far_b = yield [swap(near_x[0], "ybit"), swap(near_y[1], "xbit")]
    return assemble(half, cuts, near, near_x, near_y, far_a, far_b, place)


def reduce_weight(lefts, right, place, last=False):
    own, pass_a, pass_b, send_a, send_b = yield weight_gradient(lefts, right, place)
    got_a, got_b = yield [swap(send_a, "xbit"), swap(send_b, "ybit")]
    onward_a = (pass_a.astype(F32) + got_a[1].astype(F32)).astype(BF16)
    onward_b = (pass_b.astype(F32) + got_b[1].astype(F32)).astype(BF16)
    more_a, more_b = yield [swap(onward_a, "ybit"), swap(onward_b, "xbit")]
    keep, send = combine(own, got_a, got_b, more_a, more_b)
    step = place.span // 2
    while step > 1:
        other = yield across(send, step, place.span)
        step //= 2
        send = (keep[step:].astype(F32) + other[step:].astype(F32)).astype(BF16)
        keep = keep[:step].astype(F32) + other[:step].astype(F32)
    other = yield across(send, step, place.span)
    summed = (keep[0].astype(F32) + other[0].astype(F32)).astype(BF16)
    if lax.axis_size("outer") > 1:
        summed = lax.psum(summed, "outer")
    _, eighth, columns = summed.shape
    if last:
        near_x, near_y = yield [swap(summed, "xbit"), swap(summed, "ybit")]
        far_a, far_b = yield [swap(near_x[0], "ybit"), swap(near_y[1], "xbit")]
        half = absolute_quarters(summed, near_x, near_y, far_a, far_b, place)
        other = yield swap(half, "core")
        parts = by_core(place, half[:, None], other[:, None], 1)
    else:
        parts = yield lax.all_gather(summed, ("ybit", "xbit", "core"))
    return parts.reshape(4, 2, 2 * eighth, columns)


def gather_small(vectors, place):
    flat = jnp.concatenate([v.reshape(-1) for v in vectors])
    blocks = yield [flat] + [spin(flat, k, place.span) for k in range(1, place.span)]
    table = from_relative(blocks, place)
    out, start = [], 0
    for v in vectors:
        part = table[:, start : start + v.size].reshape(place.span, *v.shape)
        start += v.size
        part = jnp.moveaxis(part, 0, -2)
        out.append(part.reshape(*v.shape[:-1], -1).astype(F32))
    return out


def blocks_of(length, step):
    step = step if length % step == 0 else length
    return [(i * step, step) for i in range(length // step)]


def fill_bias(bias, seg_col, seg_row):
    @pl.when(pl.program_id(0) == 0)
    def _():
        row = lax.broadcasted_iota(jnp.int32, bias.shape, 0)
        col = lax.broadcasted_iota(jnp.int32, bias.shape, 1)
        mask = (col <= row) & (seg_col[...] == seg_row[...])
        bias[...] = jnp.where(mask, 0.0, -1e30)


def turn(u, tables):
    keep, upper, lower = tables
    half, lanes = ROT // 2, u.shape[1]
    return u * keep + pltpu.roll(u, lanes - half, 1) * upper + pltpu.roll(u, half, 1) * lower


def turn_back(d, tables):
    keep, upper, lower = tables
    half, lanes = ROT // 2, d.shape[1]
    return d * keep + pltpu.roll(d * upper, half, 1) + pltpu.roll(d * lower, lanes - half, 1)


def attend_kernel(scale, head, *refs):
    q_in, k_in, v_in, keep, upper, lower, seg_col, seg_row = refs[:8]
    q_ref, k_ref, v_ref, o_ref, lse_ref, bias = refs[8:]
    fill_bias(bias, seg_col, seg_row)
    tables = keep[...], upper[...], lower[...]
    q_ref[...] = turn(q_in[...], tables).astype(BF16)
    k_ref[...] = turn(k_in[...], tables).astype(BF16)
    v_ref[...] = v_in[...].astype(BF16)
    for start, step in blocks_of(q_ref.shape[0], FORWARD_ROWS):
        stop = start + step
        for h in range(q_ref.shape[1] // head):
            lanes = slice(h * head, (h + 1) * head)
            query = q_ref[start:stop, lanes] * scale
            scores = dot_t(query, k_ref[:stop, lanes]) + bias[start:stop, :stop]
            top = jnp.max(scores, -1, keepdims=True)
            expo = jnp.exp(scores - top)
            total = jnp.sum(expo, -1, keepdims=True)
            probs = (expo * (1.0 / total)).astype(BF16)
            o_ref[start:stop, lanes] = dot(probs, v_ref[:stop, lanes]).astype(BF16)
            lse_ref[h, start:stop, :] = top + jnp.log(total)


def attend_back_kernel(scale, head, *refs):
    q_ref, k_ref, v_ref, do_ref, lse_ref, keep, upper, lower, seg_col, seg_row = refs[:10]
    dq_out, dk_out, dv_out, dq_ref, dk_ref, dv_ref, bias = refs[10:]
    fill_bias(bias, seg_col, seg_row)
    over_rows = (((0,), (0,)), ((), ()))
    length = q_ref.shape[0]
    if len(blocks_of(length, BACKWARD_ROWS)) > 1:
        dk_ref[...] = jnp.zeros_like(dk_ref)
        dv_ref[...] = jnp.zeros_like(dv_ref)
    for start, step in blocks_of(length, BACKWARD_ROWS):
        stop = start + step
        for h in range(q_ref.shape[1] // head):
            lanes = slice(h * head, (h + 1) * head)
            query = q_ref[start:stop, lanes] * scale
            keys = k_ref[:stop, lanes]
            grad = do_ref[start:stop, lanes]
            scores = dot_t(query, keys) + bias[start:stop, :stop]
            probs = jnp.exp(scores - lse_ref[h, start:stop, :])
            d_probs = dot_t(grad, v_ref[:stop, lanes])
            delta = jnp.sum(probs * d_probs, -1, keepdims=True)
            d_scores = (probs * (d_probs - delta)).astype(BF16)
            dq_ref[start:stop, lanes] = dot(d_scores, keys) * scale
            d_key = lax.dot_general(d_scores, query, over_rows, preferred_element_type=F32)
            d_value = lax.dot_general(
                probs.astype(BF16), grad, over_rows, preferred_element_type=F32
            )
            if step == length:
                dk_ref[:, lanes], dv_ref[:, lanes] = d_key, d_value
            else:
                dk_ref[:stop, lanes] += d_key
                dv_ref[:stop, lanes] += d_value
    tables = keep[...], upper[...], lower[...]
    dq_out[...] = turn_back(dq_ref[...], tables).astype(BF16)
    dk_out[...] = turn_back(dk_ref[...], tables).astype(BF16)
    dv_out[...] = dv_ref[...].astype(BF16)


def attention_specs(length, width, head):
    group = max(head, 128)
    count = width // group
    wide = pl.BlockSpec((length, group), lambda i: (0, i))
    lse = pl.BlockSpec((group // head, length, 1), lambda i: (i, 0, 0))
    same = [pl.BlockSpec((length, group), lambda i: (0, 0))] * 3 + [
        pl.BlockSpec((length, 1), lambda i: (0, 0)),
        pl.BlockSpec((1, length), lambda i: (0, 0)),
    ]
    return group, count, wide, lse, same


def attend(projected, fixed, head):
    length, width = projected.shape[0], projected.shape[1] // 3
    group, count, wide, lse, same = attention_specs(length, width, head)

    def kernel(*refs):
        attend_kernel(1.0 / math.sqrt(head), head, *refs)

    low = jax.ShapeDtypeStruct((length, width), BF16)
    saved = pltpu.HBM((length, width), BF16)
    return pl.pallas_call(
        kernel,
        grid=(count,),
        in_specs=[
            wide,
            pl.BlockSpec((length, group), lambda i: (0, count + i)),
            pl.BlockSpec((length, group), lambda i: (0, 2 * count + i)),
            *same,
        ],
        out_specs=[wide, wide, wide, wide, lse],
        out_shape=[
            saved,
            saved,
            saved,
            low,
            pltpu.HBM((width // head, length, 1), F32),
        ],
        scratch_shapes=[pltpu.VMEM((length, length), F32)],
        compiler_params=pltpu.CompilerParams(vmem_limit_bytes=VMEM_LIMIT),
        cost_estimate=FILLER,
    )(projected, projected, projected, *fixed)


def attend_back(query, keys, values, d_mixed, lse_all, fixed, head):
    length, width = query.shape
    group, count, wide, lse, same = attention_specs(length, width, head)

    def kernel(*refs):
        attend_back_kernel(1.0 / math.sqrt(head), head, *refs)

    out = jax.ShapeDtypeStruct((length, width), BF16)
    return pl.pallas_call(
        kernel,
        grid=(count,),
        in_specs=[wide, wide, wide, wide, lse, *same],
        out_specs=[wide, wide, wide],
        out_shape=[out, out, out],
        scratch_shapes=[pltpu.VMEM((length, group), F32)] * 3
        + [pltpu.VMEM((length, length), F32)],
        compiler_params=pltpu.CompilerParams(vmem_limit_bytes=VMEM_LIMIT),
        cost_estimate=LIGHT,
    )(query, keys, values, d_mixed, lse_all, *fixed)


def rotary_tables(positions, head):
    half = ROT // 2
    inverse = jnp.power(10000.0, -2.0 * jnp.arange(half, dtype=F32) / ROT)
    angles = positions.astype(F32)[:, None] * inverse
    cos, sin = jnp.cos(angles), jnp.sin(angles)
    rest = jnp.zeros((positions.shape[0], head - ROT), F32)
    none = jnp.zeros_like(sin)
    keep = [cos, cos, rest + 1.0]
    upper = [-sin, none, rest]
    lower = [none, sin, rest]
    times = max(1, 128 // head)
    return [jnp.concatenate(t * times, 1) for t in (keep, upper, lower)]


def normalise(x):
    centred = x - jnp.mean(x, -1, keepdims=True)
    spread = jnp.mean(centred * centred, -1, keepdims=True)
    inverse = lax.rsqrt(spread + EPS)
    return centred * inverse, inverse


def forward_layer(x, weights, small, fixed, head):
    w_qkv, w_up, w_out, w_down = weights
    gains, shifts, b_qkv, b_out, b_up, b_down = small
    xhat, inverse = normalise(x)
    attn_low = (xhat * gains[0] + shifts[0]).astype(BF16)
    mlp_low = (xhat * gains[1] + shifts[1]).astype(BF16)
    projected = dot(attn_low, w_qkv) + b_qkv
    query, keys, values, mixed_low, lse = attend(projected, fixed, head)
    hidden_pre = dot(mlp_low, w_up) + b_up
    cdf = 0.5 * (1.0 + lax.erf(hidden_pre * ROOT_HALF))
    hidden_low = (hidden_pre * cdf).astype(BF16)
    part = (dot(mixed_low, w_out) + dot(hidden_low, w_down)).astype(BF16)
    other = swap(part, "core")
    y = x + (part.astype(F32) + other.astype(F32) + b_out + b_down)
    attention = (query, keys, values, lse)
    return y, (xhat, inverse, attn_low, mlp_low, attention, hidden_pre, mixed_low, hidden_low)


def backward_layer(dy, weights, small, saved, fixed, head, place, slots, done, last, mover):
    w_qkv, w_up, w_out, w_down = weights
    gains = small[0]
    xhat, inverse, attn_low, mlp_low, attention, hidden_pre, mixed_low, hidden_low = saved
    query, keys, values, lse = attention
    dy_low = dy.astype(BF16)
    slots.add(reduce_weight([mixed_low, hidden_low], dy_low, place), done(2))
    d_branch_b = jnp.sum(dy_low.astype(F32), 0)

    dy_low = slots.step(dy_low)
    d_hidden = dot_t(dy_low, w_down)
    d_mixed = dot_t(dy_low, w_out).astype(BF16)
    cdf = 0.5 * (1.0 + lax.erf(hidden_pre * ROOT_HALF))
    density = jnp.exp(-0.5 * hidden_pre * hidden_pre) * (1.0 / math.sqrt(2.0 * math.pi))
    d_pre = (d_hidden * (cdf + hidden_pre * density)).astype(BF16)
    slots.add(reduce_weight([mlp_low], d_pre, place), done(1))
    d_up_b = jnp.sum(d_pre.astype(F32), 0)

    d_mixed, d_pre = slots.step((d_mixed, d_pre))
    if mover is not None:
        slots.add(*mover)
    d_qkv = jnp.concatenate(
        attend_back(query, keys, values, d_mixed, lse, fixed, head), 1
    )
    slots.add(reduce_weight([attn_low], d_qkv, place, last), done(0))
    d_mlp = dot_t(d_pre, w_up)

    d_qkv, d_mlp = slots.step((d_qkv, d_mlp))
    d_qkv_b = jnp.sum(d_qkv.astype(F32), 0)
    d_attn = dot_t(d_qkv, w_qkv)
    part = (d_attn * gains[0] + d_mlp * gains[1]).astype(BF16)
    d_xhat = part.astype(F32) + swap(part, "core").astype(F32)
    dx = dy + inverse * (
        d_xhat
        - jnp.mean(d_xhat, -1, keepdims=True)
        - xhat * jnp.mean(d_xhat * xhat, -1, keepdims=True)
    )
    d_gains = jnp.stack([jnp.sum(d_attn * xhat, 0), jnp.sum(d_mlp * xhat, 0)])
    d_shifts = jnp.stack([jnp.sum(d_attn, 0), jnp.sum(d_mlp, 0)])
    return dx, (d_gains, d_shifts, d_qkv_b, d_branch_b, d_up_b)


def pick_vector(v, width, place):
    return jnp.take(v.reshape(*v.shape[:-1], -1, 2, width), place.c, axis=-2).reshape(
        *v.shape[:-1], -1
    )


def spread_vector(v, width, place):
    blocks = v.reshape(-1, 1, width)
    here = (jnp.arange(2) == place.c)[None, :, None]
    return jnp.where(here, blocks, 0.0).reshape(-1)


def reduce_small(layers, head_cols, ff_cols, place):
    span = place.span
    parts = []
    for d_gains, d_shifts, d_qkv_b, d_branch_b, d_up_b in layers:
        parts += [
            d_gains,
            d_shifts,
            spread_vector(d_qkv_b, head_cols, place),
            jnp.where(place.c == 0, d_branch_b, 0.0),
            spread_vector(d_up_b, ff_cols, place),
        ]
    tables = [p.reshape(-1, span, p.shape[-1] // span) for p in parts]
    flat = jnp.concatenate(
        [jnp.moveaxis(t, 1, 0).reshape(span, -1, 128) for t in tables], 1
    )
    for axis in ("core", "xbit", "ybit"):
        other = yield swap(flat, axis)
        flat = flat + other
    if lax.axis_size("outer") > 1:
        flat = lax.psum(flat, "outer")
    blocks = yield spread(flat, place)
    total = sum(blocks)
    total = total.reshape(-1)
    out, start = [], 0
    for p in parts:
        size = p.size // span
        out.append(total[start : start + size].reshape(*p.shape[:-1], p.shape[-1] // span))
        start += size
    count = len(parts) // len(layers)
    return [jnp.stack(out[i::count]) for i in range(count)]


def on_device(span, *arguments):
    (
        hidden_in,
        segments,
        norm_gains,
        norm_biases,
        qkv_weight,
        qkv_bias,
        out_weight,
        out_bias,
        up_weight,
        up_bias,
        down_weight,
        down_bias,
        out_grad,
    ) = arguments
    place = Place(span)
    rows = hidden_in.shape[0]
    width = hidden_in.shape[2]
    head = width // H
    head_cols = width // (2 * span)
    ff_cols = up_weight.shape[2] // (2 * span)
    assert 2 * rows == span

    found = {}

    def keep(name):
        def done(value):
            found[name] = value

        return done

    def unit(name, arrays, wait):
        qkv, up, out, down = arrays
        kind, layer = name
        if kind == "last":
            half = pick_rows((out, down), layer, place)
            split = out.shape[1] // 2
            cuts = [(0, split, 0, width), (split, half.shape[0], 0, width)]
        else:
            parts = []
            if kind != "up":
                parts.append(pick_columns(qkv, layer, head_cols, place))
            if kind != "qkv":
                parts.append(pick_columns(up, layer, ff_cols, place))
            half = jnp.concatenate(parts, 1) if len(parts) > 1 else parts[0]
            cuts, start = [], 0
            for part in parts:
                cuts.append((0, part.shape[0], start, start + part.shape[1]))
                start += part.shape[1]
        slots.add(gather_weight(half, cuts, kind != "qkv", wait, place), keep(name))

    slots = Slots()
    arrays = (qkv_weight, up_weight, out_weight, down_weight)
    vectors = (norm_gains, norm_biases, qkv_bias, out_bias, up_bias, down_bias)
    units = [("qkv", 0), ("up", 0), ("last", 0)]
    for layer in range(1, LAYERS):
        units += [("both", layer), ("last", layer)]
    unit(units[0], arrays, False)
    slots.add(row_to_chip(hidden_in, place), keep("rows"))
    seg_other = swap(segments, "core")
    arrays, vectors, out_grad = slots.step((arrays, vectors, out_grad))
    slots.add(gather_small(vectors, place), keep("vectors"))
    for name in units[1:]:
        unit(name, arrays, True)
        arrays, out_grad = slots.step((arrays, out_grad))
    slots.add(row_to_chip(out_grad, place), keep("grads"))
    while slots.parts:
        slots.step()
    weights = [
        (*found["qkv", 0], *found["up", 0], *found["last", 0]),
        *((*found["both", i], *found["last", i]) for i in range(1, LAYERS)),
    ]

    stream, dy = found["rows"].astype(F32), found["grads"].astype(F32)
    seg_all = by_core(place, segments, seg_other, 0)
    seg = lax.dynamic_index_in_dim(seg_all, place.z, 0, keepdims=False)
    seg_col, seg_row = seg[:, None], seg[None, :]
    length = seg.shape[0]
    earlier = jnp.sum((seg_row < seg_col).astype(jnp.int32), -1)
    positions = jnp.arange(length, dtype=jnp.int32) - earlier
    fixed = (*rotary_tables(positions, head), seg_col, seg_row)

    gains, shifts, b_qkv, b_out, b_up, b_down = found["vectors"]
    b_qkv = pick_vector(b_qkv, head_cols, place)
    b_up = pick_vector(b_up, ff_cols, place)
    smalls = [
        (gains[i], shifts[i], b_qkv[i], b_out[i], b_up[i], b_down[i]) for i in range(LAYERS)
    ]

    kept = []
    for layer in range(LAYERS):
        stream, saved = forward_layer(
            stream, weights[layer], smalls[layer], fixed, head
        )
        kept.append(saved)

    big = [None] * 3
    little = [None] * LAYERS
    slots = Slots()

    def done_for(layer):
        def of(index):
            def done(parts):
                if index == 2:
                    first_rows = out_weight.shape[1] // 2
                    big[2] = finish_rows(parts, first_rows, layer, big[2])
                else:
                    by = (head_cols, ff_cols)[index]
                    big[index] = finish_columns(parts, by, layer, big[index])

            return done

        return of

    out_low = stream.astype(BF16)
    for layer in reversed(range(LAYERS)):
        mover = None
        if layer == 0:
            mover = (chip_to_rows(out_low, rows, place), keep("block_out"))
        dy, little[layer] = backward_layer(
            dy,
            weights[layer],
            smalls[layer],
            kept[layer],
            fixed,
            head,
            place,
            slots,
            done_for(layer),
            layer == 0,
            mover,
        )
    slots.add(chip_to_rows(dy.astype(BF16), rows, place), keep("in_grad"))
    slots.add(reduce_small(little, head_cols, ff_cols, place), keep("sums"))
    while slots.parts:
        before = list(big)
        gated = slots.step(before)
        for i in range(3):
            if big[i] is before[i]:
                big[i] = gated[i]
    block_out, in_grad = found["block_out"], found["in_grad"].astype(F32)
    d_gains, d_shifts, d_qkv_b, d_branch_b, d_up_b = found["sums"]
    d_qkv_w, d_up_w, (d_out_w, d_down_w) = big
    d_out_w = d_out_w.reshape(LAYERS, -1, width)
    d_down_w = d_down_w.reshape(LAYERS, -1, width)
    return (
        block_out,
        in_grad,
        d_gains,
        d_shifts,
        d_qkv_w,
        d_qkv_b,
        d_out_w,
        d_branch_b,
        d_up_w,
        d_up_b,
        d_down_w,
        d_branch_b,
    )


def solution(mesh):
    rep, span = mesh.shape["rep"], mesh.shape["shard"]
    fine = Mesh(mesh.devices.reshape(rep // 8, 2, 2, 2, span), (*AXES, "shard"))
    tokens = P(AXES, "shard", None)
    last = P(None, None, "shard")
    middle = P(None, "shard", None)
    vector = P(None, "shard")
    in_specs = (
        tokens,
        P(AXES, None),
        last,
        last,
        middle,
        vector,
        middle,
        vector,
        middle,
        vector,
        middle,
        vector,
        tokens,
    )
    out_specs = (
        tokens,
        tokens,
        last,
        last,
        middle,
        vector,
        middle,
        vector,
        middle,
        vector,
        middle,
        vector,
    )

    def step(*arguments):
        return on_device(span, *arguments)

    return jax.shard_map(
        step, mesh=fine, in_specs=in_specs, out_specs=out_specs, check_vma=False
    )
```

```python
import math

import jax
import jax.numpy as jnp
from jax import lax
from jax.experimental import pallas as pl
from jax.experimental.pallas import tpu as pltpu
from jax.sharding import Mesh
from jax.sharding import PartitionSpec as P

H = 16
ROT = 16
LAYERS = 2
EPS = 1e-05
ROOT_HALF = math.sqrt(0.5)
F32 = jnp.float32
BF16 = jnp.bfloat16
AXES = ("outer", "ybit", "xbit", "core")
VMEM_LIMIT = 48 * 1024 * 1024
FORWARD_ROWS = 256
BACKWARD_ROWS = 512
FILLER = pl.CostEstimate(flops=8 * 10**9, bytes_accessed=1024, transcendentals=0)
LIGHT = pl.CostEstimate(flops=1024, bytes_accessed=1024, transcendentals=0)


def swap(x, axis):
    return lax.ppermute(x, axis, [(0, 1), (1, 0)])


def spin(x, k, span):
    return lax.ppermute(x, "shard", [(j, (j + k) % span) for j in range(span)])


def across(x, step, span):
    return lax.ppermute(x, "shard", [(j, j ^ step) for j in range(span)])


def dot(a, b):
    return jnp.dot(a, b, preferred_element_type=F32)


def dot_t(a, b):
    return lax.dot_general(a, b, (((1,), (1,)), ((), ())), preferred_element_type=F32)


class Place:
    def __init__(self, span):
        self.span = span
        self.z = lax.axis_index("shard")
        self.c = lax.axis_index("core")
        self.bx = lax.axis_index("xbit")
        self.by = lax.axis_index("ybit")
        self.q = 2 * self.by + self.bx
        self.scalars = jnp.stack([self.z, self.q, self.c]).astype(jnp.int32)


def from_relative(blocks, place):
    span = place.span
    order = [blocks[(-m) % span] for m in range(2 * span - 1)]
    return lax.dynamic_slice_in_dim(
        jnp.stack(order), lax.rem(span - place.z, span), span, 0
    )


def by_core(place, own, other, axis):
    return jnp.where(
        place.c == 0,
        jnp.concatenate([own, other], axis),
        jnp.concatenate([other, own], axis),
    )


def copy_call(body, out_shape, copies, operands, place):
    def kernel(scalars, *refs):
        ins, out, sems = refs[: len(operands)], refs[len(operands)], refs[-1]
        started = []
        for slot, (src, dst) in enumerate(body(scalars, ins, out)):
            copy = pltpu.make_async_copy(src, dst, sems.at[slot])
            copy.start()
            started.append(copy)
        for copy in started:
            copy.wait()

    return pl.pallas_call(
        kernel,
        out_shape=out_shape,
        in_specs=[pl.BlockSpec(memory_space=pltpu.SMEM)]
        + [pl.BlockSpec(memory_space=pltpu.HBM)] * len(operands),
        out_specs=pl.BlockSpec(memory_space=pltpu.VMEM),
        scratch_shapes=[pltpu.SemaphoreType.DMA((copies,))],
        compiler_params=pltpu.CompilerParams(vmem_limit_bytes=VMEM_LIMIT),
        cost_estimate=LIGHT,
    )(place.scalars, *operands)


def pick_columns(weights, layer, width, place):
    rows, columns = weights.shape[1:]
    count = columns // (2 * width)
    group = 2 if count % 2 == 0 else 1

    def kernel(scalars, *refs):
        out = refs[-1]
        for j in range(group):
            out[:, j * width : (j + 1) * width] = refs[j][0]

    def spec(j):
        return pl.BlockSpec(
            (1, rows, width), lambda i, s: (layer, 0, 2 * (group * i + j) + s[2])
        )

    return pl.pallas_call(
        kernel,
        grid_spec=pltpu.PrefetchScalarGridSpec(
            num_scalar_prefetch=1,
            grid=(count // group,),
            in_specs=[spec(j) for j in range(group)],
            out_specs=pl.BlockSpec((rows, group * width), lambda i, s: (0, i)),
        ),
        out_shape=jax.ShapeDtypeStruct((rows, count * width), weights.dtype),
        compiler_params=pltpu.CompilerParams(vmem_limit_bytes=VMEM_LIMIT),
        cost_estimate=LIGHT,
    )(place.scalars, *[weights] * group)


def pick_rows(arrays, layer, place):
    halves = [w.shape[1] // 2 for w in arrays]
    columns = arrays[0].shape[2]
    part = columns // 4 if columns % 512 == 0 else columns

    def kernel(scalars, *refs):
        start = 0
        for ref, half in zip(refs, halves, strict=False):
            refs[-1][start : start + half] = ref[0]
            start += half

    return pl.pallas_call(
        kernel,
        grid_spec=pltpu.PrefetchScalarGridSpec(
            num_scalar_prefetch=1,
            grid=(columns // part,),
            in_specs=[
                pl.BlockSpec((1, half, part), lambda i, s: (layer, s[2], i))
                for half in halves
            ],
            out_specs=pl.BlockSpec((sum(halves), part), lambda i, s: (0, i)),
        ),
        out_shape=jax.ShapeDtypeStruct((sum(halves), columns), arrays[0].dtype),
        compiler_params=pltpu.CompilerParams(vmem_limit_bytes=VMEM_LIMIT),
        cost_estimate=LIGHT,
    )(place.scalars, *arrays)


def other_shards(table, place):
    span = place.span

    def body(scalars, ins, out):
        for k in range(1, span):
            source = lax.rem(scalars[0] + (span - k), span)
            for i in range(2):
                yield ins[0].at[source, i], out.at[i, k - 1]

    shape = jax.ShapeDtypeStruct((2, span - 1, *table.shape[2:]), table.dtype)
    return copy_call(body, shape, 2 * (span - 1), [table], place)


def flipped(q, flip):
    return lax.bitwise_xor(q, jnp.int32(flip))


def overlaps(eighth, start, stop):
    for j in range(8):
        low, high = max(j * eighth, start), min((j + 1) * eighth, stop)
        if high > low:
            yield j, low, high


def assemble(half, cuts, near, near_x, near_y, far_a, far_b, place):
    span = place.span
    eighth, columns = half.shape[0] // 8, half.shape[1]
    block = (eighth, columns)

    def kernel(scalars, half_ref, n_ref, x_ref, y_ref, a_ref, b_ref, *rest):
        outs, table = rest[:-1], rest[-1]
        z, q = scalars[0], scalars[1]
        own = pl.program_id(0) == z

        @pl.when(own)
        def _():
            table[...] = half_ref[...]

        @pl.when(jnp.logical_not(own))
        def _():
            for i in range(2):
                for flip, ref in enumerate((n_ref, x_ref, y_ref)):
                    table[flipped(q, flip), i] = ref[i, 0]
            table[flipped(q, 3), 0] = a_ref[0]
            table[flipped(q, 3), 1] = b_ref[0]

        for out, (start, stop, left, right) in zip(outs, cuts, strict=True):
            for j, low, high in overlaps(eighth, start, stop):
                out[0, low - start : high - start] = table[
                    j // 2, j % 2, low - j * eighth : high - j * eighth, left:right
                ]

    def behind(j, s):
        return jnp.maximum(lax.rem(s[0] + span - j, span), 1) - 1

    near_spec = pl.BlockSpec((2, 1, *block), lambda j, s: (0, behind(j, s), 0, 0))
    far_spec = pl.BlockSpec((1, *block), lambda j, s: (behind(j, s), 0, 0))
    outs = pl.pallas_call(
        kernel,
        grid_spec=pltpu.PrefetchScalarGridSpec(
            num_scalar_prefetch=1,
            grid=(span,),
            in_specs=[
                pl.BlockSpec((4, 2, *block), lambda j, s: (0, 0, 0, 0)),
                near_spec,
                near_spec,
                near_spec,
                far_spec,
                far_spec,
            ],
            out_specs=[
                pl.BlockSpec((1, b - a, d - c), lambda j, s: (j, 0, 0)) for a, b, c, d in cuts
            ],
            scratch_shapes=[pltpu.VMEM((4, 2, *block), half.dtype)],
        ),
        out_shape=[
            jax.ShapeDtypeStruct((span, b - a, d - c), half.dtype) for a, b, c, d in cuts
        ],
        compiler_params=pltpu.CompilerParams(vmem_limit_bytes=VMEM_LIMIT),
        cost_estimate=LIGHT,
    )(
        place.scalars,
        half.reshape(4, 2, *block),
        near,
        near_x,
        near_y,
        far_a,
        far_b,
    )
    return [out.reshape(-1, out.shape[2]) for out in outs]


def absolute_quarters(summed, near_x, near_y, far_a, far_b, place):
    def body(scalars, ins, out):
        q = scalars[1]
        for flip in range(3):
            yield ins[flip], out.at[flipped(q, flip)]
        for i in range(2):
            yield ins[3 + i], out.at[flipped(q, 3), i]

    shape = jax.ShapeDtypeStruct((4, *summed.shape), summed.dtype)
    return copy_call(body, shape, 5, [summed, near_x, near_y, far_a, far_b], place)


def weight_gradient(lefts, right, place):
    span = place.span
    tokens, columns = right.shape
    sizes = [left.shape[1] // span for left in lefts]
    eighth = sum(sizes) // 8

    def kernel(scalars, *refs):
        left_refs, right_ref = refs[: len(sizes)], refs[len(sizes)]
        own, pass_a, pass_b, send_a, send_b, table = refs[len(sizes) + 1 :]
        q = scalars[1]
        start = 0
        for left_ref, size in zip(left_refs, sizes, strict=True):
            product = lax.dot_general(
                left_ref[...],
                right_ref[...],
                (((0,), (0,)), ((), ())),
                preferred_element_type=F32,
            ).astype(BF16)
            for j, low, high in overlaps(eighth, start, start + size):
                table[j // 2, j % 2, low - j * eighth : high - j * eighth] = product[
                    low - start : high - start
                ]
            start += size
        near_x, near_y, far = flipped(q, 1), flipped(q, 2), flipped(q, 3)
        own[0, 0], own[0, 1] = table[q, 0], table[q, 1]
        pass_a[0], pass_b[0] = table[near_y, 0], table[near_x, 1]
        send_a[0, 0], send_a[1, 0] = table[near_x, 0], table[far, 0]
        send_b[0, 0], send_b[1, 0] = table[near_y, 1], table[far, 1]

    block = (eighth, columns)
    one = pl.BlockSpec((1, *block), lambda k, s: (k, 0, 0))
    two = pl.BlockSpec((2, 1, *block), lambda k, s: (0, k, 0, 0))
    return pl.pallas_call(
        kernel,
        grid_spec=pltpu.PrefetchScalarGridSpec(
            num_scalar_prefetch=1,
            grid=(span,),
            in_specs=[
                *[
                    pl.BlockSpec((tokens, size), lambda k, s: (0, lax.bitwise_xor(s[0], k)))
                    for size in sizes
                ],
                pl.BlockSpec((tokens, columns), lambda k, s: (0, 0)),
            ],
            out_specs=[
                pl.BlockSpec((1, 2, *block), lambda k, s: (k, 0, 0, 0)),
                one,
                one,
                two,
                two,
            ],
            scratch_shapes=[pltpu.VMEM((4, 2, *block), BF16)],
        ),
        out_shape=[
            pltpu.HBM((span, 2, *block), BF16),
            pltpu.HBM((span, *block), BF16),
            pltpu.HBM((span, *block), BF16),
            pltpu.HBM((2, span, *block), BF16),
            pltpu.HBM((2, span, *block), BF16),
        ],
        compiler_params=pltpu.CompilerParams(vmem_limit_bytes=VMEM_LIMIT),
        cost_estimate=LIGHT,
    )(place.scalars, *lefts, right)


def combine(own, got_a, got_b, more_a, more_b):
    span, _, eighth, columns = own.shape
    part = columns // 4 if columns % 512 == 0 else columns

    def kernel(own_ref, ga_ref, gb_ref, ma_ref, mb_ref, *outs):
        for j, out in enumerate(outs):
            here = slice(j * span // 2, (j + 1) * span // 2)
            for i, (got, more) in enumerate(((ga_ref, ma_ref), (gb_ref, mb_ref))):
                total = own_ref[here, i].astype(F32) + got[0, here].astype(F32)
                out[:, i] = (total + more[here].astype(F32)).astype(BF16)

    got = pl.BlockSpec((1, span, eighth, part), lambda j: (0, 0, 0, j))
    more = pl.BlockSpec((span, eighth, part), lambda j: (0, 0, j))
    whole = pl.BlockSpec((span, 2, eighth, part), lambda j: (0, 0, 0, j))
    half = pl.BlockSpec((span // 2, 2, eighth, part), lambda j: (0, 0, 0, j))
    return pl.pallas_call(
        kernel,
        grid=(columns // part,),
        in_specs=[whole, got, got, more, more],
        out_specs=[half, half],
        out_shape=[jax.ShapeDtypeStruct((span // 2, *own.shape[1:]), BF16)] * 2,
        compiler_params=pltpu.CompilerParams(vmem_limit_bytes=VMEM_LIMIT),
        cost_estimate=LIGHT,
    )(own, got_a, got_b, more_a, more_b)


def finish_columns(parts, width, layer, previous):
    _, _, rows, columns = parts.shape

    def kernel(part_ref, *rest):
        out_ref = rest[-1]
        for core in range(2):
            for j in range(columns // width):
                start = (2 * j + core) * width
                out_ref[0, :, start : start + width] = part_ref[
                    0, core, :, j * width : (j + 1) * width
                ].astype(F32)

    operands, in_specs, aliases = (
        [parts],
        [pl.BlockSpec((1, 2, rows, columns), lambda q: (q, 0, 0, 0))],
        {},
    )
    if previous is not None:
        operands.append(previous)
        in_specs.append(pl.BlockSpec(memory_space=pl.ANY))
        aliases = {1: 0}
    return pl.pallas_call(
        kernel,
        grid=(4,),
        in_specs=in_specs,
        out_specs=pl.BlockSpec((1, rows, 2 * columns), lambda q: (layer, q, 0)),
        out_shape=jax.ShapeDtypeStruct((LAYERS, 4 * rows, 2 * columns), F32),
        input_output_aliases=aliases,
        compiler_params=pltpu.CompilerParams(vmem_limit_bytes=VMEM_LIMIT),
        cost_estimate=LIGHT,
    )(*operands)


def finish_rows(parts, first_rows, layer, previous):
    _, _, quarter, columns = parts.shape
    sizes = (first_rows, 4 * quarter - first_rows)

    def kernel(part_ref, *rest):
        first, second = rest[-2:]
        for q in range(4):
            start, stop = q * quarter, (q + 1) * quarter
            cut = min(max(first_rows, start), stop)
            if cut > start:
                first[0, :, start:cut] = part_ref[q, :, : cut - start].astype(F32)
            if stop > cut:
                second[0, :, cut - first_rows : stop - first_rows] = part_ref[
                    q, :, cut - start :
                ].astype(F32)

    half = columns // 4 if columns % 512 == 0 else columns
    operands, aliases = [parts], {}
    in_specs = [pl.BlockSpec((4, 2, quarter, half), lambda j: (0, 0, 0, j))]
    if previous is not None:
        operands += list(previous)
        in_specs += [pl.BlockSpec(memory_space=pl.ANY)] * 2
        aliases = {1: 0, 2: 1}
    return pl.pallas_call(
        kernel,
        grid=(columns // half,),
        in_specs=in_specs,
        out_specs=[
            pl.BlockSpec((1, 2, size, half), lambda j: (layer, 0, 0, j)) for size in sizes
        ],
        out_shape=[
            jax.ShapeDtypeStruct((LAYERS, 2, size, columns), F32) for size in sizes
        ],
        input_output_aliases=aliases,
        compiler_params=pltpu.CompilerParams(vmem_limit_bytes=VMEM_LIMIT),
        cost_estimate=LIGHT,
    )(*operands)


def in_order(blocks, place):
    span = place.span

    def body(scalars, ins, out):
        for k in range(span):
            yield ins[k], out.at[lax.rem(scalars[0] + (span - k), span)]

    shape = jax.ShapeDtypeStruct((span, *blocks[0].shape), blocks[0].dtype)
    return copy_call(body, shape, span, list(blocks), place)


def spread(blocks, place):
    span = place.span
    out = []
    for k in range(span):
        block = lax.dynamic_index_in_dim(
            blocks, lax.rem(place.z + k, span), 0, keepdims=False
        )
        out.append(block if k == 0 else spin(block, k, span))
    return out


def row_to_chip(x, place):
    rows, tokens, width = x.shape
    half = width // 2
    mine = lax.dynamic_slice_in_dim(x, place.c * half, half, 2)
    theirs = lax.dynamic_slice_in_dim(x, (1 - place.c) * half, half, 2)
    theirs = yield swap(theirs, "core")
    blocks = yield spread(by_core(place, mine, theirs, 0), place)
    own = in_order(blocks, place).reshape(place.span * tokens, half)
    other = yield swap(own, "core")
    return by_core(place, own, other, 1)


def chip_to_rows(y, rows, place):
    span = place.span
    width = y.shape[1]
    tokens = y.shape[0] // span
    half = width // 2
    mine = lax.dynamic_slice_in_dim(y, place.c * half, half, 1)
    blocks = yield spread(mine.reshape(span, tokens, half), place)
    stacked = in_order(blocks, place)
    own = lax.dynamic_slice_in_dim(stacked, place.c * rows, rows, 0)
    theirs = lax.dynamic_slice_in_dim(stacked, (1 - place.c) * rows, rows, 0)
    other = yield swap(theirs, "core")
    return by_core(place, own, other, 2)


class Slots:
    def __init__(self):
        self.parts = []

    def add(self, part, done):
        self.parts.append([part, next(part), done])

    def step(self, extra=()):
        pending, extra = lax.optimization_barrier(
            ([part[1] for part in self.parts], extra)
        )
        alive = []
        for part, arrived in zip(self.parts, pending, strict=True):
            try:
                part[1] = part[0].send(arrived)
                alive.append(part)
            except StopIteration as end:
                part[2](end.value)
        self.parts = alive
        return extra


def gather_weight(half, cuts, by_call, wait, place):
    span = place.span
    eighth, columns = half.shape[0] // 8, half.shape[1]
    mine = lax.dynamic_index_in_dim(
        half.reshape(4, 2, eighth, columns), place.q, 0, keepdims=False
    )
    if by_call:
        moving = lax.all_gather(mine, "shard")
    else:
        moving = [spin(mine, k, span) for k in range(1, span)]
    if wait:
        yield ()
    arrived = yield moving
    near = other_shards(arrived, place) if by_call else jnp.stack(arrived, 1)
    near_x, near_y = yield [swap(near, "xbit"), swap(near, "ybit")]
    far_a, far_b = yield [swap(near_x[0], "ybit"), swap(near_y[1], "xbit")]
    return assemble(half, cuts, near, near_x, near_y, far_a, far_b, place)


def reduce_weight(lefts, right, place, last=False):
    own, pass_a, pass_b, send_a, send_b = yield weight_gradient(lefts, right, place)
    got_a, got_b = yield [swap(send_a, "xbit"), swap(send_b, "ybit")]
    onward_a = (pass_a.astype(F32) + got_a[1].astype(F32)).astype(BF16)
    onward_b = (pass_b.astype(F32) + got_b[1].astype(F32)).astype(BF16)
    more_a, more_b = yield [swap(onward_a, "ybit"), swap(onward_b, "xbit")]
    keep, send = combine(own, got_a, got_b, more_a, more_b)
    step = place.span // 2
    while step > 1:
        other = yield across(send, step, place.span)
        step //= 2
        send = (keep[step:].astype(F32) + other[step:].astype(F32)).astype(BF16)
        keep = keep[:step].astype(F32) + other[:step].astype(F32)
    other = yield across(send, step, place.span)
    summed = (keep[0].astype(F32) + other[0].astype(F32)).astype(BF16)
    if lax.axis_size("outer") > 1:
        summed = lax.psum(summed, "outer")
    _, eighth, columns = summed.shape
    if last:
        near_x, near_y = yield [swap(summed, "xbit"), swap(summed, "ybit")]
        far_a, far_b = yield [swap(near_x[0], "ybit"), swap(near_y[1], "xbit")]
        half = absolute_quarters(summed, near_x, near_y, far_a, far_b, place)
        other = yield swap(half, "core")
        parts = by_core(place, half[:, None], other[:, None], 1)
    else:
        moving = lax.all_gather(summed, ("ybit", "xbit", "core"))
        yield ()
        yield ()
        parts = yield moving
    return parts.reshape(4, 2, 2 * eighth, columns)


def gather_small(vectors, place):
    flat = jnp.concatenate([v.reshape(-1) for v in vectors])
    blocks = yield [flat] + [spin(flat, k, place.span) for k in range(1, place.span)]
    table = from_relative(blocks, place)
    out, start = [], 0
    for v in vectors:
        part = table[:, start : start + v.size].reshape(place.span, *v.shape)
        start += v.size
        part = jnp.moveaxis(part, 0, -2)
        out.append(part.reshape(*v.shape[:-1], -1).astype(F32))
    return out


def blocks_of(length, step):
    step = step if length % step == 0 else length
    return [(i * step, step) for i in range(length // step)]


def fill_bias(bias, seg_col, seg_row):
    @pl.when(pl.program_id(0) == 0)
    def _():
        row = lax.broadcasted_iota(jnp.int32, bias.shape, 0)
        col = lax.broadcasted_iota(jnp.int32, bias.shape, 1)
        mask = (col <= row) & (seg_col[...] == seg_row[...])
        bias[...] = jnp.where(mask, 0.0, -1e30)


def turn(u, tables):
    keep, upper, lower = tables
    half, lanes = ROT // 2, u.shape[1]
    return u * keep + pltpu.roll(u, lanes - half, 1) * upper + pltpu.roll(u, half, 1) * lower


def turn_back(d, tables):
    keep, upper, lower = tables
    half, lanes = ROT // 2, d.shape[1]
    return d * keep + pltpu.roll(d * upper, half, 1) + pltpu.roll(d * lower, lanes - half, 1)


def attend_kernel(scale, head, *refs):
    q_in, k_in, v_in, keep, upper, lower, seg_col, seg_row = refs[:8]
    q_ref, k_ref, v_ref, o_ref, lse_ref, bias = refs[8:]
    fill_bias(bias, seg_col, seg_row)
    tables = keep[...], upper[...], lower[...]
    q_ref[...] = turn(q_in[...], tables).astype(BF16)
    k_ref[...] = turn(k_in[...], tables).astype(BF16)
    v_ref[...] = v_in[...].astype(BF16)
    for start, step in blocks_of(q_ref.shape[0], FORWARD_ROWS):
        stop = start + step
        for h in range(q_ref.shape[1] // head):
            lanes = slice(h * head, (h + 1) * head)
            query = q_ref[start:stop, lanes] * scale
            scores = dot_t(query, k_ref[:stop, lanes]) + bias[start:stop, :stop]
            top = jnp.max(scores, -1, keepdims=True)
            expo = jnp.exp(scores - top)
            total = jnp.sum(expo, -1, keepdims=True)
            probs = (expo * (1.0 / total)).astype(BF16)
            o_ref[start:stop, lanes] = dot(probs, v_ref[:stop, lanes]).astype(BF16)
            lse_ref[h, start:stop, :] = top + jnp.log(total)


def attend_back_kernel(scale, head, *refs):
    q_ref, k_ref, v_ref, do_ref, lse_ref, keep, upper, lower, seg_col, seg_row = refs[:10]
    dq_out, dk_out, dv_out, dq_ref, dk_ref, dv_ref, bias = refs[10:]
    fill_bias(bias, seg_col, seg_row)
    over_rows = (((0,), (0,)), ((), ()))
    length = q_ref.shape[0]
    if len(blocks_of(length, BACKWARD_ROWS)) > 1:
        dk_ref[...] = jnp.zeros_like(dk_ref)
        dv_ref[...] = jnp.zeros_like(dv_ref)
    for start, step in blocks_of(length, BACKWARD_ROWS):
        stop = start + step
        for h in range(q_ref.shape[1] // head):
            lanes = slice(h * head, (h + 1) * head)
            query = q_ref[start:stop, lanes] * scale
            keys = k_ref[:stop, lanes]
            grad = do_ref[start:stop, lanes]
            scores = dot_t(query, keys) + bias[start:stop, :stop]
            probs = jnp.exp(scores - lse_ref[h, start:stop, :])
            d_probs = dot_t(grad, v_ref[:stop, lanes])
            delta = jnp.sum(probs * d_probs, -1, keepdims=True)
            d_scores = (probs * (d_probs - delta)).astype(BF16)
            dq_ref[start:stop, lanes] = dot(d_scores, keys) * scale
            d_key = lax.dot_general(d_scores, query, over_rows, preferred_element_type=F32)
            d_value = lax.dot_general(
                probs.astype(BF16), grad, over_rows, preferred_element_type=F32
            )
            if step == length:
                dk_ref[:, lanes], dv_ref[:, lanes] = d_key, d_value
            else:
                dk_ref[:stop, lanes] += d_key
                dv_ref[:stop, lanes] += d_value
    tables = keep[...], upper[...], lower[...]
    dq_out[...] = turn_back(dq_ref[...], tables).astype(BF16)
    dk_out[...] = turn_back(dk_ref[...], tables).astype(BF16)
    dv_out[...] = dv_ref[...].astype(BF16)


def attention_specs(length, width, head):
    group = max(head, 128)
    count = width // group
    wide = pl.BlockSpec((length, group), lambda i: (0, i))
    lse = pl.BlockSpec((group // head, length, 1), lambda i: (i, 0, 0))
    same = [pl.BlockSpec((length, group), lambda i: (0, 0))] * 3 + [
        pl.BlockSpec((length, 1), lambda i: (0, 0)),
        pl.BlockSpec((1, length), lambda i: (0, 0)),
    ]
    return group, count, wide, lse, same


def attend(projected, fixed, head):
    length, width = projected.shape[0], projected.shape[1] // 3
    group, count, wide, lse, same = attention_specs(length, width, head)

    def kernel(*refs):
        attend_kernel(1.0 / math.sqrt(head), head, *refs)

    low = jax.ShapeDtypeStruct((length, width), BF16)
    saved = pltpu.HBM((length, width), BF16)
    return pl.pallas_call(
        kernel,
        grid=(count,),
        in_specs=[
            wide,
            pl.BlockSpec((length, group), lambda i: (0, count + i)),
            pl.BlockSpec((length, group), lambda i: (0, 2 * count + i)),
            *same,
        ],
        out_specs=[wide, wide, wide, wide, lse],
        out_shape=[
            saved,
            saved,
            saved,
            low,
            pltpu.HBM((width // head, length, 1), F32),
        ],
        scratch_shapes=[pltpu.VMEM((length, length), F32)],
        compiler_params=pltpu.CompilerParams(vmem_limit_bytes=VMEM_LIMIT),
        cost_estimate=FILLER,
    )(projected, projected, projected, *fixed)


def attend_back(query, keys, values, d_mixed, lse_all, fixed, head):
    length, width = query.shape
    group, count, wide, lse, same = attention_specs(length, width, head)

    def kernel(*refs):
        attend_back_kernel(1.0 / math.sqrt(head), head, *refs)

    out = jax.ShapeDtypeStruct((length, width), BF16)
    return pl.pallas_call(
        kernel,
        grid=(count,),
        in_specs=[wide, wide, wide, wide, lse, *same],
        out_specs=[wide, wide, wide],
        out_shape=[out, out, out],
        scratch_shapes=[pltpu.VMEM((length, group), F32)] * 3
        + [pltpu.VMEM((length, length), F32)],
        compiler_params=pltpu.CompilerParams(vmem_limit_bytes=VMEM_LIMIT),
        cost_estimate=LIGHT,
    )(query, keys, values, d_mixed, lse_all, *fixed)


def rotary_tables(positions, head):
    half = ROT // 2
    inverse = jnp.power(10000.0, -2.0 * jnp.arange(half, dtype=F32) / ROT)
    angles = positions.astype(F32)[:, None] * inverse
    cos, sin = jnp.cos(angles), jnp.sin(angles)
    rest = jnp.zeros((positions.shape[0], head - ROT), F32)
    none = jnp.zeros_like(sin)
    keep = [cos, cos, rest + 1.0]
    upper = [-sin, none, rest]
    lower = [none, sin, rest]
    times = max(1, 128 // head)
    return [jnp.concatenate(t * times, 1) for t in (keep, upper, lower)]


def normalise(x):
    centred = x - jnp.mean(x, -1, keepdims=True)
    spread = jnp.mean(centred * centred, -1, keepdims=True)
    inverse = lax.rsqrt(spread + EPS)
    return centred * inverse, inverse


def forward_layer(x, weights, small, fixed, head):
    w_qkv, w_up, w_out, w_down = weights
    gains, shifts, b_qkv, b_out, b_up, b_down = small
    xhat, inverse = normalise(x)
    attn_low = (xhat * gains[0] + shifts[0]).astype(BF16)
    mlp_low = (xhat * gains[1] + shifts[1]).astype(BF16)
    projected = dot(attn_low, w_qkv) + b_qkv
    query, keys, values, mixed_low, lse = attend(projected, fixed, head)
    hidden_pre = dot(mlp_low, w_up) + b_up
    cdf = 0.5 * (1.0 + lax.erf(hidden_pre * ROOT_HALF))
    hidden_low = (hidden_pre * cdf).astype(BF16)
    part = (dot(mixed_low, w_out) + dot(hidden_low, w_down)).astype(BF16)
    other = swap(part, "core")
    y = x + (part.astype(F32) + other.astype(F32) + b_out + b_down)
    attention = (query, keys, values, lse)
    return y, (xhat, inverse, attn_low, mlp_low, attention, hidden_pre, mixed_low, hidden_low)


def backward_layer(dy, weights, small, saved, fixed, head, place, slots, done, last, mover):
    w_qkv, w_up, w_out, w_down = weights
    gains = small[0]
    xhat, inverse, attn_low, mlp_low, attention, hidden_pre, mixed_low, hidden_low = saved
    query, keys, values, lse = attention
    dy_low = dy.astype(BF16)
    slots.add(reduce_weight([mixed_low, hidden_low], dy_low, place), done(2))
    d_branch_b = jnp.sum(dy_low.astype(F32), 0)

    dy_low = slots.step(dy_low)
    d_hidden = dot_t(dy_low, w_down)
    d_mixed = dot_t(dy_low, w_out).astype(BF16)
    cdf = 0.5 * (1.0 + lax.erf(hidden_pre * ROOT_HALF))
    density = jnp.exp(-0.5 * hidden_pre * hidden_pre) * (1.0 / math.sqrt(2.0 * math.pi))
    d_pre = (d_hidden * (cdf + hidden_pre * density)).astype(BF16)
    slots.add(reduce_weight([mlp_low], d_pre, place), done(1))
    d_up_b = jnp.sum(d_pre.astype(F32), 0)

    d_mixed, d_pre = slots.step((d_mixed, d_pre))
    if mover is not None:
        slots.add(*mover)
    d_qkv = jnp.concatenate(
        attend_back(query, keys, values, d_mixed, lse, fixed, head), 1
    )
    slots.add(reduce_weight([attn_low], d_qkv, place, last), done(0))
    d_mlp = dot_t(d_pre, w_up)

    d_qkv, d_mlp = slots.step((d_qkv, d_mlp))
    d_qkv_b = jnp.sum(d_qkv.astype(F32), 0)
    d_attn = dot_t(d_qkv, w_qkv)
    part = (d_attn * gains[0] + d_mlp * gains[1]).astype(BF16)
    d_xhat = part.astype(F32) + swap(part, "core").astype(F32)
    dx = dy + inverse * (
        d_xhat
        - jnp.mean(d_xhat, -1, keepdims=True)
        - xhat * jnp.mean(d_xhat * xhat, -1, keepdims=True)
    )
    d_gains = jnp.stack([jnp.sum(d_attn * xhat, 0), jnp.sum(d_mlp * xhat, 0)])
    d_shifts = jnp.stack([jnp.sum(d_attn, 0), jnp.sum(d_mlp, 0)])
    return dx, (d_gains, d_shifts, d_qkv_b, d_branch_b, d_up_b)


def pick_vector(v, width, place):
    return jnp.take(v.reshape(*v.shape[:-1], -1, 2, width), place.c, axis=-2).reshape(
        *v.shape[:-1], -1
    )


def spread_vector(v, width, place):
    blocks = v.reshape(-1, 1, width)
    here = (jnp.arange(2) == place.c)[None, :, None]
    return jnp.where(here, blocks, 0.0).reshape(-1)


def reduce_small(layers, head_cols, ff_cols, place):
    span = place.span
    parts = []
    for d_gains, d_shifts, d_qkv_b, d_branch_b, d_up_b in layers:
        parts += [
            d_gains,
            d_shifts,
            spread_vector(d_qkv_b, head_cols, place),
            jnp.where(place.c == 0, d_branch_b, 0.0),
            spread_vector(d_up_b, ff_cols, place),
        ]
    tables = [p.reshape(-1, span, p.shape[-1] // span) for p in parts]
    flat = jnp.concatenate(
        [jnp.moveaxis(t, 1, 0).reshape(span, -1, 128) for t in tables], 1
    )
    for axis in ("core", "xbit", "ybit"):
        other = yield swap(flat, axis)
        flat = flat + other
    if lax.axis_size("outer") > 1:
        flat = lax.psum(flat, "outer")
    blocks = yield spread(flat, place)
    total = sum(blocks)
    total = total.reshape(-1)
    out, start = [], 0
    for p in parts:
        size = p.size // span
        out.append(total[start : start + size].reshape(*p.shape[:-1], p.shape[-1] // span))
        start += size
    count = len(parts) // len(layers)
    return [jnp.stack(out[i::count]) for i in range(count)]


def on_device(span, *arguments):
    (
        hidden_in,
        segments,
        norm_gains,
        norm_biases,
        qkv_weight,
        qkv_bias,
        out_weight,
        out_bias,
        up_weight,
        up_bias,
        down_weight,
        down_bias,
        out_grad,
    ) = arguments
    place = Place(span)
    rows = hidden_in.shape[0]
    width = hidden_in.shape[2]
    head = width // H
    head_cols = width // (2 * span)
    ff_cols = up_weight.shape[2] // (2 * span)
    assert 2 * rows == span

    found = {}

    def keep(name):
        def done(value):
            found[name] = value

        return done

    def unit(name, arrays, wait):
        qkv, up, out, down = arrays
        kind, layer = name
        if kind == "last":
            half = pick_rows((out, down), layer, place)
            split = out.shape[1] // 2
            cuts = [(0, split, 0, width), (split, half.shape[0], 0, width)]
        else:
            parts = []
            if kind != "up":
                parts.append(pick_columns(qkv, layer, head_cols, place))
            if kind != "qkv":
                parts.append(pick_columns(up, layer, ff_cols, place))
            half = jnp.concatenate(parts, 1) if len(parts) > 1 else parts[0]
            cuts, start = [], 0
            for part in parts:
                cuts.append((0, part.shape[0], start, start + part.shape[1]))
                start += part.shape[1]
        slots.add(gather_weight(half, cuts, kind != "qkv", wait, place), keep(name))

    slots = Slots()
    arrays = (qkv_weight, up_weight, out_weight, down_weight)
    vectors = (norm_gains, norm_biases, qkv_bias, out_bias, up_bias, down_bias)
    units = [("qkv", 0), ("up", 0), ("last", 0)]
    for layer in range(1, LAYERS):
        units += [("both", layer), ("last", layer)]
    unit(units[0], arrays, False)
    slots.add(row_to_chip(hidden_in, place), keep("rows"))
    seg_other = swap(segments, "core")
    arrays, vectors, out_grad = slots.step((arrays, vectors, out_grad))
    slots.add(gather_small(vectors, place), keep("vectors"))
    for name in units[1:]:
        unit(name, arrays, True)
        arrays, out_grad = slots.step((arrays, out_grad))
    slots.add(row_to_chip(out_grad, place), keep("grads"))
    while slots.parts:
        slots.step()
    weights = [
        (*found["qkv", 0], *found["up", 0], *found["last", 0]),
        *((*found["both", i], *found["last", i]) for i in range(1, LAYERS)),
    ]

    stream, dy = found["rows"].astype(F32), found["grads"].astype(F32)
    seg_all = by_core(place, segments, seg_other, 0)
    seg = lax.dynamic_index_in_dim(seg_all, place.z, 0, keepdims=False)
    seg_col, seg_row = seg[:, None], seg[None, :]
    length = seg.shape[0]
    earlier = jnp.sum((seg_row < seg_col).astype(jnp.int32), -1)
    positions = jnp.arange(length, dtype=jnp.int32) - earlier
    fixed = (*rotary_tables(positions, head), seg_col, seg_row)

    gains, shifts, b_qkv, b_out, b_up, b_down = found["vectors"]
    b_qkv = pick_vector(b_qkv, head_cols, place)
    b_up = pick_vector(b_up, ff_cols, place)
    smalls = [
        (gains[i], shifts[i], b_qkv[i], b_out[i], b_up[i], b_down[i]) for i in range(LAYERS)
    ]

    kept = []
    for layer in range(LAYERS):
        stream, saved = forward_layer(
            stream, weights[layer], smalls[layer], fixed, head
        )
        kept.append(saved)

    big = [None] * 3
    little = [None] * LAYERS
    slots = Slots()

    def done_for(layer):
        def of(index):
            def done(parts):
                if index == 2:
                    first_rows = out_weight.shape[1] // 2
                    big[2] = finish_rows(parts, first_rows, layer, big[2])
                else:
                    by = (head_cols, ff_cols)[index]
                    big[index] = finish_columns(parts, by, layer, big[index])

            return done

        return of

    out_low = stream.astype(BF16)
    for layer in reversed(range(LAYERS)):
        mover = None
        if layer == 0:
            mover = (chip_to_rows(out_low, rows, place), keep("block_out"))
        dy, little[layer] = backward_layer(
            dy,
            weights[layer],
            smalls[layer],
            kept[layer],
            fixed,
            head,
            place,
            slots,
            done_for(layer),
            layer == 0,
            mover,
        )
    slots.add(chip_to_rows(dy.astype(BF16), rows, place), keep("in_grad"))
    slots.add(reduce_small(little, head_cols, ff_cols, place), keep("sums"))
    while slots.parts:
        before = list(big)
        gated = slots.step(before)
        for i in range(3):
            if big[i] is before[i]:
                big[i] = gated[i]
    block_out, in_grad = found["block_out"], found["in_grad"].astype(F32)
    d_gains, d_shifts, d_qkv_b, d_branch_b, d_up_b = found["sums"]
    d_qkv_w, d_up_w, (d_out_w, d_down_w) = big
    d_out_w = d_out_w.reshape(LAYERS, -1, width)
    d_down_w = d_down_w.reshape(LAYERS, -1, width)
    return (
        block_out,
        in_grad,
        d_gains,
        d_shifts,
        d_qkv_w,
        d_qkv_b,
        d_out_w,
        d_branch_b,
        d_up_w,
        d_up_b,
        d_down_w,
        d_branch_b,
    )


def solution(mesh):
    rep, span = mesh.shape["rep"], mesh.shape["shard"]
    fine = Mesh(mesh.devices.reshape(rep // 8, 2, 2, 2, span), (*AXES, "shard"))
    tokens = P(AXES, "shard", None)
    last = P(None, None, "shard")
    middle = P(None, "shard", None)
    vector = P(None, "shard")
    in_specs = (
        tokens,
        P(AXES, None),
        last,
        last,
        middle,
        vector,
        middle,
        vector,
        middle,
        vector,
        middle,
        vector,
        tokens,
    )
    out_specs = (
        tokens,
        tokens,
        last,
        last,
        middle,
        vector,
        middle,
        vector,
        middle,
        vector,
        middle,
        vector,
    )

    def step(*arguments):
        return on_device(span, *arguments)

    return jax.shard_map(
        step, mesh=fine, in_specs=in_specs, out_specs=out_specs, check_vma=False
    )
```
